128 devices in a mesh: grp: 8 (over y, z_hi), dev: 16 (over z_lo, x, core).
Axes of the slice: x: 4, y: 4, z: 4 (z_hi: 2, z_lo: 2; z = z_hi * 2 + z_lo), core: 2. Of those that a mesh axis runs over, the one named last changes fastest.
Arguments:
- line_pos: float32 [3, 256, 16384], P(None, None, ('grp', 'dev')), may hold values from -6 to 6
- line_vel: float32 [3, 256, 16384], P(None, None, ('grp', 'dev')), may hold values from -2 to 2
- stiffness: float32 [16384], P(('grp', 'dev')), may hold values from 0.1 to 0.9
- contact: int32 [8, 256, 16384], P(None, None, ('grp', 'dev')), may hold values 0 or 1
- offset: float32 [3, 16384], P(None, ('grp', 'dev')), may hold values from -3 to 3
- attach: int32 [16384], P(('grp', 'dev')), may hold values from 0 to 127
- plat_pos: float32 [3, 1024], P(None, 'grp'), may hold values from -6 to 6
- plat_vel: float32 [3, 1024], P(None, 'grp'), may hold values from -2 to 2
- inv_mass: float32 [3, 1024], P(None, 'grp'), may hold values from 0.05 to 0.3
- restoring: float32 [3, 1024], P(None, 'grp'), may hold values from 0.05 to 0.5
- kernel: float32 [8, 3, 1024], P(None, None, 'grp'), may hold values from -2.4 to 2.4
- vel_hist: float32 [8, 3, 1024], P(None, None, 'grp'), may hold values from -3 to 3
- wave: float32 [8, 3, 1024], P(None, None, 'grp'), may hold values from -6 to 6
- sample_pick: int32 [8192], P(('grp', 'dev')), may hold values from 0 to 1023
- sample_dest: int32 [8192, 1], P(('grp', 'dev')), may hold values from 0 to 15; in each aligned block of 64 rows (0 to 63, 64 to 127, ...) at most 8 rows name the same one
- w_in: bfloat16 [768, 2048], replicated, may hold values from -0.21875 to 0.21875
- gain: float32 [2048], replicated, may hold values from 0.25 to 1.75
- w_gate: bfloat16 [2048, 8192], P(None, 'dev'), may hold values from -0.125 to 0.125
- w_up: bfloat16 [2048, 8192], P(None, 'dev'), may hold values from -0.125 to 0.125
- w_down: bfloat16 [8192, 2048], P('dev'), may hold values from -0.0625 to 0.0625
- w_out: bfloat16 [2048, 768], replicated, may hold values from -0.125 to 0.125
Outputs:
- final_pos: float32 [3, 256, 16384], P(None, None, ('grp', 'dev'))
- final_plat: float32 [3, 1024], P(None, 'grp')
- slot_error: bfloat16 [16384, 768], P(('grp', 'dev'))
- grad_gate: float32 [2048, 8192], P('grp', 'dev')
- grad_up: float32 [2048, 8192], P('grp', 'dev')
The draws below stay inside these ranges and needn't reach their ends.
Inputs may be any that keep to these rules, and one draw needn't show every extreme that they name: `sample_dest`: at most 8 samples of one device name the same learner shard; some device and shard reach 8.
All inputs are finite; a program needn't handle non-finite values. No bound on the sum of `contact` on one device may be relied on, other than what follows from the above.
Results may differ from the reference program's by a relative error of at most 0.012.
Values may be sent and summed in bfloat16 or wider, within the bound.
No kernel may reach another device: no remote copies, remote signals or barrier semaphores. Data moves between devices by JAX's collectives and lax.ppermute only.
A program may use at most 128 MiB of HBM per device.

```python
import math
import jax
import jax.numpy as jnp
import numpy as np
from jax import lax

D = 2048
FF = 8192
NODES = 256
STEPS = 8
MEM = 8
LINES_DEV = 128
PLAT_GRP = 128
CAP = 8
F = 768
SAMPLES_DEV = 64
LINES = 16384
PLATS = 1024
SAMPLES = 8192
SLOTS = 16384
N_GRP = 8
N_DEV = 16
DEVICES = 128


def set_ends(values, rng, smallest, largest):
    dims = values.shape
    spot = [jax.random.randint(jax.random.fold_in(rng, axis), (), 0, dims[axis]) for axis in range(len(dims))]
    values = values.at[tuple(spot)].set(smallest)
    longest = dims.index(max(dims))
    spot[longest] = (spot[longest] + 1) % dims[longest]
    return values.at[tuple(spot)].set(largest)


def block_scale(rng, dims, split, low, largest):
    level, own = 1.0, jax.random.fold_in(rng, 6)
    for axis_at, shards_of in split:
        steps = jnp.exp(jax.random.uniform(jax.random.fold_in(own, axis_at), (shards_of,), jnp.float32, low / len(split), largest / len(split)))
        level = level * jnp.repeat(steps, dims[axis_at] // shards_of).reshape([-1 if axis == axis_at else 1 for axis in range(len(dims))])
    return level


def deal_out(key, own, number, rows, amount, top, limit, lean):
    ranking = jax.random.permutation(key, amount)
    packed, usual = load_shares(amount, rows * top, limit, lean, True), load_shares(amount, rows * top, limit, lean, False)
    places = jnp.arange(amount)

    def named(lengths, turn):
        used = int((lengths > 0).sum())
        fixed = max(1, used // 4)
        passed = fixed + (places - fixed + turn * (used - fixed)) % max(1, amount - fixed)
        return jnp.zeros((amount,), jnp.int32).at[ranking[jnp.where(places < fixed, places, passed)]].set(jnp.asarray(lengths, jnp.int32))

    lengths = jnp.where(number % 4 == 0, named(packed, number // 4), named(usual, number - number // 4 - 1))
    mixed = jax.random.permutation(jax.random.fold_in(own, 3), amount)
    giver, sink = mixed[0:amount // 2 * 2:2], mixed[1:amount // 2 * 2:2]
    margin = jnp.minimum(lengths[giver] - 1, limit - lengths[sink]) // 2
    margin = jnp.where((giver == ranking[0]) | (sink == ranking[0]) | (lengths[sink] == 0), 0, jnp.maximum(margin, 0))
    passed = jax.random.randint(jax.random.fold_in(own, 4), (amount // 2,), 0, 1 << 20) % (margin + 1)
    lengths = lengths.at[giver].add(-passed).at[sink].add(passed)
    labels = jnp.searchsorted(jnp.cumsum(lengths), jnp.arange(rows * top), side="right").astype(jnp.int32)
    grid = labels.reshape(top, rows).T
    grid = grid[jax.random.permutation(jax.random.fold_in(own, 1), rows)]
    turn = jax.random.randint(jax.random.fold_in(own, 2), (rows, 1), 0, top)
    return jnp.take_along_axis(grid, (jnp.arange(top)[None, :] + turn) % top, axis=1)


def load_shares(amount, total, bound, slope, full):
    loads = [(1 << 20) // math.isqrt(grade ** slope) + 1 for grade in range(1, amount + 1)]
    largest = bound if full else min(bound, max(-(-total // amount), total * loads[0] // sum(loads)))
    least = 1 if total - largest >= amount - 1 else 0
    counts, spare = [largest] + [least] * (amount - 1), total - largest - least * (amount - 1)
    while spare > 0:
        free = [i for i in range(1, amount) if counts[i] < largest] or [i for i in range(1, amount) if counts[i] < bound]
        mass, budget = sum([loads[i] for i in free]), spare
        for i in free:
            addition = min(bound - counts[i], max(1, budget * loads[i] // mass), spare)
            counts[i] = counts[i] + addition
            spare = spare - addition
    return np.array(counts)


def noise(key, shape, deviation, bound, split=(), kind=jnp.bfloat16):
    result = deviation * jax.random.normal(key, shape, jnp.float32)
    if split:
        result = result * block_scale(key, shape, split, -0.22, 0.18)
    return jnp.clip(result, -bound, bound).astype(kind)


def setup_inputs(seed: int = 0) -> dict:
    streams_of = jax.random.split(jax.random.key(seed), 22)
    line_pos = noise(streams_of[0], (3, NODES, LINES), 1.0, 6.0, ((2, 128),), jnp.float32)
    line_vel = noise(streams_of[1], (3, NODES, LINES), 0.3, 2.0, ((2, 128),), jnp.float32)
    stiffness = jnp.clip(jnp.exp(math.log(0.9) - 2.1972245 * jax.random.uniform(streams_of[2], (LINES,), jnp.float32) ** block_scale(streams_of[2], (LINES,), ((0, 128),), -0.2, 0.2)), 0.1, 0.9)
    contact = set_ends((jax.random.randint(streams_of[3], (STEPS, NODES, LINES), 0, 3) < 1).astype(jnp.int32), jax.random.fold_in(streams_of[3], 1), 0, 1)
    offset = noise(streams_of[4], (3, LINES), 0.5, 3.0, ((1, 128),), jnp.float32)
    attach = set_ends(jax.random.randint(streams_of[5], (LINES,), 0, PLAT_GRP), jax.random.fold_in(streams_of[5], 1), 0, PLAT_GRP - 1).astype(jnp.int32)
    plat_pos = noise(streams_of[6], (3, PLATS), 1.0, 6.0, ((1, 8),), jnp.float32)
    plat_vel = noise(streams_of[7], (3, PLATS), 0.3, 2.0, ((1, 8),), jnp.float32)
    inv_mass = jnp.clip(jnp.exp(math.log(0.3) - 1.7917595 * jax.random.uniform(streams_of[8], (3, PLATS), jnp.float32) ** block_scale(streams_of[8], (3, PLATS), ((1, 8),), -0.2, 0.2)), 0.05, 0.3)
    restoring = jnp.clip(jnp.exp(math.log(0.5) - 2.3025851 * jax.random.uniform(streams_of[9], (3, PLATS), jnp.float32) ** block_scale(streams_of[9], (3, PLATS), ((1, 8),), -0.2, 0.2)), 0.05, 0.5)
    kernel = noise(streams_of[10], (MEM, 3, PLATS), 0.4, 2.4, ((2, 8),), jnp.float32)
    vel_hist = noise(streams_of[11], (MEM, 3, PLATS), 0.5, 3.0, ((2, 8),), jnp.float32)
    wave = noise(streams_of[12], (STEPS, 3, PLATS), 1.0, 6.0, ((2, 8),), jnp.float32)
    sample_pick = set_ends(jax.random.randint(streams_of[13], (SAMPLES,), 0, LINES_DEV * STEPS), jax.random.fold_in(streams_of[13], 1), 0, (LINES_DEV * STEPS) - 1).astype(jnp.int32)
    sample_dest_keys = jax.random.split(jax.random.fold_in(streams_of[14], 1), SAMPLES // SAMPLES_DEV)
    sample_dest_turns = jax.random.permutation(jax.random.fold_in(streams_of[14], 3), SAMPLES // SAMPLES_DEV)
    sample_dest = jax.vmap(lambda own, number: deal_out(jax.random.fold_in(streams_of[14], 2), own, number, SAMPLES_DEV, N_DEV, 1, CAP, 2))(sample_dest_keys, sample_dest_turns).reshape((SAMPLES, 1))
    w_in = noise(streams_of[15], (F, D), F ** -0.5, 0.21875)
    gain = jnp.clip(1.0 + 0.15 * jax.random.normal(streams_of[16], (D,), jnp.float32), 0.25, 1.75)
    w_gate = noise(streams_of[17], (D, FF), D ** -0.5, 0.125, ((1, 16),))
    w_up = noise(streams_of[18], (D, FF), D ** -0.5, 0.125, ((1, 16),))
    w_down = noise(streams_of[19], (FF, D), FF ** -0.5, 0.0625, ((0, 16),))
    w_out = noise(streams_of[20], (D, F), D ** -0.5, 0.125)
    return dict(line_pos=line_pos, line_vel=line_vel, stiffness=stiffness, contact=contact, offset=offset, attach=attach, plat_pos=plat_pos, plat_vel=plat_vel, inv_mass=inv_mass, restoring=restoring, kernel=kernel, vel_hist=vel_hist, wave=wave, sample_pick=sample_pick, sample_dest=sample_dest, w_in=w_in, gain=gain, w_gate=w_gate, w_up=w_up, w_down=w_down, w_out=w_out)


HIGH = lax.Precision.HIGHEST

def evolve(line_pos, line_vel, stiffness, contact, offset, attach, plat_pos, plat_vel, inv_mass, restoring, kernel, vel_hist, wave):
    line_ids = jnp.arange(LINES, dtype=jnp.int32)
    owner = attach + line_ids // (LINES_DEV * N_DEV) * PLAT_GRP
    onehot = (owner[None, :] == jnp.arange(PLATS, dtype=jnp.int32)[:, None]).astype(jnp.float32)
    pos, vel = (line_pos, line_vel)
    plat_q, plat_u, history = (plat_pos, plat_vel, vel_hist)
    states = []
    for step in range(STEPS):
        fair = jnp.dot(plat_q, onehot, precision=HIGH) + offset
        fair_vel = jnp.dot(plat_u, onehot, precision=HIGH)
        pos = jnp.concatenate([pos[:, :-1], fair[:, None]], axis=1)
        vel = jnp.concatenate([vel[:, :-1], fair_vel[:, None]], axis=1)
        states.append(pos)
        tension = stiffness[None, :] * (pos[:, -2] - pos[:, -1])
        force = jnp.dot(tension, onehot.T, precision=HIGH)
        touch = contact[step, 1:-1].astype(jnp.float32)
        inner = pos[:, 1:-1]
        accel = stiffness[None, None, :] * (pos[:, 2:] - 2.0 * inner + pos[:, :-2]) - (0.02 + 0.1 * touch)[None] * vel[:, 1:-1]
        lift = -0.05 - 0.3 * touch * (inner[2] + 2.0)
        accel = accel + jnp.stack([jnp.zeros_like(lift), jnp.zeros_like(lift), lift])
        new_vel = vel[:, 1:-1] + accel
        new_pos = inner + new_vel
        pos = jnp.concatenate([pos[:, :1], new_pos, pos[:, -1:]], axis=1)
        vel = jnp.concatenate([vel[:, :1], new_vel, vel[:, -1:]], axis=1)
        memory = lax.optimization_barrier(jnp.sum(kernel * history, axis=0))
        plat_u = plat_u + inv_mass * (force - restoring * plat_q - memory + wave[step])
        plat_q = plat_q + plat_u
        history = jnp.concatenate([plat_u[None], history[:-1]], axis=0)
    fair = jnp.dot(plat_q, onehot, precision=HIGH) + offset
    pos = jnp.concatenate([pos[:, :-1], fair[:, None]], axis=1)
    states.append(pos)
    return (pos, plat_q, jnp.stack(states))

def reference(line_pos, line_vel, stiffness, contact, offset, attach, plat_pos, plat_vel, inv_mass, restoring, kernel, vel_hist, wave, sample_pick, sample_dest, w_in, gain, w_gate, w_up, w_down, w_out):
    final_pos, final_plat, states = evolve(line_pos, line_vel, stiffness, contact, offset, attach, plat_pos, plat_vel, inv_mass, restoring, kernel, vel_hist, wave)
    sample_ids = jnp.arange(SAMPLES, dtype=jnp.int32)
    device = sample_ids // SAMPLES_DEV
    line = (device * LINES_DEV + sample_pick // STEPS).astype(jnp.int32)
    step = (sample_pick % STEPS).astype(jnp.int32)
    inputs = states[step, :, :, line].reshape(SAMPLES, F).astype(jnp.bfloat16)
    targets = states[step + 1, :, :, line].reshape(SAMPLES, F).astype(jnp.bfloat16)
    dest = sample_dest[:, 0].reshape(DEVICES, SAMPLES_DEV)
    hot = (dest[:, :, None] == jnp.arange(N_DEV, dtype=jnp.int32)[None, None, :]).astype(jnp.int32)
    rank = lax.optimization_barrier(jnp.sum((jnp.cumsum(hot, axis=1) - hot) * hot, axis=2))
    slot = (dest * CAP + rank).astype(jnp.int32)

    def place(rows, where):
        return jnp.zeros((N_DEV * CAP, F), jnp.bfloat16).at[where].set(rows)
    send_x = jax.vmap(place)(inputs.reshape(DEVICES, SAMPLES_DEV, F), slot)
    send_t = jax.vmap(place)(targets.reshape(DEVICES, SAMPLES_DEV, F), slot)
    group_rows = N_DEV * N_DEV * CAP
    recv_x = send_x.reshape(N_GRP, N_DEV, N_DEV, CAP, F).transpose(0, 2, 1, 3, 4).reshape(N_GRP, group_rows, F)
    recv_t = send_t.reshape(N_GRP, N_DEV, N_DEV, CAP, F).transpose(0, 2, 1, 3, 4).reshape(N_GRP, group_rows, F)
    block = FF // N_DEV

    def one_group(carry, data):
        rows_x, rows_t = data
        hidden0 = jnp.dot(rows_x, w_in, preferred_element_type=jnp.float32).astype(jnp.bfloat16)
        wide = hidden0.astype(jnp.float32)
        normed = (wide * lax.rsqrt(lax.optimization_barrier(jnp.mean(wide * wide, axis=1, keepdims=True)) + 1e-06) * gain).astype(jnp.bfloat16)
        gate = jnp.dot(normed, w_gate, preferred_element_type=jnp.float32)
        upper = jnp.dot(normed, w_up, preferred_element_type=jnp.float32)
        sigma = jax.nn.sigmoid(gate)
        act = (gate * sigma * upper).astype(jnp.bfloat16)
        out = jnp.zeros((group_rows, D), jnp.float32)
        for index in range(N_DEV):
            part = jnp.dot(act[:, index * block:(index + 1) * block], w_down[index * block:(index + 1) * block], preferred_element_type=jnp.float32)
            part = lax.optimization_barrier(part.astype(jnp.bfloat16))
            out = out + part.astype(jnp.float32)
        hidden1 = (wide + out).astype(jnp.bfloat16)
        err = jnp.dot(hidden1, w_out, preferred_element_type=jnp.float32) - rows_t.astype(jnp.float32)
        dpred = (err / 64.0).astype(jnp.bfloat16)
        dout = lax.dot_general(dpred, w_out, (((1,), (1,)), ((), ())), preferred_element_type=jnp.float32).astype(jnp.bfloat16)
        dact = lax.dot_general(dout, w_down, (((1,), (1,)), ((), ())), preferred_element_type=jnp.float32)
        dgate = (dact * upper * sigma * (1.0 + gate * (1.0 - sigma))).astype(jnp.bfloat16)
        dup = (dact * gate * sigma).astype(jnp.bfloat16)
        grad_g = lax.dot_general(normed, dgate, (((0,), (0,)), ((), ())), preferred_element_type=jnp.float32)
        grad_u = lax.dot_general(normed, dup, (((0,), (0,)), ((), ())), preferred_element_type=jnp.float32)
        return ((carry[0] + grad_g, carry[1] + grad_u), err.astype(jnp.bfloat16))
    start = (jnp.zeros((D, FF), jnp.float32), jnp.zeros((D, FF), jnp.float32))
    grads, errors = lax.scan(one_group, start, (recv_x, recv_t))
    return (final_pos, final_plat, errors.reshape(SLOTS, F), grads[0], grads[1])
```

```python
import functools
import jax
import jax.numpy as jnp
from jax import lax
from jax.experimental import pallas as pl
from jax.experimental.pallas import tpu as pltpu
from jax.sharding import Mesh, PartitionSpec as P

STEPS = 8
CAP = 8
NODES = 256
TAIL = 8
LANES = 128
COUNT = 64
FEATS = 768
ROWS = 72
ONES_ROW = 24
CODE_ROW = 67
HIGH = lax.Precision.HIGHEST
F32 = jnp.float32
BF16 = jnp.bfloat16
DEV = ("zl", "x", "core")
CHIP = ("zl", "x")
GRP = ("y", "zh")
ALL = GRP + DEV
PAIRS = [(s, t) for s in range(2, STEPS) for t in range(1, s)]
SWAP = [(0, 1), (1, 0)]


def nt(left, right, precision=None):
    return lax.dot_general(
        left, right, (((1,), (1,)), ((), ())), precision=precision, preferred_element_type=F32
    )


def iota(shape, dim):
    return lax.broadcasted_iota(jnp.int32, shape, dim)


def pick_matrix(pick_ref):
    count = pick_ref.shape[1]
    eye = iota((count, count), 0) == iota((count, count), 1)
    pick = jnp.sum(jnp.where(eye, pick_ref[...].astype(F32), 0.0), axis=1, keepdims=True).astype(jnp.int32)
    at = (pick >> 3) + LANES * (pick & 7)
    at = jnp.concatenate([at, at + LANES], axis=0)
    return (iota((2 * count, LANES * (STEPS + 1)), 1) == at).astype(F32).astype(BF16)


def evolve_kernel(
    pos_ref, vel_ref, stiff_ref, contact_ref, off_ref, attach_ref, plat_ref, pick_ref, dest_ref,
    pay_ref, rows_ref, bound_ref, fpos_ref, stack, lin,
):
    k = stiff_ref[...]
    onehot = (attach_ref[...] == iota((LANES, LANES), 0)).astype(F32)
    off = off_ref[...]
    fair = jnp.dot(plat_ref[...], onehot, precision=HIGH, preferred_element_type=F32) + off
    row = iota((NODES, LANES), 0)
    first, last, bulk = row == 0, row == NODES - 1, row < NODES - TAIL
    lin[...] = jnp.zeros_like(lin)
    lin[ONES_ROW : ONES_ROW + 1] = jnp.ones((1, LANES), F32)
    pos = [jnp.where(last, fair[c : c + 1], pos_ref[c]) for c in range(3)]
    vel = [vel_ref[c] for c in range(3)]
    for step in range(STEPS):
        touch = contact_ref[step].astype(F32)
        damp = 0.02 + 0.1 * touch
        for c in range(3):
            p = pos[c]
            stack[c * NODES : (c + 1) * NODES, step * LANES : (step + 1) * LANES] = jnp.where(bulk, p, 0.0).astype(BF16)
            bound_ref[step * 3 + c : step * 3 + c + 1] = p[NODES - TAIL - 1 : NODES - TAIL]
            lin[step * 3 + c : step * 3 + c + 1] = p[NODES - 2 : NODES - 1] - p[NODES - 1 : NODES]
            accel = k * (pltpu.roll(p, NODES - 1, 0) - 2.0 * p + pltpu.roll(p, 1, 0)) - damp * vel[c]
            if c == 2:
                accel = accel + (-0.05 - 0.3 * touch * (p + 2.0))
            vel[c] = vel[c] + accel
            pos[c] = jnp.where(first, p, jnp.where(last, off[c : c + 1], p + vel[c]))
    for c in range(3):
        stack[c * NODES : (c + 1) * NODES, STEPS * LANES :] = jnp.where(bulk, pos[c], 0.0).astype(BF16)
        fpos_ref[c] = pos[c]
    rows_ref[...] = nt(pick_matrix(pick_ref), stack[...]).astype(BF16)
    trow = iota((TAIL, LANES), 0)
    zero = jnp.zeros((TAIL, LANES), F32)
    for kind in range(2):
        rp, rv = [zero] * 6, [zero] * 6
        for step in range(1, STEPS):
            for t in range(1, step):
                at = ONES_ROW + 1 + 2 * PAIRS.index((step, t)) + kind
                lin[at : at + 1] = rp[t - 1][TAIL - 2 : TAIL - 1]
            if step == STEPS - 1:
                break
            touch = contact_ref[step, NODES - TAIL : NODES].astype(F32)
            damp = 0.02 + 0.1 * touch
            for t in range(1, step + 1):
                p = jnp.where(trow == TAIL - 1, 1.0 if t == step else 0.0, rp[t - 1])
                up = pltpu.roll(p, TAIL - 1, 0)
                down = jnp.where(trow == 0, 0.0, pltpu.roll(p, 1, 0))
                accel = k * (up - 2.0 * p + down) - damp * rv[t - 1]
                if kind == 1:
                    accel = accel - 0.3 * touch * p
                rv[t - 1] = rv[t - 1] + accel
                rp[t - 1] = p + rv[t - 1]
    sums = nt(lin[...] * k, onehot, HIGH)
    count = dest_ref.shape[0]
    lane, sub = iota((count, LANES), 1), iota((count, LANES), 0)
    dest_col = dest_ref[...].astype(F32)
    dest = jnp.sum(jnp.where(lane == sub, dest_col, 0.0), axis=0, keepdims=True)
    rank = jnp.sum(jnp.where((dest_col == dest) & (sub < lane), 1.0, 0.0), axis=0, keepdims=True)
    codes = jnp.where(iota((1, LANES), 1) < count, dest * CAP + rank, -1.0)
    pay_ref[...] = jnp.where(iota((ROWS, LANES), 0) == CODE_ROW, codes, sums)


def finish_kernel(
    recv_ref, plat_ref, plat_vel_ref, inv_ref, rest_ref, kern_ref, hist_ref, wave_ref,
    pos_ref, vel_ref, contact_ref, stiff_ref, off_ref, attach_ref, pick_ref, bound_ref, rows_ref, fpos_in,
    x_ref, t_ref, plat_out, fpos_ref, tails, final, sem,
):
    total = recv_ref[0]
    for d in range(1, recv_ref.shape[0]):
        total = total + recv_ref[d]
    q, u = plat_ref[...], plat_vel_ref[...]
    hist = [hist_ref[m] for m in range(STEPS)]
    ones = total[ONES_ROW : ONES_ROW + 1]
    qs = [q]
    for step in range(STEPS):
        force = total[3 * step : 3 * step + 3]
        if step > 0:
            force = force - ones * q
        for t in range(1, step):
            at = ONES_ROW + 1 + 2 * PAIRS.index((step, t))
            coef = jnp.concatenate([total[at : at + 1], total[at : at + 2]], axis=0)
            force = force + coef * qs[t]
        memory = kern_ref[0] * hist[0]
        for m in range(1, STEPS):
            memory = memory + kern_ref[m] * hist[m]
        u = u + inv_ref[...] * (force - rest_ref[...] * q - memory + wave_ref[step])
        q = q + u
        hist = [u] + hist[:-1]
        qs.append(q)
    plat_out[...] = q
    k = stiff_ref[...]
    onehot = (attach_ref[...] == iota((LANES, LANES), 0)).astype(F32)
    fair = jnp.dot(jnp.concatenate(qs, axis=0), onehot, precision=HIGH, preferred_element_type=F32)
    trow = iota((TAIL, LANES), 0)
    pos = [pos_ref[c] for c in range(3)]
    vel = [vel_ref[c] for c in range(3)]
    for step in range(STEPS + 1):
        for c in range(3):
            here = fair[step * 3 + c : step * 3 + c + 1] + off_ref[c : c + 1]
            p = jnp.where(trow == TAIL - 1, here, pos[c])
            tails[c * TAIL : (c + 1) * TAIL, step * LANES : (step + 1) * LANES] = p
            if step == STEPS:
                final[c] = p
                continue
            touch = contact_ref[step].astype(F32)
            up = pltpu.roll(p, TAIL - 1, 0)
            bound = bound_ref[step * 3 + c : step * 3 + c + 1]
            down = jnp.where(trow == 0, bound, pltpu.roll(p, 1, 0))
            accel = k * (up - 2.0 * p + down) - (0.02 + 0.1 * touch) * vel[c]
            if c == 2:
                accel = accel + (-0.05 - 0.3 * touch * (p + 2.0))
            vel[c] = vel[c] + accel
            pos[c] = p + vel[c]
    copy = pltpu.make_async_copy(final, fpos_ref.at[:, NODES - TAIL : NODES, :], sem)
    copy.start()
    picked = nt(pick_matrix(pick_ref), tails[...].astype(BF16)).astype(BF16)
    at = iota((3 * TAIL, FEATS), 0)
    where = (at // TAIL) * NODES + (NODES - TAIL) + at % TAIL
    place = (iota((3 * TAIL, FEATS), 1) == where).astype(F32).astype(BF16)
    rows = rows_ref[...].astype(F32) + jnp.dot(picked, place, preferred_element_type=F32)
    count = x_ref.shape[0]
    x_ref[...] = rows[:count].astype(BF16)
    t_ref[...] = rows[count:].astype(BF16)
    copy.wait()


VM = pl.BlockSpec(memory_space=pltpu.VMEM)


def evolve(line_pos, line_vel, stiff, contact, offset, attach, plat_pos, pick, dest):
    sds = jax.ShapeDtypeStruct
    return pl.pallas_call(
        evolve_kernel,
        out_shape=(
            sds((ROWS, LANES), F32),
            sds((2 * COUNT, FEATS), BF16),
            sds((3 * STEPS, LANES), F32),
            sds((3, NODES, LANES), F32),
        ),
        in_specs=[VM] * 9,
        out_specs=(VM,) * 4,
        scratch_shapes=[
            pltpu.VMEM((3 * NODES, LANES * (STEPS + 1)), BF16),
            pltpu.VMEM((ROWS, LANES), F32),
        ],
        compiler_params=pltpu.CompilerParams(vmem_limit_bytes=40 * 1024 * 1024),
        name="evolve",
    )(line_pos, line_vel, stiff, contact, offset, attach, plat_pos, pick, dest)


def finish(recv, plats, lines, bound, rows, fpos):
    sds = jax.ShapeDtypeStruct
    whole = lambda a: pl.BlockSpec(a.shape, lambda i: (0,) * a.ndim)
    tail = lambda a: pl.BlockSpec((a.shape[0], TAIL, LANES), lambda i: (0, NODES // TAIL - 1, 0))
    line_pos, line_vel, contact, stiff, offset, attach, pick = lines
    args = (recv, *plats, line_pos, line_vel, contact, stiff, offset, attach, pick, bound, rows)
    specs = [whole(a) for a in args]
    at = 1 + len(plats)
    for i in range(at, at + 3):
        specs[i] = tail(args[i])
    out = (sds((COUNT, FEATS), BF16), sds((COUNT, FEATS), BF16), sds((3, LANES), F32))
    return pl.pallas_call(
        finish_kernel,
        grid=(1,),
        out_shape=out + (sds(fpos.shape, F32),),
        in_specs=specs + [pl.BlockSpec(memory_space=pl.ANY)],
        out_specs=tuple(whole(a) for a in out) + (pl.BlockSpec(memory_space=pl.ANY),),
        scratch_shapes=[
            pltpu.VMEM((3 * TAIL, LANES * (STEPS + 1)), F32),
            pltpu.VMEM((3, TAIL, LANES), F32),
            pltpu.SemaphoreType.DMA,
        ],
        input_output_aliases={len(args): 3},
        compiler_params=pltpu.CompilerParams(vmem_limit_bytes=40 * 1024 * 1024),
        name="finish",
    )(*args, fpos)


def exchange(x, axes):
    return lax.all_to_all(x, axes, split_axis=0, concat_axis=0, tiled=True)


def spread(x, axes):
    return exchange(jnp.broadcast_to(x[None], (lax.axis_size(axes),) + x.shape), axes)


def body(
    line_pos, line_vel, stiffness, contact, offset, attach, plat_pos, plat_vel, inv_mass, restoring,
    kernel, vel_hist, wave, sample_pick, sample_dest, w_in, gain, w_gate, w_up, w_down, w_out,
):
    chips = lax.axis_size(CHIP)
    half = chips * COUNT
    stiff, att, pick = stiffness[None], attach[None], sample_pick[None]
    pay, rows, bound, fpos = evolve(
        line_pos, line_vel, stiff, contact, offset, att, plat_pos, pick, sample_dest
    )
    recv = spread(pay, DEV)
    x_own, target, final_plat, final_pos = finish(
        recv,
        (plat_pos, plat_vel, inv_mass, restoring, kernel, vel_hist, wave),
        (line_pos, line_vel, contact, stiff, offset, att, pick),
        bound, rows, fpos,
    )
    x_mine = spread(x_own, CHIP).reshape(half, FEATS)
    x_other = lax.ppermute(x_mine, "core", SWAP)
    x_all = jnp.concatenate([x_mine, x_other], axis=0)
    fused = jnp.dot(w_down, w_out, preferred_element_type=F32).astype(BF16)
    hidden = jnp.dot(x_all, w_in, preferred_element_type=F32).astype(BF16)
    wide = hidden.astype(F32)
    normed = (wide * lax.rsqrt(jnp.mean(wide * wide, axis=1, keepdims=True) + 1e-06) * gain).astype(BF16)
    gate = jnp.dot(normed, w_gate, preferred_element_type=F32)
    upper = jnp.dot(normed, w_up, preferred_element_type=F32)
    sigma = jax.nn.sigmoid(gate)
    act = (gate * sigma * upper).astype(BF16)
    part = jnp.dot(act, fused, preferred_element_type=F32)
    from_core = lax.ppermute(part[half:].astype(BF16), "core", SWAP)
    both = (part[:half] + from_core.astype(F32)).astype(BF16)
    parts = exchange(both.reshape(chips, COUNT, FEATS), CHIP)
    chip = lax.axis_index(CHIP)
    core = lax.axis_index("core")
    own_hidden = lax.dynamic_slice_in_dim(hidden, chip * COUNT, COUNT, 0)
    err = (
        jnp.dot(own_hidden, w_out, preferred_element_type=F32)
        + jnp.sum(parts.astype(F32), axis=0)
        - target.astype(F32)
    ).astype(BF16)
    err_mine = spread(err, CHIP).reshape(half, FEATS)
    err_other = lax.ppermute(err_mine, "core", SWAP)
    err_all = jnp.concatenate([err_mine, err_other], axis=0)
    dpred = (err_all.astype(F32) / 64.0).astype(BF16)
    dact = nt(dpred, fused)
    dgate = (dact * upper * sigma * (1.0 + gate * (1.0 - sigma))).astype(BF16)
    dup = (dact * gate * sigma).astype(BF16)
    joined = jnp.concatenate([dgate, dup], axis=1)
    width = dgate.shape[1]
    grads = lax.dot_general(normed, joined, (((0,), (0,)), ((), ())), preferred_element_type=F32).astype(BF16)
    groups = lax.axis_size(GRP)
    grads = exchange(grads.reshape(groups, -1, 2 * width), GRP)
    grads = jnp.sum(grads.astype(F32), axis=0)
    codes = recv[:, CODE_ROW, :COUNT].reshape(chips, 2, COUNT)
    codes = lax.dynamic_slice_in_dim(jnp.concatenate([codes, codes], axis=1), core, 2, 1)
    codes = codes.transpose(1, 0, 2).reshape(1, 2 * half)
    me = chip * 2 + core
    number = jnp.arange(2 * half, dtype=jnp.int32)
    source = ((number // COUNT) % chips) * 2 + (number // half + core) % 2
    slot = jnp.arange(2 * chips * CAP, dtype=jnp.int32)[:, None]
    match = (source[None] == slot // CAP) & (codes == (me * CAP + slot % CAP).astype(F32))
    slot_error = jnp.dot(match.astype(BF16), err_all, preferred_element_type=F32).astype(BF16)
    return (final_pos, final_plat, slot_error, grads[:, :width], grads[:, width:])


def solution(mesh):
    sizes = (4, 2, 2, 4, 2)
    if mesh.devices.shape[0] == 1:
        sizes = (1, 1, 2, 4, 2)
    fine = Mesh(mesh.devices.reshape(sizes), ALL)
    in_specs = (
        P(None, None, ALL),
        P(None, None, ALL),
        P(ALL),
        P(None, None, ALL),
        P(None, ALL),
        P(ALL),
        P(None, GRP),
        P(None, GRP),
        P(None, GRP),
        P(None, GRP),
        P(None, None, GRP),
        P(None, None, GRP),
        P(None, None, GRP),
        P(ALL),
        P(ALL, None),
        P(),
        P(),
        P(None, DEV),
        P(None, DEV),
        P(DEV, None),
        P(),
    )
    out_specs = (
        P(None, None, ALL),
        P(None, GRP),
        P(ALL, None),
        P(GRP, DEV),
        P(GRP, DEV),
    )
    return jax.shard_map(body, mesh=fine, in_specs=in_specs, out_specs=out_specs, check_vma=False)
```

```python
import functools
import jax
import jax.numpy as jnp
from jax import lax
from jax.experimental import pallas as pl
from jax.experimental.pallas import tpu as pltpu
from jax.sharding import Mesh, PartitionSpec as P

STEPS = 8
CAP = 8
NODES = 256
TAIL = 8
LANES = 128
COUNT = 64
FEATS = 768
ROWS = 72
ONES_ROW = 24
CODE_ROW = 67
HIGH = lax.Precision.HIGHEST
F32 = jnp.float32
BF16 = jnp.bfloat16
DEV = ("zl", "x", "core")
CHIP = ("zl", "x")
GRP = ("y", "zh")
ALL = GRP + DEV
PAIRS = [(s, t) for s in range(2, STEPS) for t in range(1, s)]
SWAP = [(0, 1), (1, 0)]


def nt(left, right, precision=None):
    return lax.dot_general(
        left, right, (((1,), (1,)), ((), ())), precision=precision, preferred_element_type=F32
    )


def iota(shape, dim):
    return lax.broadcasted_iota(jnp.int32, shape, dim)


def pick_matrix(pick_ref):
    count = pick_ref.shape[1]
    eye = iota((count, count), 0) == iota((count, count), 1)
    pick = jnp.sum(jnp.where(eye, pick_ref[...].astype(F32), 0.0), axis=1, keepdims=True).astype(jnp.int32)
    at = (pick >> 3) + LANES * (pick & 7)
    at = jnp.concatenate([at, at + LANES], axis=0)
    return (iota((2 * count, LANES * (STEPS + 1)), 1) == at).astype(F32).astype(BF16)


def fetch(refs, bufs, sem):
    copies = [pltpu.make_async_copy(r, b, sem.at[i]) for i, (r, b) in enumerate(zip(refs, bufs))]
    for c in copies:
        c.start()
    return copies


def evolve_kernel(
    pos_ref, vel_ref, stiff_ref, contact_ref, off_ref, attach_ref, plat_ref, pick_ref, dest_ref,
    pay_ref, rows_ref, bound_ref, fpos_ref,
    posb, velb, contactb, stiffb, offb, attachb, platb, pickb, destb, stack, lin, sem,
):
    small = fetch(
        (stiff_ref, off_ref, attach_ref, plat_ref, pick_ref, dest_ref),
        (stiffb, offb, attachb, platb, pickb, destb),
        sem.at[0],
    )
    large = fetch(
        (pos_ref, vel_ref) + tuple(contact_ref.at[s] for s in range(STEPS)),
        (posb, velb) + tuple(contactb.at[s] for s in range(STEPS)),
        sem.at[1],
    )
    for c in small:
        c.wait()
    k = stiffb[...]
    onehot = (attachb[...] == iota((LANES, LANES), 0)).astype(F32)
    off = offb[...]
    fair = jnp.dot(platb[...], onehot, precision=HIGH, preferred_element_type=F32) + off
    picks = pick_matrix(pickb)
    row = iota((NODES, LANES), 0)
    first, last, bulk = row == 0, row == NODES - 1, row < NODES - TAIL
    lin[...] = jnp.zeros_like(lin)
    lin[ONES_ROW : ONES_ROW + 1] = jnp.ones((1, LANES), F32)
    large[0].wait()
    large[1].wait()
    pos = [jnp.where(last, fair[c : c + 1], posb[c]) for c in range(3)]
    vel = [velb[c] for c in range(3)]
    for step in range(STEPS):
        large[2 + step].wait()
        touch = contactb[step].astype(F32)
        damp = 0.02 + 0.1 * touch
        for c in range(3):
            p = pos[c]
            stack[c * NODES : (c + 1) * NODES, step * LANES : (step + 1) * LANES] = jnp.where(bulk, p, 0.0).astype(BF16)
            bound_ref[step * 3 + c : step * 3 + c + 1] = p[NODES - TAIL - 1 : NODES - TAIL]
            lin[step * 3 + c : step * 3 + c + 1] = p[NODES - 2 : NODES - 1] - p[NODES - 1 : NODES]
            accel = k * (pltpu.roll(p, NODES - 1, 0) - 2.0 * p + pltpu.roll(p, 1, 0)) - damp * vel[c]
            if c == 2:
                accel = accel + (-0.05 - 0.3 * touch * (p + 2.0))
            vel[c] = vel[c] + accel
            pos[c] = jnp.where(first, p, jnp.where(last, off[c : c + 1], p + vel[c]))
    for c in range(3):
        stack[c * NODES : (c + 1) * NODES, STEPS * LANES :] = jnp.where(bulk, pos[c], 0.0).astype(BF16)
        fpos_ref[c] = pos[c]
    rows_ref[...] = nt(picks, stack[...]).astype(BF16)
    trow = iota((TAIL, LANES), 0)
    zero = jnp.zeros((TAIL, LANES), F32)
    for kind in range(2):
        rp, rv = [zero] * 6, [zero] * 6
        for step in range(1, STEPS):
            for t in range(1, step):
                at = ONES_ROW + 1 + 2 * PAIRS.index((step, t)) + kind
                lin[at : at + 1] = rp[t - 1][TAIL - 2 : TAIL - 1]
            if step == STEPS - 1:
                break
            touch = contactb[step, NODES - TAIL : NODES].astype(F32)
            damp = 0.02 + 0.1 * touch
            for t in range(1, step + 1):
                p = jnp.where(trow == TAIL - 1, 1.0 if t == step else 0.0, rp[t - 1])
                up = pltpu.roll(p, TAIL - 1, 0)
                down = jnp.where(trow == 0, 0.0, pltpu.roll(p, 1, 0))
                accel = k * (up - 2.0 * p + down) - damp * rv[t - 1]
                if kind == 1:
                    accel = accel - 0.3 * touch * p
                rv[t - 1] = rv[t - 1] + accel
                rp[t - 1] = p + rv[t - 1]
    sums = nt(lin[...] * k, onehot, HIGH)
    count = destb.shape[1]
    lane, sub = iota((count, count), 1), iota((count, count), 0)
    dest = destb[...].astype(F32)
    dest_col = jnp.sum(jnp.where(lane == sub, dest, 0.0), axis=1, keepdims=True)
    rank = jnp.sum(jnp.where((dest_col == dest) & (sub < lane), 1.0, 0.0), axis=0, keepdims=True)
    codes = jnp.concatenate([dest * CAP + rank, jnp.full((1, LANES - count), -1.0, F32)], axis=1)
    pay_ref[...] = jnp.where(iota((ROWS, LANES), 0) == CODE_ROW, codes, sums)


def finish_kernel(
    recv_ref, bound_ref, rows_ref, plat_ref, plat_vel_ref, inv_ref, rest_ref, kern_ref, hist_ref, wave_ref,
    pos_ref, vel_ref, contact_ref, stiff_ref, off_ref, attach_ref, pick_ref, w_in_ref, fpos_in,
    x_ref, t_ref, h_ref, plat_out, fpos_ref,
    recvb, boundb, rowsb, platb, plat_velb, invb, restb, kernb, histb, waveb,
    posb, velb, contactb, stiffb, offb, attachb, pickb, w_inb, tails, final, sem, out_sem,
):
    at = pl.ds(NODES - TAIL, TAIL)
    copies = fetch(
        (
            recv_ref, plat_ref, plat_vel_ref, inv_ref, rest_ref, kern_ref, hist_ref, wave_ref,
            stiff_ref, off_ref, attach_ref, pick_ref, bound_ref, rows_ref,
            pos_ref.at[:, at, :], vel_ref.at[:, at, :], contact_ref.at[:, at, :], w_in_ref,
        ),
        (
            recvb, platb, plat_velb, invb, restb, kernb, histb, waveb,
            stiffb, offb, attachb, pickb, boundb, rowsb, posb, velb, contactb, w_inb,
        ),
        sem,
    )
    for c in copies[:-1]:
        c.wait()
    total = recvb[0]
    for d in range(1, recvb.shape[0]):
        total = total + recvb[d]
    q, u = platb[...], plat_velb[...]
    hist = [histb[:, m] for m in range(STEPS)]
    kern = [kernb[:, m] for m in range(STEPS)]
    ones = total[ONES_ROW : ONES_ROW + 1]
    qs = [q]
    for step in range(STEPS):
        force = total[3 * step : 3 * step + 3]
        if step > 0:
            force = force - ones * q
        for t in range(1, step):
            at = ONES_ROW + 1 + 2 * PAIRS.index((step, t))
            coef = jnp.concatenate([total[at : at + 1], total[at : at + 2]], axis=0)
            force = force + coef * qs[t]
        memory = kern[0] * hist[0]
        for m in range(1, STEPS):
            memory = memory + kern[m] * hist[m]
        u = u + invb[...] * (force - restb[...] * q - memory + waveb[:, step])
        q = q + u
        hist = [u] + hist[:-1]
        qs.append(q)
    plat_out[...] = q
    k = stiffb[...]
    onehot = (attachb[...] == iota((LANES, LANES), 0)).astype(F32)
    fair = jnp.dot(jnp.concatenate(qs, axis=0), onehot, precision=HIGH, preferred_element_type=F32)
    trow = iota((TAIL, LANES), 0)
    pos = [posb[c] for c in range(3)]
    vel = [velb[c] for c in range(3)]
    for step in range(STEPS + 1):
        for c in range(3):
            here = fair[step * 3 + c : step * 3 + c + 1] + offb[c : c + 1]
            p = jnp.where(trow == TAIL - 1, here, pos[c])
            tails[c * TAIL : (c + 1) * TAIL, step * LANES : (step + 1) * LANES] = p
            if step == STEPS:
                final[c] = p
                continue
            touch = contactb[step].astype(F32)
            up = pltpu.roll(p, TAIL - 1, 0)
            bound = boundb[step * 3 + c : step * 3 + c + 1]
            down = jnp.where(trow == 0, bound, pltpu.roll(p, 1, 0))
            accel = k * (up - 2.0 * p + down) - (0.02 + 0.1 * touch) * vel[c]
            if c == 2:
                accel = accel + (-0.05 - 0.3 * touch * (p + 2.0))
            vel[c] = vel[c] + accel
            pos[c] = p + vel[c]
    copy = pltpu.make_async_copy(final, fpos_ref.at[:, NODES - TAIL : NODES, :], out_sem)
    copy.start()
    picked = nt(pick_matrix(pickb), tails[...].astype(BF16)).astype(BF16)
    at = iota((3 * TAIL, FEATS), 0)
    where = (at // TAIL) * NODES + (NODES - TAIL) + at % TAIL
    place = (iota((3 * TAIL, FEATS), 1) == where).astype(F32).astype(BF16)
    rows = rowsb[...].astype(F32) + jnp.dot(picked, place, preferred_element_type=F32)
    count = x_ref.shape[0]
    t_ref[...] = rows[count:].astype(BF16)
    copies[-1].wait()
    hidden = jnp.dot(rows[:count].astype(BF16), w_inb[...], preferred_element_type=F32).astype(BF16)
    h_ref[...] = hidden
    wide = hidden.astype(F32)
    scale = lax.rsqrt(jnp.mean(wide * wide, axis=1, keepdims=True) + 1e-06)
    x_ref[...] = (rows[:count] * scale).astype(BF16)
    copy.wait()


VM = pl.BlockSpec(memory_space=pltpu.VMEM)
HB = pl.BlockSpec(memory_space=pltpu.HBM)


def vmem_like(a, tail=False):
    shape = (a.shape[0], TAIL, LANES) if tail else a.shape
    return pltpu.VMEM(shape, a.dtype)


def evolve(line_pos, line_vel, stiff, contact, offset, attach, plat_pos, pick, dest):
    sds = jax.ShapeDtypeStruct
    large = (line_pos, line_vel, contact)
    small = (stiff, offset, attach, plat_pos, pick, dest)
    return pl.pallas_call(
        evolve_kernel,
        out_shape=(
            sds((ROWS, LANES), F32),
            sds((2 * COUNT, FEATS), BF16),
            sds((3 * STEPS, LANES), F32),
            sds((3, NODES, LANES), F32),
        ),
        in_specs=[HB] * 9,
        out_specs=(VM,) * 4,
        scratch_shapes=[vmem_like(a) for a in large + small]
        + [
            pltpu.VMEM((3 * NODES, LANES * (STEPS + 1)), BF16),
            pltpu.VMEM((ROWS, LANES), F32),
            pltpu.SemaphoreType.DMA((2, 2 + STEPS)),
        ],
        compiler_params=pltpu.CompilerParams(vmem_limit_bytes=32 * 1024 * 1024),
        cost_estimate=pl.CostEstimate(flops=260000000, bytes_accessed=3000000, transcendentals=0),
        name="evolve",
    )(line_pos, line_vel, stiff, contact, offset, attach, plat_pos, pick, dest)


def finish(recv, bound, rows, plats, lines, w_in, fpos):
    sds = jax.ShapeDtypeStruct
    args = (recv, bound, rows, *plats, *lines, w_in)
    at = 3 + len(plats)
    bufs = [vmem_like(a, at <= i < at + 3) for i, a in enumerate(args)]
    out = (
        sds((COUNT, FEATS), BF16),
        sds((COUNT, FEATS), BF16),
        sds((COUNT, w_in.shape[1]), BF16),
        sds((3, LANES), F32),
    )
    return pl.pallas_call(
        finish_kernel,
        out_shape=out + (sds(fpos.shape, F32),),
        in_specs=[HB] * (len(args) + 1),
        out_specs=(VM,) * len(out) + (HB,),
        scratch_shapes=bufs
        + [
            pltpu.VMEM((3 * TAIL, LANES * (STEPS + 1)), F32),
            pltpu.VMEM((3, TAIL, LANES), F32),
            pltpu.SemaphoreType.DMA((len(args),)),
            pltpu.SemaphoreType.DMA,
        ],
        input_output_aliases={len(args): len(out)},
        compiler_params=pltpu.CompilerParams(vmem_limit_bytes=32 * 1024 * 1024),
        cost_estimate=pl.CostEstimate(flops=300000000, bytes_accessed=4000000, transcendentals=0),
        name="finish",
    )(*args, fpos)


def exchange(x, axes):
    return lax.all_to_all(x, axes, split_axis=0, concat_axis=0, tiled=True)


def spread(x, axes):
    return exchange(jnp.broadcast_to(x[None], (lax.axis_size(axes),) + x.shape), axes)


def dot(left, right):
    return jnp.dot(left, right, preferred_element_type=F32)


def tn(left, right):
    return lax.dot_general(left, right, (((0,), (0,)), ((), ())), preferred_element_type=F32)


def swap(x):
    return lax.ppermute(x, "core", SWAP)


def body(
    line_pos, line_vel, stiffness, contact, offset, attach, plat_pos, plat_vel, inv_mass, restoring,
    kernel, vel_hist, wave, sample_pick, sample_dest, w_in, gain, w_gate, w_up, w_down, w_out,
):
    chips = lax.axis_size(CHIP)
    groups = lax.axis_size(GRP)
    half = chips * COUNT
    width = w_gate.shape[1]
    stiff, att, pick, dest = stiffness[None], attach[None], sample_pick[None], sample_dest.reshape(1, -1)
    pay, rows, bound, fpos = evolve(
        line_pos, line_vel, stiff, contact, offset, att, plat_pos, pick, dest
    )
    other = swap(pay)
    pay = jnp.concatenate(
        [pay[:CODE_ROW] + other[:CODE_ROW], pay[CODE_ROW : CODE_ROW + 1], other[CODE_ROW : CODE_ROW + 1], pay[CODE_ROW + 2 :]],
        axis=0,
    )
    recv = spread(pay, CHIP)
    scaled = (w_in.astype(F32) * gain).astype(BF16)
    gate_w = dot(scaled, w_gate).astype(BF16)
    up_w = dot(scaled, w_up).astype(BF16)
    down_w = dot(w_down, w_out).astype(BF16)
    gate_w = jnp.concatenate([gate_w, swap(gate_w)], axis=1)
    up_w = jnp.concatenate([up_w, swap(up_w)], axis=1)
    down_w = jnp.concatenate([down_w, swap(down_w)], axis=0)
    turned = lambda a: a.transpose(1, 0, 2)
    x_own, target, hidden, final_plat, final_pos = finish(
        recv, bound, rows,
        (plat_pos, plat_vel, inv_mass, restoring, turned(kernel), turned(vel_hist), turned(wave)),
        (line_pos, line_vel, contact, stiff, offset, att, pick),
        w_in, fpos,
    )
    x = spread(x_own, CHIP).reshape(half, FEATS)
    base = lax.optimization_barrier(dot(hidden, w_out) - target.astype(F32))
    gate = dot(x, gate_w)
    upper = dot(x, up_w)
    sigma = jax.nn.sigmoid(gate)
    act = (gate * sigma * upper).astype(BF16)
    part = dot(act, down_w).astype(BF16)
    parts = exchange(part.reshape(chips, COUNT, FEATS), CHIP)
    err = (base + jnp.sum(parts.astype(F32), axis=0)).astype(BF16)
    err_mine = spread(err, CHIP).reshape(half, FEATS)
    dpred = (err_mine.astype(F32) / 64.0).astype(BF16)
    dact = nt(dpred, down_w)
    dgate = (dact * upper * sigma * (1.0 + gate * (1.0 - sigma))).astype(BF16)
    dup = (dact * gate * sigma).astype(BF16)
    theirs = swap(tn(x, jnp.concatenate([dgate[:, width:], dup[:, width:]], axis=1)).astype(BF16))
    mine = tn(x, jnp.concatenate([dgate[:, :width], dup[:, :width]], axis=1))
    feat_grads = (mine + theirs.astype(F32)).astype(BF16)
    feat_grads = exchange(feat_grads.reshape(groups, FEATS // groups, 2 * width), GRP)
    feat_grads = jnp.sum(feat_grads.astype(F32), axis=0).astype(BF16)
    feat_grads = spread(feat_grads, GRP).reshape(FEATS, 2 * width)
    at = lax.axis_index(GRP)
    block = w_in.shape[1] // groups
    w_in_own = lax.dynamic_slice_in_dim(w_in, at * block, block, 1)
    gain_own = lax.dynamic_slice_in_dim(gain, at * block, block, 0)[:, None]
    grad_gate = gain_own * tn(w_in_own, feat_grads[:, :width])
    grad_up = gain_own * tn(w_in_own, feat_grads[:, width:])
    err_all = jnp.concatenate([err_mine, swap(err_mine)], axis=0)
    codes = recv[:, CODE_ROW : CODE_ROW + 2, :COUNT].transpose(1, 0, 2).reshape(1, 2 * half)
    core = lax.axis_index("core")
    me = lax.axis_index(CHIP) * 2 + core
    number = jnp.arange(2 * half, dtype=jnp.int32)
    source = ((number // COUNT) % chips) * 2 + (number // half + core) % 2
    slot = jnp.arange(2 * chips * CAP, dtype=jnp.int32)[:, None]
    match = (source[None] == slot // CAP) & (codes == (me * CAP + slot % CAP).astype(F32))
    slot_error = dot(match.astype(BF16), err_all).astype(BF16)
    return (final_pos, final_plat, slot_error, grad_gate, grad_up)


def solution(mesh):
    sizes = (4, 2, 2, 4, 2)
    if mesh.devices.shape[0] == 1:
        sizes = (1, 1, 2, 4, 2)
    fine = Mesh(mesh.devices.reshape(sizes), ALL)
    in_specs = (
        P(None, None, ALL),
        P(None, None, ALL),
        P(ALL),
        P(None, None, ALL),
        P(None, ALL),
        P(ALL),
        P(None, GRP),
        P(None, GRP),
        P(None, GRP),
        P(None, GRP),
        P(None, None, GRP),
        P(None, None, GRP),
        P(None, None, GRP),
        P(ALL),
        P(ALL, None),
        P(),
        P(),
        P(None, DEV),
        P(None, DEV),
        P(DEV, None),
        P(),
    )
    out_specs = (
        P(None, None, ALL),
        P(None, GRP),
        P(ALL, None),
        P(GRP, DEV),
        P(GRP, DEV),
    )
    return jax.shard_map(body, mesh=fine, in_specs=in_specs, out_specs=out_specs, check_vma=False)
```

```python
import functools
import jax
import jax.numpy as jnp
from jax import lax
from jax.experimental import pallas as pl
from jax.experimental.pallas import tpu as pltpu
from jax.sharding import Mesh, PartitionSpec as P

STEPS = 8
CAP = 8
NODES = 256
TAIL = 8
LANES = 128
COUNT = 64
FEATS = 768
ROWS = 72
ONES_ROW = 24
CODE_ROW = 67
LIMIT = 60 * 1024 * 1024
HIGH = lax.Precision.HIGHEST
F32 = jnp.float32
BF16 = jnp.bfloat16
DEV = ("zl", "x", "core")
CHIP = ("zl", "x")
GRP = ("y", "zh")
ALL = GRP + DEV
PAIRS = [(s, t) for s in range(2, STEPS) for t in range(1, s)]
SWAP = [(0, 1), (1, 0)]


def nt(left, right, precision=None):
    return lax.dot_general(
        left, right, (((1,), (1,)), ((), ())), precision=precision, preferred_element_type=F32
    )


def iota(shape, dim):
    return lax.broadcasted_iota(jnp.int32, shape, dim)


def pick_matrix(pick_ref):
    count = pick_ref.shape[1]
    eye = iota((count, count), 0) == iota((count, count), 1)
    pick = jnp.sum(jnp.where(eye, pick_ref[...].astype(F32), 0.0), axis=1, keepdims=True).astype(jnp.int32)
    at = (pick >> 3) + LANES * (pick & 7)
    at = jnp.concatenate([at, at + LANES], axis=0)
    return (iota((2 * count, LANES * (STEPS + 1)), 1) == at).astype(F32).astype(BF16)


def fetch(refs, bufs, sem):
    copies = [pltpu.make_async_copy(r, b, sem.at[i]) for i, (r, b) in enumerate(zip(refs, bufs))]
    for c in copies:
        c.start()
    return copies


def evolve_kernel(
    pos_ref, vel_ref, stiff_ref, contact_ref, off_ref, attach_ref, plat_ref, pick_ref, dest_ref,
    pay_ref, rows_ref, bound_ref, fpos_ref,
    posb, velb, contactb, stiffb, offb, attachb, platb, pickb, destb, stack, lin, sem,
):
    small = fetch(
        (stiff_ref, off_ref, attach_ref, plat_ref, pick_ref, dest_ref),
        (stiffb, offb, attachb, platb, pickb, destb),
        sem.at[0],
    )
    large = fetch(
        (pos_ref, vel_ref) + tuple(contact_ref.at[s] for s in range(STEPS)),
        (posb, velb) + tuple(contactb.at[s] for s in range(STEPS)),
        sem.at[1],
    )
    for c in small:
        c.wait()
    k = stiffb[...]
    onehot = (attachb[...] == iota((LANES, LANES), 0)).astype(F32)
    off = offb[...]
    fair = jnp.dot(platb[...], onehot, precision=HIGH, preferred_element_type=F32) + off
    picks = pick_matrix(pickb)
    row = iota((NODES, LANES), 0)
    first, last, bulk = row == 0, row == NODES - 1, row < NODES - TAIL
    lin[...] = jnp.zeros_like(lin)
    lin[ONES_ROW : ONES_ROW + 1] = jnp.ones((1, LANES), F32)
    large[0].wait()
    large[1].wait()
    pos = [jnp.where(last, fair[c : c + 1], posb[c]) for c in range(3)]
    vel = [velb[c] for c in range(3)]
    for step in range(STEPS):
        large[2 + step].wait()
        touch = contactb[step].astype(F32)
        damp = 0.02 + 0.1 * touch
        for c in range(3):
            p = pos[c]
            stack[c * NODES : (c + 1) * NODES, step * LANES : (step + 1) * LANES] = jnp.where(bulk, p, 0.0).astype(BF16)
            bound_ref[step * 3 + c : step * 3 + c + 1] = p[NODES - TAIL - 1 : NODES - TAIL]
            lin[step * 3 + c : step * 3 + c + 1] = p[NODES - 2 : NODES - 1] - p[NODES - 1 : NODES]
            accel = k * (pltpu.roll(p, NODES - 1, 0) - 2.0 * p + pltpu.roll(p, 1, 0)) - damp * vel[c]
            if c == 2:
                accel = accel + (-0.05 - 0.3 * touch * (p + 2.0))
            vel[c] = vel[c] + accel
            pos[c] = jnp.where(first, p, jnp.where(last, off[c : c + 1], p + vel[c]))
    for c in range(3):
        stack[c * NODES : (c + 1) * NODES, STEPS * LANES :] = jnp.where(bulk, pos[c], 0.0).astype(BF16)
        fpos_ref[c] = pos[c]
    rows_ref[...] = nt(picks, stack[...]).astype(BF16)
    trow = iota((TAIL, LANES), 0)
    zero = jnp.zeros((TAIL, LANES), F32)
    for kind in range(2):
        rp, rv = [zero] * 6, [zero] * 6
        for step in range(1, STEPS):
            for t in range(1, step):
                at = ONES_ROW + 1 + 2 * PAIRS.index((step, t)) + kind
                lin[at : at + 1] = rp[t - 1][TAIL - 2 : TAIL - 1]
            if step == STEPS - 1:
                break
            touch = contactb[step, NODES - TAIL : NODES].astype(F32)
            damp = 0.02 + 0.1 * touch
            for t in range(1, step + 1):
                p = jnp.where(trow == TAIL - 1, 1.0 if t == step else 0.0, rp[t - 1])
                up = pltpu.roll(p, TAIL - 1, 0)
                down = jnp.where(trow == 0, 0.0, pltpu.roll(p, 1, 0))
                accel = k * (up - 2.0 * p + down) - damp * rv[t - 1]
                if kind == 1:
                    accel = accel - 0.3 * touch * p
                rv[t - 1] = rv[t - 1] + accel
                rp[t - 1] = p + rv[t - 1]
    sums = nt(lin[...] * k, onehot, HIGH)
    count = destb.shape[1]
    lane, sub = iota((count, count), 1), iota((count, count), 0)
    dest = destb[...].astype(F32)
    dest_col = jnp.sum(jnp.where(lane == sub, dest, 0.0), axis=1, keepdims=True)
    rank = jnp.sum(jnp.where((dest_col == dest) & (sub < lane), 1.0, 0.0), axis=0, keepdims=True)
    codes = jnp.concatenate([dest * CAP + rank, jnp.full((1, LANES - count), -1.0, F32)], axis=1)
    pay_ref[...] = jnp.where(iota((ROWS, LANES), 0) == CODE_ROW + lax.axis_index("core"), codes, sums)


def finish_kernel(
    recv_ref, bound_ref, rows_ref, plat_ref, plat_vel_ref, inv_ref, rest_ref, kern_ref, hist_ref, wave_ref,
    pos_ref, vel_ref, contact_ref, stiff_ref, off_ref, attach_ref, pick_ref, w_in_ref, fpos_in,
    x_ref, t_ref, h_ref, plat_out, fpos_ref,
    recvb, boundb, rowsb, platb, plat_velb, invb, restb, kernb, histb, waveb,
    posb, velb, contactb, stiffb, offb, attachb, pickb, w_inb, tails, final, sem, out_sem,
):
    at = pl.ds(NODES - TAIL, TAIL)
    copies = fetch(
        (
            recv_ref, plat_ref, plat_vel_ref, inv_ref, rest_ref, kern_ref, hist_ref, wave_ref,
            stiff_ref, off_ref, attach_ref, pick_ref, bound_ref, rows_ref,
            pos_ref.at[:, at, :], vel_ref.at[:, at, :], contact_ref.at[:, at, :], w_in_ref,
        ),
        (
            recvb, platb, plat_velb, invb, restb, kernb, histb, waveb,
            stiffb, offb, attachb, pickb, boundb, rowsb, posb, velb, contactb, w_inb,
        ),
        sem,
    )
    for c in copies[:-1]:
        c.wait()
    total = recvb[0]
    for d in range(1, recvb.shape[0]):
        total = total + recvb[d]
    q, u = platb[...], plat_velb[...]
    hist = [histb[:, m] for m in range(STEPS)]
    kern = [kernb[:, m] for m in range(STEPS)]
    ones = total[ONES_ROW : ONES_ROW + 1]
    qs = [q]
    for step in range(STEPS):
        force = total[3 * step : 3 * step + 3]
        if step > 0:
            force = force - ones * q
        for t in range(1, step):
            at = ONES_ROW + 1 + 2 * PAIRS.index((step, t))
            coef = jnp.concatenate([total[at : at + 1], total[at : at + 2]], axis=0)
            force = force + coef * qs[t]
        memory = kern[0] * hist[0]
        for m in range(1, STEPS):
            memory = memory + kern[m] * hist[m]
        u = u + invb[...] * (force - restb[...] * q - memory + waveb[:, step])
        q = q + u
        hist = [u] + hist[:-1]
        qs.append(q)
    plat_out[...] = q
    k = stiffb[...]
    onehot = (attachb[...] == iota((LANES, LANES), 0)).astype(F32)
    fair = jnp.dot(jnp.concatenate(qs, axis=0), onehot, precision=HIGH, preferred_element_type=F32)
    trow = iota((TAIL, LANES), 0)
    pos = [posb[c] for c in range(3)]
    vel = [velb[c] for c in range(3)]
    for step in range(STEPS + 1):
        for c in range(3):
            here = fair[step * 3 + c : step * 3 + c + 1] + offb[c : c + 1]
            p = jnp.where(trow == TAIL - 1, here, pos[c])
            tails[c * TAIL : (c + 1) * TAIL, step * LANES : (step + 1) * LANES] = p
            if step == STEPS:
                final[c] = p
                continue
            touch = contactb[step].astype(F32)
            up = pltpu.roll(p, TAIL - 1, 0)
            bound = boundb[step * 3 + c : step * 3 + c + 1]
            down = jnp.where(trow == 0, bound, pltpu.roll(p, 1, 0))
            accel = k * (up - 2.0 * p + down) - (0.02 + 0.1 * touch) * vel[c]
            if c == 2:
                accel = accel + (-0.05 - 0.3 * touch * (p + 2.0))
            vel[c] = vel[c] + accel
            pos[c] = p + vel[c]
    copy = pltpu.make_async_copy(final, fpos_ref.at[:, NODES - TAIL : NODES, :], out_sem)
    copy.start()
    picked = nt(pick_matrix(pickb), tails[...].astype(BF16)).astype(BF16)
    at = iota((3 * TAIL, FEATS), 0)
    where = (at // TAIL) * NODES + (NODES - TAIL) + at % TAIL
    place = (iota((3 * TAIL, FEATS), 1) == where).astype(F32).astype(BF16)
    rows = rowsb[...].astype(F32) + jnp.dot(picked, place, preferred_element_type=F32)
    count = t_ref.shape[0]
    t_ref[...] = rows[count:].astype(BF16)
    copies[-1].wait()
    hidden = jnp.dot(rows[:count].astype(BF16), w_inb[...], preferred_element_type=F32).astype(BF16)
    h_ref[...] = hidden
    wide = hidden.astype(F32)
    scale = lax.rsqrt(jnp.mean(wide * wide, axis=1, keepdims=True) + 1e-06)
    scaled = (rows[:count] * scale).astype(BF16)
    for d in range(x_ref.shape[0]):
        x_ref[d] = scaled
    copy.wait()


def forward_kernel(
    x_ref, g0_ref, u0_ref, d0_ref, g1_ref, u1_ref, d1_ref, part_ref, a_ref, b_ref,
    xb, g0b, u0b, d0b, g1b, u1b, d1b, sem,
):
    copies = fetch(
        (x_ref, g0_ref, u0_ref, d0_ref, g1_ref, u1_ref, d1_ref), (xb, g0b, u0b, d0b, g1b, u1b, d1b), sem
    )
    copies[0].wait()
    x = xb[...].reshape(-1, xb.shape[-1])
    part = None
    for side, (g, u, d) in enumerate(((g0b, u0b, d0b), (g1b, u1b, d1b))):
        copies[1 + 3 * side].wait()
        gate = dot(x, g[...])
        copies[2 + 3 * side].wait()
        upper = dot(x, u[...])
        sigma = jax.nn.sigmoid(gate)
        silu = gate * sigma
        a_ref[side] = (upper * sigma * (1.0 + gate * (1.0 - sigma))).astype(BF16)
        b_ref[side] = silu.astype(BF16)
        copies[3 + 3 * side].wait()
        term = dot((silu * upper).astype(BF16), d[...])
        part = term if part is None else part + term
    part_ref[...] = part.astype(BF16).reshape(part_ref.shape)


def error_kernel(parts_ref, base_ref, err_ref):
    total = base_ref[...]
    for d in range(parts_ref.shape[0]):
        total = total + parts_ref[d].astype(F32)
    total = total.astype(BF16)
    for d in range(err_ref.shape[0]):
        err_ref[d] = total


def backward_kernel(side, err_ref, d_ref, a_ref, b_ref, xt_ref, y_ref, errb, db, ab, bb, xtb, sem):
    copies = fetch((err_ref, d_ref, a_ref.at[side], b_ref.at[side], xt_ref), (errb, db, ab, bb, xtb), sem)
    copies[0].wait()
    dpred = (errb[...].astype(F32) / 64.0).astype(BF16).reshape(-1, errb.shape[-1])
    copies[1].wait()
    dact = nt(dpred, db[...])
    copies[2].wait()
    dgate = (dact * ab[...].astype(F32)).astype(BF16)
    copies[3].wait()
    dup = (dact * bb[...].astype(F32)).astype(BF16)
    copies[4].wait()
    width = dgate.shape[1]
    y_ref[:, :width] = dot(xtb[...], dgate).astype(y_ref.dtype)
    y_ref[:, width:] = dot(xtb[...], dup).astype(y_ref.dtype)


def sum_kernel(parts_ref, out_ref):
    total = parts_ref[0].astype(F32)
    for d in range(1, parts_ref.shape[0]):
        total = total + parts_ref[d].astype(F32)
    total = total.astype(BF16)
    for d in range(out_ref.shape[0]):
        out_ref[d] = total


def last_kernel(y_ref, w_ref, gate_ref, up_ref):
    width = gate_ref.shape[1]
    y = y_ref[...].reshape(w_ref.shape[1], 2 * width)
    gate_ref[...] = dot(w_ref[...], y[:, :width])
    up_ref[...] = dot(w_ref[...], y[:, width:])


VM = pl.BlockSpec(memory_space=pltpu.VMEM)
HB = pl.BlockSpec(memory_space=pltpu.HBM)


def vmem_like(a, tail=False):
    shape = (a.shape[0], TAIL, LANES) if tail else a.shape
    return pltpu.VMEM(shape, a.dtype)


def evolve(line_pos, line_vel, stiff, contact, offset, attach, plat_pos, pick, dest):
    sds = jax.ShapeDtypeStruct
    large = (line_pos, line_vel, contact)
    small = (stiff, offset, attach, plat_pos, pick, dest)
    return pl.pallas_call(
        evolve_kernel,
        out_shape=(
            sds((ROWS, LANES), F32),
            sds((2 * COUNT, FEATS), BF16),
            sds((3 * STEPS, LANES), F32),
            sds((3, NODES, LANES), F32),
        ),
        in_specs=[HB] * 9,
        out_specs=(VM,) * 4,
        scratch_shapes=[vmem_like(a) for a in large + small]
        + [
            pltpu.VMEM((3 * NODES, LANES * (STEPS + 1)), BF16),
            pltpu.VMEM((ROWS, LANES), F32),
            pltpu.SemaphoreType.DMA((2, 2 + STEPS)),
        ],
        compiler_params=pltpu.CompilerParams(vmem_limit_bytes=LIMIT),
        cost_estimate=pl.CostEstimate(flops=260000000, bytes_accessed=3000000, transcendentals=0),
        name="evolve",
    )(line_pos, line_vel, stiff, contact, offset, attach, plat_pos, pick, dest)


def finish(recv, bound, rows, plats, lines, w_in, fpos):
    sds = jax.ShapeDtypeStruct
    args = (recv, bound, rows, *plats, *lines, w_in)
    at = 3 + len(plats)
    bufs = [vmem_like(a, at <= i < at + 3) for i, a in enumerate(args)]
    out = (
        sds((recv.shape[0], COUNT, FEATS), BF16),
        sds((COUNT, FEATS), BF16),
        sds((COUNT, w_in.shape[1]), BF16),
        sds((3, LANES), F32),
    )
    return pl.pallas_call(
        finish_kernel,
        out_shape=out + (sds(fpos.shape, F32),),
        in_specs=[HB] * (len(args) + 1),
        out_specs=(VM,) * len(out) + (HB,),
        scratch_shapes=bufs
        + [
            pltpu.VMEM((3 * TAIL, LANES * (STEPS + 1)), F32),
            pltpu.VMEM((3, TAIL, LANES), F32),
            pltpu.SemaphoreType.DMA((len(args),)),
            pltpu.SemaphoreType.DMA,
        ],
        input_output_aliases={len(args): len(out)},
        compiler_params=pltpu.CompilerParams(vmem_limit_bytes=LIMIT),
        cost_estimate=pl.CostEstimate(flops=300000000, bytes_accessed=4000000, transcendentals=0),
        name="finish",
    )(*args, fpos)


def forward(x, weights):
    sds = jax.ShapeDtypeStruct
    args = (x, *weights)
    rows, width = x.shape[0] * x.shape[1], weights[0].shape[1]
    return pl.pallas_call(
        forward_kernel,
        out_shape=(sds(x.shape, BF16), sds((2, rows, width), BF16), sds((2, rows, width), BF16)),
        in_specs=[HB] * len(args),
        out_specs=(VM,) * 3,
        scratch_shapes=[vmem_like(a) for a in args] + [pltpu.SemaphoreType.DMA((len(args),))],
        compiler_params=pltpu.CompilerParams(vmem_limit_bytes=LIMIT),
        cost_estimate=pl.CostEstimate(flops=2400000000, bytes_accessed=9000000, transcendentals=500000),
        name="forward",
    )(*args)


def backward(side, err, down, a, b, xt, kind):
    args = (err, down, a, b, xt)
    bufs = [vmem_like(v) for v in (err, down)] + [pltpu.VMEM(a.shape[1:], BF16)] * 2 + [vmem_like(xt)]
    return pl.pallas_call(
        functools.partial(backward_kernel, side),
        out_shape=jax.ShapeDtypeStruct((xt.shape[0], 2 * a.shape[2]), kind),
        in_specs=[HB] * len(args),
        out_specs=VM,
        scratch_shapes=bufs + [pltpu.SemaphoreType.DMA((len(args),))],
        compiler_params=pltpu.CompilerParams(vmem_limit_bytes=LIMIT),
        cost_estimate=pl.CostEstimate(flops=1200000000, bytes_accessed=6000000, transcendentals=0),
        name="backward",
    )(*args)


def simple(kernel, name, out_shape, *args):
    return pl.pallas_call(
        kernel,
        out_shape=out_shape,
        compiler_params=pltpu.CompilerParams(vmem_limit_bytes=LIMIT),
        name=name,
    )(*args)


def exchange(x, axes):
    return lax.all_to_all(x, axes, split_axis=0, concat_axis=0, tiled=True)


def dot(left, right):
    return jnp.dot(left, right, preferred_element_type=F32)


def swap(x):
    return lax.ppermute(x, "core", SWAP)


def after(x, *others):
    return lax.optimization_barrier((x,) + others)[0]


def body(
    line_pos, line_vel, stiffness, contact, offset, attach, plat_pos, plat_vel, inv_mass, restoring,
    kernel, vel_hist, wave, sample_pick, sample_dest, w_in, gain, w_gate, w_up, w_down, w_out,
):
    sds = jax.ShapeDtypeStruct
    chips = lax.axis_size(CHIP)
    groups = lax.axis_size(GRP)
    half = chips * COUNT
    width = w_gate.shape[1]
    stiff, att, pick, dest = stiffness[None], attach[None], sample_pick[None], sample_dest.reshape(1, -1)
    pay, rows, bound, fpos = evolve(
        line_pos, line_vel, stiff, contact, offset, att, plat_pos, pick, dest
    )
    pay = jnp.broadcast_to((pay + swap(pay))[None], (chips,) + pay.shape)
    pay, w_in_late, w_down_late = lax.optimization_barrier((pay, w_in, w_down))
    recv = exchange(pay, CHIP)
    scaled = lax.optimization_barrier((w_in_late.astype(F32) * gain).astype(BF16))
    gate_w = dot(scaled, w_gate).astype(BF16)
    gate_o = swap(gate_w)
    up_w = dot(scaled, w_up).astype(BF16)
    up_o = swap(up_w)
    turned = lambda a: a.transpose(1, 0, 2)
    x_own, target, hidden, final_plat, final_pos = finish(
        recv, bound, rows,
        (plat_pos, plat_vel, inv_mass, restoring, turned(kernel), turned(vel_hist), turned(wave)),
        (line_pos, line_vel, contact, stiff, offset, att, pick),
        w_in, fpos,
    )
    x_own, w_down_late = lax.optimization_barrier((x_own, w_down_late))
    x = exchange(x_own, CHIP)
    down_w = dot(w_down_late, w_out).astype(BF16)
    down_o = swap(down_w)
    part, slope_a, slope_b = forward(x, (gate_w, up_w, down_w, gate_o, up_o, down_o))
    part, hidden, x_late, scaled_late = lax.optimization_barrier((part, hidden, x, scaled))
    parts = exchange(part, CHIP)
    base = lax.optimization_barrier(dot(hidden, w_out) - target.astype(F32))
    xt = lax.optimization_barrier(x_late.reshape(half, FEATS).T)
    at = lax.axis_index(GRP)
    block = w_in.shape[1] // groups
    w_own = lax.optimization_barrier(lax.dynamic_slice_in_dim(scaled_late, at * block, block, 1).T)
    err_own = simple(error_kernel, "error", sds((chips, COUNT, FEATS), BF16), parts, base)
    err = exchange(err_own, CHIP)
    theirs = swap(backward(1, err, down_o, slope_a, slope_b, xt, BF16))
    mine = backward(0, err, down_w, slope_a, slope_b, xt, F32)
    feat_grads = (mine + theirs.astype(F32)).astype(BF16)
    feat_grads = exchange(feat_grads.reshape(groups, FEATS // groups, 2 * width), GRP)
    feat_grads = simple(sum_kernel, "total", sds(feat_grads.shape, BF16), feat_grads)
    feat_grads, err_late = lax.optimization_barrier((feat_grads, err))
    feat_grads = exchange(feat_grads, GRP)
    grad_gate, grad_up = simple(
        last_kernel, "last", (sds((block, width), F32), sds((block, width), F32)), feat_grads, w_own
    )
    err_late = err_late.reshape(half, FEATS)
    err_all = jnp.concatenate([err_late, swap(err_late)], axis=0)
    core = lax.axis_index("core")
    codes = recv[:, CODE_ROW : CODE_ROW + 2, :COUNT]
    codes = jnp.where(core == 0, codes, codes[:, ::-1]).transpose(1, 0, 2).reshape(1, 2 * half)
    me = lax.axis_index(CHIP) * 2 + core
    number = jnp.arange(2 * half, dtype=jnp.int32)
    source = ((number // COUNT) % chips) * 2 + (number // half + core) % 2
    slot = jnp.arange(2 * chips * CAP, dtype=jnp.int32)[:, None]
    match = (source[None] == slot // CAP) & (codes == (me * CAP + slot % CAP).astype(F32))
    slot_error = dot(match.astype(BF16), err_all).astype(BF16)
    return (final_pos, final_plat, slot_error, grad_gate, grad_up)


def solution(mesh):
    sizes = (4, 2, 2, 4, 2)
    if mesh.devices.shape[0] == 1:
        sizes = (1, 1, 2, 4, 2)
    fine = Mesh(mesh.devices.reshape(sizes), ALL)
    in_specs = (
        P(None, None, ALL),
        P(None, None, ALL),
        P(ALL),
        P(None, None, ALL),
        P(None, ALL),
        P(ALL),
        P(None, GRP),
        P(None, GRP),
        P(None, GRP),
        P(None, GRP),
        P(None, None, GRP),
        P(None, None, GRP),
        P(None, None, GRP),
        P(ALL),
        P(ALL, None),
        P(),
        P(),
        P(None, DEV),
        P(None, DEV),
        P(DEV, None),
        P(),
    )
    out_specs = (
        P(None, None, ALL),
        P(None, GRP),
        P(ALL, None),
        P(GRP, DEV),
        P(GRP, DEV),
    )
    return jax.shard_map(body, mesh=fine, in_specs=in_specs, out_specs=out_specs, check_vma=False)
```

```python
import functools
import jax
import jax.numpy as jnp
from jax import lax
from jax.experimental import pallas as pl
from jax.experimental.pallas import tpu as pltpu
from jax.sharding import Mesh, PartitionSpec as P

STEPS = 8
CAP = 8
NODES = 256
TAIL = 8
LANES = 128
COUNT = 64
FEATS = 768
ROWS = 72
ONES_ROW = 24
CODE_ROW = 67
LIMIT = 60 * 1024 * 1024
HIGH = lax.Precision.HIGHEST
F32 = jnp.float32
BF16 = jnp.bfloat16
DEV = ("zl", "x", "core")
CHIP = ("zl", "x")
GRP = ("y", "zh")
ALL = GRP + DEV
PAIRS = [(s, t) for s in range(2, STEPS) for t in range(1, s)]
SWAP = [(0, 1), (1, 0)]


def nt(left, right, precision=None):
    return lax.dot_general(
        left, right, (((1,), (1,)), ((), ())), precision=precision, preferred_element_type=F32
    )


def iota(shape, dim):
    return lax.broadcasted_iota(jnp.int32, shape, dim)


def pick_matrix(pick_ref):
    count = pick_ref.shape[1]
    eye = iota((count, count), 0) == iota((count, count), 1)
    pick = jnp.sum(jnp.where(eye, pick_ref[...].astype(F32), 0.0), axis=1, keepdims=True).astype(jnp.int32)
    at = (pick >> 3) + LANES * (pick & 7)
    at = jnp.concatenate([at, at + LANES], axis=0)
    return (iota((2 * count, LANES * (STEPS + 1)), 1) == at).astype(F32).astype(BF16)


def fetch(refs, bufs, sem):
    copies = [pltpu.make_async_copy(r, b, sem.at[i]) for i, (r, b) in enumerate(zip(refs, bufs))]
    for c in copies:
        c.start()
    return copies


def evolve_kernel(
    pos_ref, vel_ref, stiff_ref, contact_ref, off_ref, attach_ref, plat_ref, pick_ref, dest_ref,
    pay_ref, rows_ref, bound_ref, fpos_ref,
    posb, velb, contactb, stiffb, offb, attachb, platb, pickb, destb, stack, lin, sem,
):
    small = fetch(
        (stiff_ref, off_ref, attach_ref, plat_ref, pick_ref, dest_ref),
        (stiffb, offb, attachb, platb, pickb, destb),
        sem.at[0],
    )
    large = fetch(
        (pos_ref, vel_ref) + tuple(contact_ref.at[s] for s in range(STEPS)),
        (posb, velb) + tuple(contactb.at[s] for s in range(STEPS)),
        sem.at[1],
    )
    for c in small:
        c.wait()
    k = stiffb[...]
    onehot = (attachb[...] == iota((LANES, LANES), 0)).astype(F32)
    off = offb[...]
    fair = jnp.dot(platb[...], onehot, precision=HIGH, preferred_element_type=F32) + off
    picks = pick_matrix(pickb)
    row = iota((NODES, LANES), 0)
    first, last, bulk = row == 0, row == NODES - 1, row < NODES - TAIL
    lin[...] = jnp.zeros_like(lin)
    lin[ONES_ROW : ONES_ROW + 1] = jnp.ones((1, LANES), F32)
    large[0].wait()
    large[1].wait()
    pos = [jnp.where(last, fair[c : c + 1], posb[c]) for c in range(3)]
    vel = [velb[c] for c in range(3)]
    for step in range(STEPS):
        large[2 + step].wait()
        touch = contactb[step].astype(F32)
        damp = 0.02 + 0.1 * touch
        for c in range(3):
            p = pos[c]
            stack[c * NODES : (c + 1) * NODES, step * LANES : (step + 1) * LANES] = jnp.where(bulk, p, 0.0).astype(BF16)
            bound_ref[step * 3 + c : step * 3 + c + 1] = p[NODES - TAIL - 1 : NODES - TAIL]
            lin[step * 3 + c : step * 3 + c + 1] = p[NODES - 2 : NODES - 1] - p[NODES - 1 : NODES]
            accel = k * (pltpu.roll(p, NODES - 1, 0) - 2.0 * p + pltpu.roll(p, 1, 0)) - damp * vel[c]
            if c == 2:
                accel = accel + (-0.05 - 0.3 * touch * (p + 2.0))
            vel[c] = vel[c] + accel
            pos[c] = jnp.where(first, p, jnp.where(last, off[c : c + 1], p + vel[c]))
    for c in range(3):
        stack[c * NODES : (c + 1) * NODES, STEPS * LANES :] = jnp.where(bulk, pos[c], 0.0).astype(BF16)
        fpos_ref[c] = pos[c]
    rows_ref[...] = nt(picks, stack[...]).astype(BF16)
    trow = iota((TAIL, LANES), 0)
    zero = jnp.zeros((TAIL, LANES), F32)
    for kind in range(2):
        rp, rv = [zero] * 6, [zero] * 6
        for step in range(1, STEPS):
            for t in range(1, step):
                at = ONES_ROW + 1 + 2 * PAIRS.index((step, t)) + kind
                lin[at : at + 1] = rp[t - 1][TAIL - 2 : TAIL - 1]
            if step == STEPS - 1:
                break
            touch = contactb[step, NODES - TAIL : NODES].astype(F32)
            damp = 0.02 + 0.1 * touch
            for t in range(1, step + 1):
                p = jnp.where(trow == TAIL - 1, 1.0 if t == step else 0.0, rp[t - 1])
                up = pltpu.roll(p, TAIL - 1, 0)
                down = jnp.where(trow == 0, 0.0, pltpu.roll(p, 1, 0))
                accel = k * (up - 2.0 * p + down) - damp * rv[t - 1]
                if kind == 1:
                    accel = accel - 0.3 * touch * p
                rv[t - 1] = rv[t - 1] + accel
                rp[t - 1] = p + rv[t - 1]
    sums = nt(lin[...] * k, onehot, HIGH)
    count = destb.shape[1]
    lane, sub = iota((count, count), 1), iota((count, count), 0)
    dest = destb[...].astype(F32)
    dest_col = jnp.sum(jnp.where(lane == sub, dest, 0.0), axis=1, keepdims=True)
    rank = jnp.sum(jnp.where((dest_col == dest) & (sub < lane), 1.0, 0.0), axis=0, keepdims=True)
    codes = jnp.concatenate([dest * CAP + rank, jnp.full((1, LANES - count), -1.0, F32)], axis=1)
    pay_ref[...] = jnp.where(iota((ROWS, LANES), 0) == CODE_ROW + lax.axis_index("core"), codes, sums)


def finish_kernel(
    recv_ref, bound_ref, rows_ref, plat_ref, plat_vel_ref, inv_ref, rest_ref, kern_ref, hist_ref, wave_ref,
    pos_ref, vel_ref, contact_ref, stiff_ref, off_ref, attach_ref, pick_ref, w_in_ref, fpos_in,
    x_ref, t_ref, h_ref, plat_out, fpos_ref,
    recvb, boundb, rowsb, platb, plat_velb, invb, restb, kernb, histb, waveb,
    posb, velb, contactb, stiffb, offb, attachb, pickb, w_inb, tails, final, sem, out_sem,
):
    at = pl.ds(NODES - TAIL, TAIL)
    copies = fetch(
        (
            recv_ref, plat_ref, plat_vel_ref, inv_ref, rest_ref, kern_ref, hist_ref, wave_ref,
            stiff_ref, off_ref, attach_ref, pick_ref, bound_ref, rows_ref,
            pos_ref.at[:, at, :], vel_ref.at[:, at, :], contact_ref.at[:, at, :], w_in_ref,
        ),
        (
            recvb, platb, plat_velb, invb, restb, kernb, histb, waveb,
            stiffb, offb, attachb, pickb, boundb, rowsb, posb, velb, contactb, w_inb,
        ),
        sem,
    )
    for c in copies[:-1]:
        c.wait()
    total = recvb[0]
    for d in range(1, recvb.shape[0]):
        total = total + recvb[d]
    q, u = platb[...], plat_velb[...]
    hist = [histb[:, m] for m in range(STEPS)]
    kern = [kernb[:, m] for m in range(STEPS)]
    ones = total[ONES_ROW : ONES_ROW + 1]
    qs = [q]
    for step in range(STEPS):
        force = total[3 * step : 3 * step + 3]
        if step > 0:
            force = force - ones * q
        for t in range(1, step):
            at = ONES_ROW + 1 + 2 * PAIRS.index((step, t))
            coef = jnp.concatenate([total[at : at + 1], total[at : at + 2]], axis=0)
            force = force + coef * qs[t]
        memory = kern[0] * hist[0]
        for m in range(1, STEPS):
            memory = memory + kern[m] * hist[m]
        u = u + invb[...] * (force - restb[...] * q - memory + waveb[:, step])
        q = q + u
        hist = [u] + hist[:-1]
        qs.append(q)
    plat_out[...] = q
    k = stiffb[...]
    onehot = (attachb[...] == iota((LANES, LANES), 0)).astype(F32)
    fair = jnp.dot(jnp.concatenate(qs, axis=0), onehot, precision=HIGH, preferred_element_type=F32)
    trow = iota((TAIL, LANES), 0)
    pos = [posb[c] for c in range(3)]
    vel = [velb[c] for c in range(3)]
    for step in range(STEPS + 1):
        for c in range(3):
            here = fair[step * 3 + c : step * 3 + c + 1] + offb[c : c + 1]
            p = jnp.where(trow == TAIL - 1, here, pos[c])
            tails[c * TAIL : (c + 1) * TAIL, step * LANES : (step + 1) * LANES] = p
            if step == STEPS:
                final[c] = p
                continue
            touch = contactb[step].astype(F32)
            up = pltpu.roll(p, TAIL - 1, 0)
            bound = boundb[step * 3 + c : step * 3 + c + 1]
            down = jnp.where(trow == 0, bound, pltpu.roll(p, 1, 0))
            accel = k * (up - 2.0 * p + down) - (0.02 + 0.1 * touch) * vel[c]
            if c == 2:
                accel = accel + (-0.05 - 0.3 * touch * (p + 2.0))
            vel[c] = vel[c] + accel
            pos[c] = p + vel[c]
    copy = pltpu.make_async_copy(final, fpos_ref.at[:, NODES - TAIL : NODES, :], out_sem)
    copy.start()
    picked = nt(pick_matrix(pickb), tails[...].astype(BF16)).astype(BF16)
    at = iota((3 * TAIL, FEATS), 0)
    where = (at // TAIL) * NODES + (NODES - TAIL) + at % TAIL
    place = (iota((3 * TAIL, FEATS), 1) == where).astype(F32).astype(BF16)
    rows = rowsb[...].astype(F32) + jnp.dot(picked, place, preferred_element_type=F32)
    count = t_ref.shape[0]
    t_ref[...] = rows[count:].astype(BF16)
    copies[-1].wait()
    hidden = jnp.dot(rows[:count].astype(BF16), w_inb[...], preferred_element_type=F32).astype(BF16)
    h_ref[...] = hidden
    wide = hidden.astype(F32)
    scale = lax.rsqrt(jnp.mean(wide * wide, axis=1, keepdims=True) + 1e-06)
    scaled = (rows[:count] * scale).astype(BF16)
    for d in range(x_ref.shape[0]):
        x_ref[d] = scaled
    copy.wait()


def products_kernel(w_in_ref, gain_ref, gate_ref, up_ref, g_ref, u_ref, w_inb, gainb, gateb, upb, scaled, sem):
    copies = fetch((gain_ref, w_in_ref, gate_ref, up_ref), (gainb, w_inb, gateb, upb), sem)
    copies[0].wait()
    copies[1].wait()
    rows = 256
    for i in range(w_inb.shape[0] // rows):
        at = pl.ds(i * rows, rows)
        scaled[at] = (w_inb[at].astype(F32) * gainb[...]).astype(BF16)
        if i == 0:
            copies[2].wait()
        g_ref[at] = dot(scaled[at], gateb[...]).astype(BF16)
        if i == 0:
            copies[3].wait()
        u_ref[at] = dot(scaled[at], upb[...]).astype(BF16)


def down_kernel(w0_ref, w1_ref, out_ref, d0_ref, d1_ref, w0b, w1b, outb, sem):
    copies = fetch((w0_ref, out_ref, w1_ref), (w0b, outb, w1b), sem)
    copies[0].wait()
    copies[1].wait()
    d0_ref[...] = dot(w0b[...], outb[...]).astype(BF16)
    copies[2].wait()
    d1_ref[...] = dot(w1b[...], outb[...]).astype(BF16)


def forward_kernel(
    x_ref, g0_ref, u0_ref, d0_ref, g1_ref, u1_ref, d1_ref, part_ref, gate_ref, up_ref,
    xb, g0b, u0b, d0b, g1b, u1b, d1b, gateb, upb, sem, out_sem,
):
    copies = fetch(
        (x_ref, g0_ref, u0_ref, d0_ref, g1_ref, u1_ref, d1_ref), (xb, g0b, u0b, d0b, g1b, u1b, d1b), sem
    )
    copies[0].wait()
    x = xb[...].reshape(-1, xb.shape[-1])
    part, outs = None, []
    for side, (g, u, d) in enumerate(((g0b, u0b, d0b), (g1b, u1b, d1b))):
        copies[1 + 3 * side].wait()
        gate = dot(x, g[...])
        gateb[side] = gate
        copies[2 + 3 * side].wait()
        upper = dot(x, u[...])
        upb[side] = upper
        for i, (buf, ref) in enumerate(((gateb, gate_ref), (upb, up_ref))):
            out = pltpu.make_async_copy(buf.at[side], ref.at[side], out_sem.at[2 * side + i])
            out.start()
            outs.append(out)
        act = (gate * jax.nn.sigmoid(gate) * upper).astype(BF16)
        copies[3 + 3 * side].wait()
        term = dot(act, d[...])
        part = term if part is None else part + term
    part_ref[...] = part.astype(BF16).reshape(part_ref.shape)
    for out in outs:
        out.wait()


def slopes_kernel(gate_ref, up_ref, a_ref, b_ref):
    gate, upper = gate_ref[...], up_ref[...]
    sigma = jax.nn.sigmoid(gate)
    a_ref[...] = (upper * sigma * (1.0 + gate * (1.0 - sigma))).astype(BF16)
    b_ref[...] = (gate * sigma).astype(BF16)


def error_kernel(parts_ref, base_ref, err_ref):
    total = base_ref[...]
    for d in range(parts_ref.shape[0]):
        total = total + parts_ref[d].astype(F32)
    total = total.astype(BF16)
    for d in range(err_ref.shape[0]):
        err_ref[d] = total


def backward_kernel(
    e0_ref, e1_ref, d_ref, a0_ref, b0_ref, a1_ref, b1_ref, x0_ref, x1_ref, y_ref,
    e0b, e1b, db, a0b, b0b, a1b, b1b, x0b, x1b, grads, sem,
):
    copies = fetch(
        (e0_ref, d_ref, a0_ref.at[0], b0_ref.at[0], e1_ref, a1_ref, b1_ref, x0_ref, x1_ref),
        (e0b, db, a0b, b0b, e1b, a1b, b1b, x0b, x1b),
        sem,
    )
    width = a0b.shape[1]
    order = ((e0b, a0b, b0b, 0), (e1b, a1b, b1b, 4))
    for side, (eb, ab, bb, first) in enumerate(order):
        for i in range(3 if side else 4):
            copies[first + i].wait()
        dpred = (eb[...].astype(F32) / 64.0).astype(BF16).reshape(-1, eb.shape[-1])
        dact = nt(dpred, db[...])
        rows = pl.ds(side * dact.shape[0], dact.shape[0])
        grads[rows, :width] = (dact * ab[...].astype(F32)).astype(BF16)
        grads[rows, width:] = (dact * bb[...].astype(F32)).astype(BF16)
    copies[7].wait()
    copies[8].wait()
    half = x0b.shape[1]
    tall = 256
    for i in range(y_ref.shape[0] // tall):
        at = pl.ds(i * tall, tall)
        y = dot(x0b[at], grads[:half]) + dot(x1b[at], grads[half:])
        y_ref[at] = y.astype(BF16)


def sum_kernel(parts_ref, out_ref):
    total = parts_ref[0].astype(F32)
    for d in range(1, parts_ref.shape[0]):
        total = total + parts_ref[d].astype(F32)
    total = total.astype(BF16)
    for d in range(out_ref.shape[0]):
        out_ref[d] = total


def last_kernel(yg_ref, yu_ref, w_ref, gate_ref, up_ref):
    for y_ref, out_ref in ((yg_ref, gate_ref), (yu_ref, up_ref)):
        y = y_ref[...].reshape(w_ref.shape[0], out_ref.shape[1])
        out_ref[...] = lax.dot_general(
            w_ref[...], y, (((0,), (0,)), ((), ())), preferred_element_type=F32
        )


VM = pl.BlockSpec(memory_space=pltpu.VMEM)
HB = pl.BlockSpec(memory_space=pl.ANY)


def vmem_like(a, tail=False):
    shape = (a.shape[0], TAIL, LANES) if tail else a.shape
    return pltpu.VMEM(shape, a.dtype)


def evolve(line_pos, line_vel, stiff, contact, offset, attach, plat_pos, pick, dest):
    sds = jax.ShapeDtypeStruct
    large = (line_pos, line_vel, contact)
    small = (stiff, offset, attach, plat_pos, pick, dest)
    return pl.pallas_call(
        evolve_kernel,
        out_shape=(
            sds((ROWS, LANES), F32),
            sds((2 * COUNT, FEATS), BF16),
            sds((3 * STEPS, LANES), F32),
            sds((3, NODES, LANES), F32),
        ),
        in_specs=[HB] * 9,
        out_specs=(VM,) * 4,
        scratch_shapes=[vmem_like(a) for a in large + small]
        + [
            pltpu.VMEM((3 * NODES, LANES * (STEPS + 1)), BF16),
            pltpu.VMEM((ROWS, LANES), F32),
            pltpu.SemaphoreType.DMA((2, 2 + STEPS)),
        ],
        compiler_params=pltpu.CompilerParams(vmem_limit_bytes=LIMIT),
        cost_estimate=pl.CostEstimate(flops=260000000, bytes_accessed=3000000, transcendentals=0),
        name="evolve",
    )(line_pos, line_vel, stiff, contact, offset, attach, plat_pos, pick, dest)


def finish(recv, bound, rows, plats, lines, w_in, fpos):
    sds = jax.ShapeDtypeStruct
    args = (recv, bound, rows, *plats, *lines, w_in)
    at = 3 + len(plats)
    bufs = [vmem_like(a, at <= i < at + 3) for i, a in enumerate(args)]
    out = (
        sds((recv.shape[0], COUNT, FEATS), BF16),
        sds((COUNT, FEATS), BF16),
        sds((COUNT, w_in.shape[1]), BF16),
        sds((3, LANES), F32),
    )
    return pl.pallas_call(
        finish_kernel,
        out_shape=out + (sds(fpos.shape, F32),),
        in_specs=[HB] * (len(args) + 1),
        out_specs=(VM,) * len(out) + (HB,),
        scratch_shapes=bufs
        + [
            pltpu.VMEM((3 * TAIL, LANES * (STEPS + 1)), F32),
            pltpu.VMEM((3, TAIL, LANES), F32),
            pltpu.SemaphoreType.DMA((len(args),)),
            pltpu.SemaphoreType.DMA,
        ],
        input_output_aliases={len(args): len(out)},
        compiler_params=pltpu.CompilerParams(vmem_limit_bytes=LIMIT),
        cost_estimate=pl.CostEstimate(flops=300000000, bytes_accessed=4000000, transcendentals=0),
        name="finish",
    )(*args, fpos)


PARAMS = pltpu.CompilerParams(vmem_limit_bytes=LIMIT)
SMALL = pltpu.CompilerParams(vmem_limit_bytes=16 * 1024 * 1024)


def staged(kernel, name, args, out_shape, scratch, flops, sems, out_specs=VM, bufs=None):
    bufs = [vmem_like(a) for a in args] if bufs is None else bufs
    return pl.pallas_call(
        kernel,
        out_shape=out_shape,
        in_specs=[HB] * len(args),
        out_specs=out_specs,
        scratch_shapes=bufs + scratch + [pltpu.SemaphoreType.DMA((n,)) for n in sems],
        compiler_params=PARAMS,
        cost_estimate=pl.CostEstimate(flops=flops, bytes_accessed=8000000, transcendentals=0),
        name=name,
    )(*args)


def cut(shape, parts, offset=0):
    block = shape[:-1] + (shape[-1] // parts,)
    return pl.BlockSpec(block, lambda i: (0,) * (len(shape) - 1) + (i + offset,))


def exchange(x, axes):
    return lax.all_to_all(x, axes, split_axis=0, concat_axis=0, tiled=True)


def dot(left, right):
    return jnp.dot(left, right, preferred_element_type=F32)


def swap(x):
    return lax.ppermute(x, "core", SWAP)


def after(x, *others):
    return lax.optimization_barrier((x,) + others)[0]


def body(
    line_pos, line_vel, stiffness, contact, offset, attach, plat_pos, plat_vel, inv_mass, restoring,
    kernel, vel_hist, wave, sample_pick, sample_dest, w_in, gain, w_gate, w_up, w_down, w_out,
):
    sds = jax.ShapeDtypeStruct
    chips = lax.axis_size(CHIP)
    groups = lax.axis_size(GRP)
    half = chips * COUNT
    width = w_gate.shape[1]
    stiff, att, pick, dest = stiffness[None], attach[None], sample_pick[None], sample_dest.reshape(1, -1)
    pay, rows, bound, fpos = evolve(
        line_pos, line_vel, stiff, contact, offset, att, plat_pos, pick, dest
    )
    pay = jnp.broadcast_to((pay + swap(pay))[None], (chips,) + pay.shape)
    pay, w_in_late, w_down_late = lax.optimization_barrier((pay, w_in, w_down))
    recv = exchange(pay, CHIP)
    product = sds((FEATS, width), BF16)
    gate_w, up_w = staged(
        products_kernel, "products", (w_in_late, gain[None], w_gate, w_up), (product, product),
        [pltpu.VMEM(w_in.shape, BF16)], 3300000000, (4,), (VM,) * 2,
    )
    gate_o, up_o = swap(gate_w), swap(up_w)
    w_down_o = swap(w_down)
    turned = lambda a: a.transpose(1, 0, 2)
    x_own, target, hidden, final_plat, final_pos = finish(
        recv, bound, rows,
        (plat_pos, plat_vel, inv_mass, restoring, turned(kernel), turned(vel_hist), turned(wave)),
        (line_pos, line_vel, contact, stiff, offset, att, pick),
        w_in, fpos,
    )
    x_own, w_down_late, w_down_o, hidden = lax.optimization_barrier((x_own, w_down_late, w_down_o, hidden))
    x = exchange(x_own, CHIP)
    product = sds((width, FEATS), BF16)
    down_w, down_o = staged(
        down_kernel, "down", (w_down_late, w_down_o, w_out), (product, product), [], 3300000000, (3,), (VM,) * 2
    )
    base = lax.optimization_barrier(dot(hidden, w_out) - target.astype(F32))
    args = (x, gate_w, up_w, down_w, gate_o, up_o, down_o)
    wide = sds((2, half, width), F32)
    part, gate, upper = staged(
        forward_kernel, "forward", args, (sds(x.shape, BF16), wide, wide),
        [pltpu.VMEM(wide.shape, F32)] * 2, 2500000000, (7, 4), (VM, HB, HB),
    )
    part, gate, upper, x_late, w_in_late = lax.optimization_barrier((part, gate, upper, x, w_in_late))
    parts = exchange(part, CHIP)
    slope = sds(wide.shape, BF16)
    rows_of = lambda: pl.BlockSpec((2, half // 4, width), lambda i: (0, i, 0))
    slope_a, slope_b = pl.pallas_call(
        slopes_kernel, grid=(4,), out_shape=(slope, slope), in_specs=[rows_of(), rows_of()],
        out_specs=(rows_of(), rows_of()), compiler_params=PARAMS, name="slopes",
        cost_estimate=pl.CostEstimate(flops=8000000, bytes_accessed=6000000, transcendentals=1000000),
    )(gate, upper)
    slope_ao, slope_bo = swap(slope_a[1]), swap(slope_b[1])
    x_late = lax.optimization_barrier(x_late.reshape(half, FEATS).T)
    x_other = swap(x_late)
    at = lax.axis_index(GRP)
    block = w_in.shape[1] // groups
    w_own = lax.optimization_barrier(lax.dynamic_slice_in_dim(w_in_late, at * block, block, 1))
    gain_own = lax.dynamic_slice_in_dim(gain, at * block, block, 0)
    w_own = lax.optimization_barrier((w_own.astype(F32) * gain_own).astype(BF16))
    err_own = pl.pallas_call(
        error_kernel, grid=(3,), out_shape=sds((chips, COUNT, FEATS), BF16),
        in_specs=[cut(parts.shape, 3), cut(base.shape, 3)], out_specs=cut(parts.shape, 3),
        compiler_params=SMALL, name="error",
    )(parts, base)
    err_own, slope_ao, slope_bo, x_other = lax.optimization_barrier((err_own, slope_ao, slope_bo, x_other))
    err = exchange(err_own, CHIP)
    err_other = swap(err)
    args = (err, err_other, down_w, slope_a, slope_b, slope_ao, slope_bo, x_late, x_other)
    part_like = pltpu.VMEM((half, width), BF16)
    bufs = [vmem_like(err)] * 2 + [vmem_like(down_w)] + [part_like] * 4 + [vmem_like(x_late)] * 2
    feat_grads = staged(
        backward_kernel, "backward", args, sds((FEATS, 2 * width), BF16),
        [pltpu.VMEM((2 * half, 2 * width), BF16)], 2500000000, (9,), bufs=bufs,
    )
    feat_grads = exchange(feat_grads.reshape(groups, FEATS // groups, 2 * width), GRP)
    feat_grads = pl.pallas_call(
        sum_kernel, grid=(4,), out_shape=sds(feat_grads.shape, BF16), in_specs=[cut(feat_grads.shape, 4)],
        out_specs=cut(feat_grads.shape, 4), compiler_params=SMALL, name="total",
    )(feat_grads)
    feat_grads, err_late, err_other = lax.optimization_barrier((feat_grads, err, err_other))
    feat_grads = exchange(feat_grads, GRP)
    grad = sds((block, width), F32)
    grad_gate, grad_up = pl.pallas_call(
        last_kernel, grid=(2,), out_shape=(grad, grad),
        in_specs=[
            cut(feat_grads.shape, 4), cut(feat_grads.shape, 4, 2), pl.BlockSpec(w_own.shape, lambda i: (0, 0))
        ],
        out_specs=(cut(grad.shape, 2),) * 2, compiler_params=SMALL, name="last",
    )(feat_grads, feat_grads, w_own)
    err_all = jnp.concatenate([err_late, err_other], axis=0).reshape(2 * half, FEATS)
    core = lax.axis_index("core")
    codes = recv[:, CODE_ROW : CODE_ROW + 2, :COUNT]
    codes = jnp.where(core == 0, codes, codes[:, ::-1]).transpose(1, 0, 2).reshape(1, 2 * half)
    me = lax.axis_index(CHIP) * 2 + core
    number = jnp.arange(2 * half, dtype=jnp.int32)
    source = ((number // COUNT) % chips) * 2 + (number // half + core) % 2
    slot = jnp.arange(2 * chips * CAP, dtype=jnp.int32)[:, None]
    match = (source[None] == slot // CAP) & (codes == (me * CAP + slot % CAP).astype(F32))
    slot_error = dot(match.astype(BF16), err_all).astype(BF16)
    return (final_pos, final_plat, slot_error, grad_gate, grad_up)


def solution(mesh):
    sizes = (4, 2, 2, 4, 2)
    if mesh.devices.shape[0] == 1:
        sizes = (1, 1, 2, 4, 2)
    fine = Mesh(mesh.devices.reshape(sizes), ALL)
    in_specs = (
        P(None, None, ALL),
        P(None, None, ALL),
        P(ALL),
        P(None, None, ALL),
        P(None, ALL),
        P(ALL),
        P(None, GRP),
        P(None, GRP),
        P(None, GRP),
        P(None, GRP),
        P(None, None, GRP),
        P(None, None, GRP),
        P(None, None, GRP),
        P(ALL),
        P(ALL, None),
        P(),
        P(),
        P(None, DEV),
        P(None, DEV),
        P(DEV, None),
        P(),
    )
    out_specs = (
        P(None, None, ALL),
        P(None, GRP),
        P(ALL, None),
        P(GRP, DEV),
        P(GRP, DEV),
    )
    return jax.shard_map(body, mesh=fine, in_specs=in_specs, out_specs=out_specs, check_vma=False)
```

```python
import functools
import jax
import jax.numpy as jnp
from jax import lax
from jax.experimental import pallas as pl
from jax.experimental.pallas import tpu as pltpu
from jax.sharding import Mesh, PartitionSpec as P

STEPS = 8
CAP = 8
NODES = 256
TAIL = 8
LANES = 128
COUNT = 64
FEATS = 768
ROWS = 72
ONES_ROW = 24
CODE_ROW = 67
LIMIT = 60 * 1024 * 1024
HIGH = lax.Precision.HIGHEST
F32 = jnp.float32
BF16 = jnp.bfloat16
DEV = ("zl", "x", "core")
CHIP = ("zl", "x")
GRP = ("y", "zh")
ALL = GRP + DEV
PAIRS = [(s, t) for s in range(2, STEPS) for t in range(1, s)]
SWAP = [(0, 1), (1, 0)]


def nt(left, right, precision=None):
    return lax.dot_general(
        left, right, (((1,), (1,)), ((), ())), precision=precision, preferred_element_type=F32
    )


def iota(shape, dim):
    return lax.broadcasted_iota(jnp.int32, shape, dim)


def pick_matrix(pick_ref):
    count = pick_ref.shape[1]
    eye = iota((count, count), 0) == iota((count, count), 1)
    pick = jnp.sum(jnp.where(eye, pick_ref[...].astype(F32), 0.0), axis=1, keepdims=True).astype(jnp.int32)
    at = (pick >> 3) + LANES * (pick & 7)
    at = jnp.concatenate([at, at + LANES], axis=0)
    return (iota((2 * count, LANES * (STEPS + 1)), 1) == at).astype(F32).astype(BF16)


def fetch(refs, bufs, sem):
    copies = [pltpu.make_async_copy(r, b, sem.at[i]) for i, (r, b) in enumerate(zip(refs, bufs))]
    for c in copies:
        c.start()
    return copies


def evolve_kernel(
    pos_ref, vel_ref, stiff_ref, contact_ref, off_ref, attach_ref, plat_ref, pick_ref, dest_ref,
    pay_ref, rows_ref, bound_ref, fpos_ref,
    posb, velb, contactb, stiffb, offb, attachb, platb, pickb, destb, stack, lin, sem,
):
    small = fetch(
        (stiff_ref, off_ref, attach_ref, plat_ref, pick_ref, dest_ref),
        (stiffb, offb, attachb, platb, pickb, destb),
        sem.at[0],
    )
    large = fetch(
        (pos_ref, vel_ref) + tuple(contact_ref.at[s] for s in range(STEPS)),
        (posb, velb) + tuple(contactb.at[s] for s in range(STEPS)),
        sem.at[1],
    )
    for c in small:
        c.wait()
    k = stiffb[...]
    onehot = (attachb[...] == iota((LANES, LANES), 0)).astype(F32)
    off = offb[...]
    fair = jnp.dot(platb[...], onehot, precision=HIGH, preferred_element_type=F32) + off
    picks = pick_matrix(pickb)
    row = iota((NODES, LANES), 0)
    first, last, bulk = row == 0, row == NODES - 1, row < NODES - TAIL
    lin[...] = jnp.zeros_like(lin)
    lin[ONES_ROW : ONES_ROW + 1] = jnp.ones((1, LANES), F32)
    large[0].wait()
    large[1].wait()
    pos = [jnp.where(last, fair[c : c + 1], posb[c]) for c in range(3)]
    vel = [velb[c] for c in range(3)]
    for step in range(STEPS):
        large[2 + step].wait()
        touch = contactb[step].astype(F32)
        damp = 0.02 + 0.1 * touch
        for c in range(3):
            p = pos[c]
            stack[c * NODES : (c + 1) * NODES, step * LANES : (step + 1) * LANES] = jnp.where(bulk, p, 0.0).astype(BF16)
            bound_ref[step * 3 + c : step * 3 + c + 1] = p[NODES - TAIL - 1 : NODES - TAIL]
            lin[step * 3 + c : step * 3 + c + 1] = p[NODES - 2 : NODES - 1] - p[NODES - 1 : NODES]
            accel = k * (pltpu.roll(p, NODES - 1, 0) - 2.0 * p + pltpu.roll(p, 1, 0)) - damp * vel[c]
            if c == 2:
                accel = accel + (-0.05 - 0.3 * touch * (p + 2.0))
            vel[c] = vel[c] + accel
            pos[c] = jnp.where(first, p, jnp.where(last, off[c : c + 1], p + vel[c]))
    for c in range(3):
        stack[c * NODES : (c + 1) * NODES, STEPS * LANES :] = jnp.where(bulk, pos[c], 0.0).astype(BF16)
        fpos_ref[c] = pos[c]
    rows_ref[...] = nt(picks, stack[...]).astype(BF16)
    trow = iota((TAIL, LANES), 0)
    zero = jnp.zeros((TAIL, LANES), F32)
    for kind in range(2):
        rp, rv = [zero] * 6, [zero] * 6
        for step in range(1, STEPS):
            for t in range(1, step):
                at = ONES_ROW + 1 + 2 * PAIRS.index((step, t)) + kind
                lin[at : at + 1] = rp[t - 1][TAIL - 2 : TAIL - 1]
            if step == STEPS - 1:
                break
            touch = contactb[step, NODES - TAIL : NODES].astype(F32)
            damp = 0.02 + 0.1 * touch
            for t in range(1, step + 1):
                p = jnp.where(trow == TAIL - 1, 1.0 if t == step else 0.0, rp[t - 1])
                up = pltpu.roll(p, TAIL - 1, 0)
                down = jnp.where(trow == 0, 0.0, pltpu.roll(p, 1, 0))
                accel = k * (up - 2.0 * p + down) - damp * rv[t - 1]
                if kind == 1:
                    accel = accel - 0.3 * touch * p
                rv[t - 1] = rv[t - 1] + accel
                rp[t - 1] = p + rv[t - 1]
    sums = nt(lin[...] * k, onehot, HIGH)
    count = destb.shape[1]
    lane, sub = iota((count, count), 1), iota((count, count), 0)
    dest = destb[...].astype(F32)
    dest_col = jnp.sum(jnp.where(lane == sub, dest, 0.0), axis=1, keepdims=True)
    rank = jnp.sum(jnp.where((dest_col == dest) & (sub < lane), 1.0, 0.0), axis=0, keepdims=True)
    codes = jnp.concatenate([dest * CAP + rank, jnp.full((1, LANES - count), -1.0, F32)], axis=1)
    pay_ref[...] = jnp.where(iota((ROWS, LANES), 0) == CODE_ROW + lax.axis_index("core"), codes, sums)


def finish_kernel(
    recv_ref, bound_ref, rows_ref, plat_ref, plat_vel_ref, inv_ref, rest_ref, kern_ref, hist_ref, wave_ref,
    pos_ref, vel_ref, contact_ref, stiff_ref, off_ref, attach_ref, pick_ref, w_in_ref, fpos_in,
    x_ref, t_ref, h_ref, plat_out, fpos_ref,
    recvb, boundb, rowsb, platb, plat_velb, invb, restb, kernb, histb, waveb,
    posb, velb, contactb, stiffb, offb, attachb, pickb, w_inb, tails, final, sem, out_sem,
):
    at = pl.ds(NODES - TAIL, TAIL)
    copies = fetch(
        (
            recv_ref, plat_ref, plat_vel_ref, inv_ref, rest_ref, kern_ref, hist_ref, wave_ref,
            stiff_ref, off_ref, attach_ref, pick_ref, bound_ref, rows_ref,
            pos_ref.at[:, at, :], vel_ref.at[:, at, :], contact_ref.at[:, at, :], w_in_ref,
        ),
        (
            recvb, platb, plat_velb, invb, restb, kernb, histb, waveb,
            stiffb, offb, attachb, pickb, boundb, rowsb, posb, velb, contactb, w_inb,
        ),
        sem,
    )
    for c in copies[:-1]:
        c.wait()
    total = recvb[0]
    for d in range(1, recvb.shape[0]):
        total = total + recvb[d]
    q, u = platb[...], plat_velb[...]
    hist = [histb[:, m] for m in range(STEPS)]
    kern = [kernb[:, m] for m in range(STEPS)]
    ones = total[ONES_ROW : ONES_ROW + 1]
    qs = [q]
    for step in range(STEPS):
        force = total[3 * step : 3 * step + 3]
        if step > 0:
            force = force - ones * q
        for t in range(1, step):
            at = ONES_ROW + 1 + 2 * PAIRS.index((step, t))
            coef = jnp.concatenate([total[at : at + 1], total[at : at + 2]], axis=0)
            force = force + coef * qs[t]
        memory = kern[0] * hist[0]
        for m in range(1, STEPS):
            memory = memory + kern[m] * hist[m]
        u = u + invb[...] * (force - restb[...] * q - memory + waveb[:, step])
        q = q + u
        hist = [u] + hist[:-1]
        qs.append(q)
    plat_out[...] = q
    k = stiffb[...]
    onehot = (attachb[...] == iota((LANES, LANES), 0)).astype(F32)
    fair = jnp.dot(jnp.concatenate(qs, axis=0), onehot, precision=HIGH, preferred_element_type=F32)
    trow = iota((TAIL, LANES), 0)
    pos = [posb[c] for c in range(3)]
    vel = [velb[c] for c in range(3)]
    for step in range(STEPS + 1):
        for c in range(3):
            here = fair[step * 3 + c : step * 3 + c + 1] + offb[c : c + 1]
            p = jnp.where(trow == TAIL - 1, here, pos[c])
            tails[c * TAIL : (c + 1) * TAIL, step * LANES : (step + 1) * LANES] = p
            if step == STEPS:
                final[c] = p
                continue
            touch = contactb[step].astype(F32)
            up = pltpu.roll(p, TAIL - 1, 0)
            bound = boundb[step * 3 + c : step * 3 + c + 1]
            down = jnp.where(trow == 0, bound, pltpu.roll(p, 1, 0))
            accel = k * (up - 2.0 * p + down) - (0.02 + 0.1 * touch) * vel[c]
            if c == 2:
                accel = accel + (-0.05 - 0.3 * touch * (p + 2.0))
            vel[c] = vel[c] + accel
            pos[c] = p + vel[c]
    copy = pltpu.make_async_copy(final, fpos_ref.at[:, NODES - TAIL : NODES, :], out_sem)
    copy.start()
    picked = nt(pick_matrix(pickb), tails[...].astype(BF16)).astype(BF16)
    at = iota((3 * TAIL, FEATS), 0)
    where = (at // TAIL) * NODES + (NODES - TAIL) + at % TAIL
    place = (iota((3 * TAIL, FEATS), 1) == where).astype(F32).astype(BF16)
    rows = rowsb[...].astype(F32) + jnp.dot(picked, place, preferred_element_type=F32)
    count = t_ref.shape[0]
    t_ref[...] = rows[count:].astype(BF16)
    copies[-1].wait()
    hidden = jnp.dot(rows[:count].astype(BF16), w_inb[...], preferred_element_type=F32).astype(BF16)
    h_ref[...] = hidden
    wide = hidden.astype(F32)
    scale = lax.rsqrt(jnp.mean(wide * wide, axis=1, keepdims=True) + 1e-06)
    scaled = (rows[:count] * scale).astype(BF16)
    for d in range(x_ref.shape[0]):
        x_ref[d] = scaled
    copy.wait()


def products_kernel(w_in_ref, gain_ref, gate_ref, up_ref, g_ref, u_ref, w_inb, gainb, gateb, upb, scaled, sem):
    copies = fetch((gain_ref, w_in_ref, gate_ref, up_ref), (gainb, w_inb, gateb, upb), sem)
    copies[0].wait()
    copies[1].wait()
    rows = 256
    for i in range(w_inb.shape[0] // rows):
        at = pl.ds(i * rows, rows)
        scaled[at] = (w_inb[at].astype(F32) * gainb[...]).astype(BF16)
        if i == 0:
            copies[2].wait()
        g_ref[at] = dot(scaled[at], gateb[...]).astype(BF16)
        if i == 0:
            copies[3].wait()
        u_ref[at] = dot(scaled[at], upb[...]).astype(BF16)


def down_kernel(w0_ref, w1_ref, out_ref, d0_ref, d1_ref, w0b, w1b, outb, sem):
    copies = fetch((out_ref, w0_ref, w1_ref), (outb, w0b, w1b), sem)
    copies[0].wait()
    tall = 256
    for copy, w, d_ref in ((copies[1], w0b, d0_ref), (copies[2], w1b, d1_ref)):
        copy.wait()
        for i in range(w.shape[0] // tall):
            at = pl.ds(i * tall, tall)
            d_ref[at] = dot(w[at], outb[...]).astype(BF16)


def forward_kernel(
    x_ref, g0_ref, u0_ref, d0_ref, g1_ref, u1_ref, d1_ref, part_ref, gate_ref, up_ref,
    xb, g0b, u0b, d0b, g1b, u1b, d1b, gateb, upb, sem, out_sem,
):
    copies = fetch(
        (x_ref, g0_ref, u0_ref, d0_ref, g1_ref, u1_ref, d1_ref), (xb, g0b, u0b, d0b, g1b, u1b, d1b), sem
    )
    copies[0].wait()
    x = xb[...].reshape(-1, xb.shape[-1])
    part, outs = None, []
    for side, (g, u, d) in enumerate(((g0b, u0b, d0b), (g1b, u1b, d1b))):
        copies[1 + 3 * side].wait()
        gate = dot(x, g[...])
        gateb[side] = gate
        copies[2 + 3 * side].wait()
        upper = dot(x, u[...])
        upb[side] = upper
        for i, (buf, ref) in enumerate(((gateb, gate_ref), (upb, up_ref))):
            out = pltpu.make_async_copy(buf.at[side], ref.at[side], out_sem.at[2 * side + i])
            out.start()
            outs.append(out)
        act = (gate * jax.nn.sigmoid(gate) * upper).astype(BF16)
        copies[3 + 3 * side].wait()
        term = dot(act, d[...])
        part = term if part is None else part + term
    part_ref[...] = part.astype(BF16).reshape(part_ref.shape)
    for out in outs:
        out.wait()


def slopes_kernel(gate_ref, up_ref, a0_ref, b0_ref, a1_ref, b1_ref):
    for side, (a_ref, b_ref) in enumerate(((a0_ref, b0_ref), (a1_ref, b1_ref))):
        gate, upper = gate_ref[side], up_ref[side]
        sigma = jax.nn.sigmoid(gate)
        a_ref[...] = (upper * sigma * (1.0 + gate * (1.0 - sigma))).astype(BF16)
        b_ref[...] = (gate * sigma).astype(BF16)


def error_kernel(parts_ref, base_ref, err_ref):
    total = base_ref[...]
    for d in range(parts_ref.shape[0]):
        total = total + parts_ref[d].astype(F32)
    total = total.astype(BF16)
    for d in range(err_ref.shape[0]):
        err_ref[d] = total


def hidden_grads(err_buf, down_buf, a_buf, b_buf, copies):
    copies[0].wait()
    dpred = (err_buf[...].astype(F32) / 64.0).astype(BF16).reshape(-1, err_buf.shape[-1])
    copies[1].wait()
    dact = nt(dpred, down_buf[...])
    copies[2].wait()
    dgate = (dact * a_buf[...].astype(F32)).astype(BF16)
    copies[3].wait()
    return dgate, (dact * b_buf[...].astype(F32)).astype(BF16)


def own_kernel(err_ref, d_ref, a_ref, b_ref, dg_ref, du_ref, errb, db, ab, bb, sem):
    copies = fetch((err_ref, d_ref, a_ref, b_ref), (errb, db, ab, bb), sem)
    dg_ref[...], du_ref[...] = hidden_grads(errb, db, ab, bb, copies)


def other_kernel(
    err_ref, d_ref, a_ref, b_ref, x0_ref, dg_ref, du_ref, x1_ref, y_ref,
    errb, db, ab, bb, x0b, dgb, dub, x1b, sem,
):
    copies = fetch(
        (err_ref, d_ref, a_ref, b_ref, x0_ref, dg_ref, du_ref, x1_ref),
        (errb, db, ab, bb, x0b, dgb, dub, x1b),
        sem,
    )
    dgate, dup = hidden_grads(errb, db, ab, bb, copies)
    for c in copies[4:]:
        c.wait()
    width, tall = dgate.shape[1], 256
    for i in range(y_ref.shape[0] // tall):
        at = pl.ds(i * tall, tall)
        y_ref[at, :width] = (dot(x0b[at], dgb[...]) + dot(x1b[at], dgate)).astype(BF16)
        y_ref[at, width:] = (dot(x0b[at], dub[...]) + dot(x1b[at], dup)).astype(BF16)


def sum_kernel(parts_ref, out_ref):
    total = parts_ref[0].astype(F32)
    for d in range(1, parts_ref.shape[0]):
        total = total + parts_ref[d].astype(F32)
    total = total.astype(BF16)
    for d in range(out_ref.shape[0]):
        out_ref[d] = total


def last_kernel(yg_ref, yu_ref, w_ref, gate_ref, up_ref):
    for y_ref, out_ref in ((yg_ref, gate_ref), (yu_ref, up_ref)):
        y = y_ref[...].reshape(w_ref.shape[0], out_ref.shape[1])
        out_ref[...] = lax.dot_general(
            w_ref[...], y, (((0,), (0,)), ((), ())), preferred_element_type=F32
        )


VM = pl.BlockSpec(memory_space=pltpu.VMEM)
HB = pl.BlockSpec(memory_space=pl.ANY)


def vmem_like(a, tail=False):
    shape = (a.shape[0], TAIL, LANES) if tail else a.shape
    return pltpu.VMEM(shape, a.dtype)


def evolve(line_pos, line_vel, stiff, contact, offset, attach, plat_pos, pick, dest):
    sds = jax.ShapeDtypeStruct
    large = (line_pos, line_vel, contact)
    small = (stiff, offset, attach, plat_pos, pick, dest)
    return pl.pallas_call(
        evolve_kernel,
        out_shape=(
            sds((ROWS, LANES), F32),
            sds((2 * COUNT, FEATS), BF16),
            sds((3 * STEPS, LANES), F32),
            sds((3, NODES, LANES), F32),
        ),
        in_specs=[HB] * 9,
        out_specs=(VM,) * 4,
        scratch_shapes=[vmem_like(a) for a in large + small]
        + [
            pltpu.VMEM((3 * NODES, LANES * (STEPS + 1)), BF16),
            pltpu.VMEM((ROWS, LANES), F32),
            pltpu.SemaphoreType.DMA((2, 2 + STEPS)),
        ],
        compiler_params=pltpu.CompilerParams(vmem_limit_bytes=LIMIT),
        cost_estimate=pl.CostEstimate(flops=260000000, bytes_accessed=3000000, transcendentals=0),
        name="evolve",
    )(line_pos, line_vel, stiff, contact, offset, attach, plat_pos, pick, dest)


def finish(recv, bound, rows, plats, lines, w_in, fpos):
    sds = jax.ShapeDtypeStruct
    args = (recv, bound, rows, *plats, *lines, w_in)
    at = 3 + len(plats)
    bufs = [vmem_like(a, at <= i < at + 3) for i, a in enumerate(args)]
    out = (
        sds((recv.shape[0], COUNT, FEATS), BF16),
        sds((COUNT, FEATS), BF16),
        sds((COUNT, w_in.shape[1]), BF16),
        sds((3, LANES), F32),
    )
    return pl.pallas_call(
        finish_kernel,
        out_shape=out + (sds(fpos.shape, F32),),
        in_specs=[HB] * (len(args) + 1),
        out_specs=(VM,) * len(out) + (HB,),
        scratch_shapes=bufs
        + [
            pltpu.VMEM((3 * TAIL, LANES * (STEPS + 1)), F32),
            pltpu.VMEM((3, TAIL, LANES), F32),
            pltpu.SemaphoreType.DMA((len(args),)),
            pltpu.SemaphoreType.DMA,
        ],
        input_output_aliases={len(args): len(out)},
        compiler_params=pltpu.CompilerParams(vmem_limit_bytes=LIMIT),
        cost_estimate=pl.CostEstimate(flops=300000000, bytes_accessed=4000000, transcendentals=0),
        name="finish",
    )(*args, fpos)


PARAMS = pltpu.CompilerParams(vmem_limit_bytes=LIMIT)
MIDDLE = pltpu.CompilerParams(vmem_limit_bytes=24 * 1024 * 1024)
SMALL = pltpu.CompilerParams(vmem_limit_bytes=16 * 1024 * 1024)


def staged(kernel, name, args, out_shape, scratch, flops, sems, out_specs=VM, bufs=None, params=PARAMS):
    bufs = [vmem_like(a) for a in args] if bufs is None else bufs
    return pl.pallas_call(
        kernel,
        out_shape=out_shape,
        in_specs=[HB] * len(args),
        out_specs=out_specs,
        scratch_shapes=bufs + scratch + [pltpu.SemaphoreType.DMA((n,)) for n in sems],
        compiler_params=params,
        cost_estimate=pl.CostEstimate(flops=flops, bytes_accessed=8000000, transcendentals=0),
        name=name,
    )(*args)


def cut(shape, parts, offset=0):
    block = shape[:-1] + (shape[-1] // parts,)
    return pl.BlockSpec(block, lambda i: (0,) * (len(shape) - 1) + (i + offset,))


def exchange(x, axes):
    return lax.all_to_all(x, axes, split_axis=0, concat_axis=0, tiled=True)


def dot(left, right):
    return jnp.dot(left, right, preferred_element_type=F32)


def swap(x):
    return lax.ppermute(x, "core", SWAP)


def after(x, *others):
    return lax.optimization_barrier((x,) + others)[0]


def body(
    line_pos, line_vel, stiffness, contact, offset, attach, plat_pos, plat_vel, inv_mass, restoring,
    kernel, vel_hist, wave, sample_pick, sample_dest, w_in, gain, w_gate, w_up, w_down, w_out,
):
    sds = jax.ShapeDtypeStruct
    chips = lax.axis_size(CHIP)
    groups = lax.axis_size(GRP)
    half = chips * COUNT
    width = w_gate.shape[1]
    stiff, att, pick, dest = stiffness[None], attach[None], sample_pick[None], sample_dest.reshape(1, -1)
    pay, rows, bound, fpos = evolve(
        line_pos, line_vel, stiff, contact, offset, att, plat_pos, pick, dest
    )
    pay = jnp.broadcast_to((pay + swap(pay))[None], (chips,) + pay.shape)
    pay, w_in_late, w_down_late = lax.optimization_barrier((pay, w_in, w_down))
    recv = exchange(pay, CHIP)
    product = sds((FEATS, width), BF16)
    gate_w, up_w = staged(
        products_kernel, "products", (w_in_late, gain[None], w_gate, w_up), (product, product),
        [pltpu.VMEM(w_in.shape, BF16)], 3300000000, (4,), (VM,) * 2,
    )
    gate_o, up_o = swap(gate_w), swap(up_w)
    w_down_o = swap(w_down)
    turned = lambda a: a.transpose(1, 0, 2)
    x_own, target, hidden, final_plat, final_pos = finish(
        recv, bound, rows,
        (plat_pos, plat_vel, inv_mass, restoring, turned(kernel), turned(vel_hist), turned(wave)),
        (line_pos, line_vel, contact, stiff, offset, att, pick),
        w_in, fpos,
    )
    x_own, w_down_late, w_down_o, hidden = lax.optimization_barrier((x_own, w_down_late, w_down_o, hidden))
    x = exchange(x_own, CHIP)
    product = sds((width, FEATS), BF16)
    down_w, down_o = staged(
        down_kernel, "down", (w_down_late, w_down_o, w_out), (product, product), [], 3300000000, (3,), (VM,) * 2
    )
    base = lax.optimization_barrier(dot(hidden, w_out) - target.astype(F32))
    args = (x, gate_w, up_w, down_w, gate_o, up_o, down_o)
    wide = sds((2, half, width), F32)
    part, gate, upper = staged(
        forward_kernel, "forward", args, (sds(x.shape, BF16), wide, wide),
        [pltpu.VMEM(wide.shape, F32)] * 2, 2500000000, (7, 4), (VM, HB, HB),
    )
    part, gate, upper, x_late, w_in_late = lax.optimization_barrier((part, gate, upper, x, w_in_late))
    parts = exchange(part, CHIP)
    slope = sds((half, width), BF16)
    wide_rows = pl.BlockSpec((2, half // 4, width), lambda i: (0, i, 0))
    slope_rows = pl.BlockSpec((half // 4, width), lambda i: (i, 0))
    slope_a, slope_b, slope_ao, slope_bo = pl.pallas_call(
        slopes_kernel, grid=(4,), out_shape=(slope,) * 4, in_specs=[wide_rows] * 2,
        out_specs=(slope_rows,) * 4, compiler_params=PARAMS, name="slopes",
        cost_estimate=pl.CostEstimate(flops=8000000, bytes_accessed=6000000, transcendentals=1000000),
    )(gate, upper)
    slope_ao, slope_bo = swap(slope_ao), swap(slope_bo)
    x_late, slope_a = lax.optimization_barrier((x_late, slope_a))
    x_late = lax.optimization_barrier(x_late.reshape(half, FEATS).T)
    x_other = swap(x_late)
    at = lax.axis_index(GRP)
    block = w_in.shape[1] // groups
    w_own = lax.optimization_barrier(lax.dynamic_slice_in_dim(w_in_late, at * block, block, 1))
    gain_own = lax.dynamic_slice_in_dim(gain, at * block, block, 0)
    w_own = lax.optimization_barrier((w_own.astype(F32) * gain_own).astype(BF16))
    err_own = pl.pallas_call(
        error_kernel, grid=(3,), out_shape=sds((chips, COUNT, FEATS), BF16),
        in_specs=[cut(parts.shape, 3), cut(base.shape, 3)], out_specs=cut(parts.shape, 3),
        compiler_params=SMALL, name="error",
    )(parts, base)
    err_own, slope_ao, slope_bo = lax.optimization_barrier((err_own, slope_ao, slope_bo))
    err = exchange(err_own, CHIP)
    err_other = swap(err)
    dg, du = staged(
        own_kernel, "own", (err, down_w, slope_a, slope_b), (slope, slope), [], 400000000, (4,), (VM,) * 2, params=MIDDLE,
    )
    feat_grads = staged(
        other_kernel, "other", (err_other, down_w, slope_ao, slope_bo, x_late, dg, du, x_other),
        sds((FEATS, 2 * width), BF16), [], 2000000000, (8,), params=MIDDLE,
    )
    feat_grads = exchange(feat_grads.reshape(groups, FEATS // groups, 2 * width), GRP)
    feat_grads = pl.pallas_call(
        sum_kernel, grid=(4,), out_shape=sds(feat_grads.shape, BF16), in_specs=[cut(feat_grads.shape, 4)],
        out_specs=cut(feat_grads.shape, 4), compiler_params=SMALL, name="total",
    )(feat_grads)
    feat_grads, err_late, err_other = lax.optimization_barrier((feat_grads, err, err_other))
    feat_grads = exchange(feat_grads, GRP)
    grad = sds((block, width), F32)
    grad_gate, grad_up = pl.pallas_call(
        last_kernel, grid=(2,), out_shape=(grad, grad),
        in_specs=[
            cut(feat_grads.shape, 4), cut(feat_grads.shape, 4, 2), pl.BlockSpec(w_own.shape, lambda i: (0, 0))
        ],
        out_specs=(cut(grad.shape, 2),) * 2, compiler_params=SMALL, name="last",
    )(feat_grads, feat_grads, w_own)
    err_all = jnp.concatenate([err_late, err_other], axis=0).reshape(2 * half, FEATS)
    core = lax.axis_index("core")
    codes = recv[:, CODE_ROW : CODE_ROW + 2, :COUNT]
    codes = jnp.where(core == 0, codes, codes[:, ::-1]).transpose(1, 0, 2).reshape(1, 2 * half)
    me = lax.axis_index(CHIP) * 2 + core
    number = jnp.arange(2 * half, dtype=jnp.int32)
    source = ((number // COUNT) % chips) * 2 + (number // half + core) % 2
    slot = jnp.arange(2 * chips * CAP, dtype=jnp.int32)[:, None]
    match = (source[None] == slot // CAP) & (codes == (me * CAP + slot % CAP).astype(F32))
    slot_error = dot(match.astype(BF16), err_all).astype(BF16)
    return (final_pos, final_plat, slot_error, grad_gate, grad_up)


def solution(mesh):
    sizes = (4, 2, 2, 4, 2)
    if mesh.devices.shape[0] == 1:
        sizes = (1, 1, 2, 4, 2)
    fine = Mesh(mesh.devices.reshape(sizes), ALL)
    in_specs = (
        P(None, None, ALL),
        P(None, None, ALL),
        P(ALL),
        P(None, None, ALL),
        P(None, ALL),
        P(ALL),
        P(None, GRP),
        P(None, GRP),
        P(None, GRP),
        P(None, GRP),
        P(None, None, GRP),
        P(None, None, GRP),
        P(None, None, GRP),
        P(ALL),
        P(ALL, None),
        P(),
        P(),
        P(None, DEV),
        P(None, DEV),
        P(DEV, None),
        P(),
    )
    out_specs = (
        P(None, None, ALL),
        P(None, GRP),
        P(ALL, None),
        P(GRP, DEV),
        P(GRP, DEV),
    )
    return jax.shard_map(body, mesh=fine, in_specs=in_specs, out_specs=out_specs, check_vma=False)
```

```python
import functools
import jax
import jax.numpy as jnp
from jax import lax
from jax.experimental import pallas as pl
from jax.experimental.pallas import tpu as pltpu
from jax.sharding import Mesh, PartitionSpec as P

STEPS = 8
CAP = 8
NODES = 256
TAIL = 8
LANES = 128
COUNT = 64
FEATS = 768
ROWS = 72
ONES_ROW = 24
CODE_ROW = 67
LIMIT = 60 * 1024 * 1024
HIGH = lax.Precision.HIGHEST
F32 = jnp.float32
BF16 = jnp.bfloat16
DEV = ("zl", "x", "core")
CHIP = ("zl", "x")
GRP = ("y", "zh")
ALL = GRP + DEV
PAIRS = [(s, t) for s in range(2, STEPS) for t in range(1, s)]
SWAP = [(0, 1), (1, 0)]
SHIFTS = (1, 3, 2)
SENT = [(flip, d) for flip in (1, 0) for d in SHIFTS + (0,)]
GOT = [(0, 0), (1, 0)] + [(flip, d) for flip in (0, 1) for d in SHIFTS]


def nt(left, right, precision=None):
    return lax.dot_general(
        left, right, (((1,), (1,)), ((), ())), precision=precision, preferred_element_type=F32
    )


def iota(shape, dim):
    return lax.broadcasted_iota(jnp.int32, shape, dim)


def pick_matrix(pick_ref):
    count = pick_ref.shape[1]
    eye = iota((count, count), 0) == iota((count, count), 1)
    pick = jnp.sum(jnp.where(eye, pick_ref[...].astype(F32), 0.0), axis=1, keepdims=True).astype(jnp.int32)
    at = (pick >> 3) + LANES * (pick & 7)
    at = jnp.concatenate([at, at + LANES], axis=0)
    return (iota((2 * count, LANES * (STEPS + 1)), 1) == at).astype(F32).astype(BF16)


def fetch(refs, bufs, sem):
    copies = [pltpu.make_async_copy(r, b, sem.at[i]) for i, (r, b) in enumerate(zip(refs, bufs))]
    for c in copies:
        c.start()
    return copies


def evolve_kernel(
    pos_ref, vel_ref, stiff_ref, contact_ref, off_ref, attach_ref, plat_ref, pick_ref, dest_ref,
    pay_ref, rows_ref, bound_ref, fpos_ref,
    posb, velb, contactb, stiffb, offb, attachb, platb, pickb, destb, stack, lin, sem,
):
    small = fetch(
        (stiff_ref, off_ref, attach_ref, plat_ref, pick_ref, dest_ref),
        (stiffb, offb, attachb, platb, pickb, destb),
        sem.at[0],
    )
    large = fetch(
        (pos_ref, vel_ref) + tuple(contact_ref.at[s] for s in range(STEPS)),
        (posb, velb) + tuple(contactb.at[s] for s in range(STEPS)),
        sem.at[1],
    )
    for c in small:
        c.wait()
    k = stiffb[...]
    onehot = (attachb[...] == iota((LANES, LANES), 0)).astype(F32)
    off = offb[...]
    fair = jnp.dot(platb[...], onehot, precision=HIGH, preferred_element_type=F32) + off
    picks = pick_matrix(pickb)
    row = iota((NODES, LANES), 0)
    first, last, bulk = row == 0, row == NODES - 1, row < NODES - TAIL
    lin[...] = jnp.zeros_like(lin)
    lin[ONES_ROW : ONES_ROW + 1] = jnp.ones((1, LANES), F32)
    large[0].wait()
    large[1].wait()
    pos = [jnp.where(last, fair[c : c + 1], posb[c]) for c in range(3)]
    vel = [velb[c] for c in range(3)]
    for step in range(STEPS):
        large[2 + step].wait()
        touch = contactb[step].astype(F32)
        damp = 0.02 + 0.1 * touch
        for c in range(3):
            p = pos[c]
            stack[c * NODES : (c + 1) * NODES, step * LANES : (step + 1) * LANES] = jnp.where(bulk, p, 0.0).astype(BF16)
            bound_ref[step * 3 + c : step * 3 + c + 1] = p[NODES - TAIL - 1 : NODES - TAIL]
            lin[step * 3 + c : step * 3 + c + 1] = p[NODES - 2 : NODES - 1] - p[NODES - 1 : NODES]
            accel = k * (pltpu.roll(p, NODES - 1, 0) - 2.0 * p + pltpu.roll(p, 1, 0)) - damp * vel[c]
            if c == 2:
                accel = accel + (-0.05 - 0.3 * touch * (p + 2.0))
            vel[c] = vel[c] + accel
            pos[c] = jnp.where(first, p, jnp.where(last, off[c : c + 1], p + vel[c]))
    for c in range(3):
        stack[c * NODES : (c + 1) * NODES, STEPS * LANES :] = jnp.where(bulk, pos[c], 0.0).astype(BF16)
        fpos_ref[c] = pos[c]
    rows_ref[...] = nt(picks, stack[...]).astype(BF16)
    trow = iota((TAIL, LANES), 0)
    zero = jnp.zeros((TAIL, LANES), F32)
    for kind in range(2):
        rp, rv = [zero] * 6, [zero] * 6
        for step in range(1, STEPS):
            for t in range(1, step):
                at = ONES_ROW + 1 + 2 * PAIRS.index((step, t)) + kind
                lin[at : at + 1] = rp[t - 1][TAIL - 2 : TAIL - 1]
            if step == STEPS - 1:
                break
            touch = contactb[step, NODES - TAIL : NODES].astype(F32)
            damp = 0.02 + 0.1 * touch
            for t in range(1, step + 1):
                p = jnp.where(trow == TAIL - 1, 1.0 if t == step else 0.0, rp[t - 1])
                up = pltpu.roll(p, TAIL - 1, 0)
                down = jnp.where(trow == 0, 0.0, pltpu.roll(p, 1, 0))
                accel = k * (up - 2.0 * p + down) - damp * rv[t - 1]
                if kind == 1:
                    accel = accel - 0.3 * touch * p
                rv[t - 1] = rv[t - 1] + accel
                rp[t - 1] = p + rv[t - 1]
    sums = nt(lin[...] * k, onehot, HIGH)
    count = destb.shape[1]
    lane, sub = iota((count, count), 1), iota((count, count), 0)
    dest = destb[...].astype(F32)
    dest_col = jnp.sum(jnp.where(lane == sub, dest, 0.0), axis=1, keepdims=True)
    rank = jnp.sum(jnp.where((dest_col == dest) & (sub < lane), 1.0, 0.0), axis=0, keepdims=True)
    codes = jnp.concatenate([dest * CAP + rank, jnp.full((1, LANES - count), -1.0, F32)], axis=1)
    pay_ref[...] = jnp.where(iota((ROWS, LANES), 0) == CODE_ROW + lax.axis_index("core"), codes, sums)


def finish_kernel(
    recv_ref, bound_ref, rows_ref, plat_ref, plat_vel_ref, inv_ref, rest_ref, kern_ref, hist_ref, wave_ref,
    pos_ref, vel_ref, contact_ref, stiff_ref, off_ref, attach_ref, pick_ref, w_in_ref, fpos_in,
    x_ref, t_ref, h_ref, plat_out, fpos_ref,
    recvb, boundb, rowsb, platb, plat_velb, invb, restb, kernb, histb, waveb,
    posb, velb, contactb, stiffb, offb, attachb, pickb, w_inb, tails, final, sem, out_sem,
):
    at = pl.ds(NODES - TAIL, TAIL)
    copies = fetch(
        (
            recv_ref, plat_ref, plat_vel_ref, inv_ref, rest_ref, kern_ref, hist_ref, wave_ref,
            stiff_ref, off_ref, attach_ref, pick_ref, bound_ref, rows_ref,
            pos_ref.at[:, at, :], vel_ref.at[:, at, :], contact_ref.at[:, at, :], w_in_ref,
        ),
        (
            recvb, platb, plat_velb, invb, restb, kernb, histb, waveb,
            stiffb, offb, attachb, pickb, boundb, rowsb, posb, velb, contactb, w_inb,
        ),
        sem,
    )
    for c in copies[:-1]:
        c.wait()
    total = recvb[0]
    for d in range(1, recvb.shape[0]):
        total = total + recvb[d]
    q, u = platb[...], plat_velb[...]
    hist = [histb[:, m] for m in range(STEPS)]
    kern = [kernb[:, m] for m in range(STEPS)]
    ones = total[ONES_ROW : ONES_ROW + 1]
    qs = [q]
    for step in range(STEPS):
        force = total[3 * step : 3 * step + 3]
        if step > 0:
            force = force - ones * q
        for t in range(1, step):
            at = ONES_ROW + 1 + 2 * PAIRS.index((step, t))
            coef = jnp.concatenate([total[at : at + 1], total[at : at + 2]], axis=0)
            force = force + coef * qs[t]
        memory = kern[0] * hist[0]
        for m in range(1, STEPS):
            memory = memory + kern[m] * hist[m]
        u = u + invb[...] * (force - restb[...] * q - memory + waveb[:, step])
        q = q + u
        hist = [u] + hist[:-1]
        qs.append(q)
    plat_out[...] = q
    k = stiffb[...]
    onehot = (attachb[...] == iota((LANES, LANES), 0)).astype(F32)
    fair = jnp.dot(jnp.concatenate(qs, axis=0), onehot, precision=HIGH, preferred_element_type=F32)
    trow = iota((TAIL, LANES), 0)
    pos = [posb[c] for c in range(3)]
    vel = [velb[c] for c in range(3)]
    for step in range(STEPS + 1):
        for c in range(3):
            here = fair[step * 3 + c : step * 3 + c + 1] + offb[c : c + 1]
            p = jnp.where(trow == TAIL - 1, here, pos[c])
            tails[c * TAIL : (c + 1) * TAIL, step * LANES : (step + 1) * LANES] = p
            if step == STEPS:
                final[c] = p
                continue
            touch = contactb[step].astype(F32)
            up = pltpu.roll(p, TAIL - 1, 0)
            bound = boundb[step * 3 + c : step * 3 + c + 1]
            down = jnp.where(trow == 0, bound, pltpu.roll(p, 1, 0))
            accel = k * (up - 2.0 * p + down) - (0.02 + 0.1 * touch) * vel[c]
            if c == 2:
                accel = accel + (-0.05 - 0.3 * touch * (p + 2.0))
            vel[c] = vel[c] + accel
            pos[c] = p + vel[c]
    copy = pltpu.make_async_copy(final, fpos_ref.at[:, NODES - TAIL : NODES, :], out_sem)
    copy.start()
    picked = nt(pick_matrix(pickb), tails[...].astype(BF16)).astype(BF16)
    at = iota((3 * TAIL, FEATS), 0)
    where = (at // TAIL) * NODES + (NODES - TAIL) + at % TAIL
    place = (iota((3 * TAIL, FEATS), 1) == where).astype(F32).astype(BF16)
    rows = rowsb[...].astype(F32) + jnp.dot(picked, place, preferred_element_type=F32)
    count = t_ref.shape[0]
    t_ref[...] = rows[count:].astype(BF16)
    copies[-1].wait()
    hidden = jnp.dot(rows[:count].astype(BF16), w_inb[...], preferred_element_type=F32).astype(BF16)
    h_ref[...] = hidden
    wide = hidden.astype(F32)
    scale = lax.rsqrt(jnp.mean(wide * wide, axis=1, keepdims=True) + 1e-06)
    scaled = (rows[:count] * scale).astype(BF16)
    for d in range(x_ref.shape[0]):
        x_ref[d] = scaled
    copy.wait()


def products_kernel(w_in_ref, gain_ref, gate_ref, up_ref, g_ref, u_ref, w_inb, gainb, gateb, upb, scaled, sem):
    copies = fetch((gain_ref, w_in_ref, gate_ref, up_ref), (gainb, w_inb, gateb, upb), sem)
    copies[0].wait()
    copies[1].wait()
    rows = 256
    for i in range(w_inb.shape[0] // rows):
        at = pl.ds(i * rows, rows)
        scaled[at] = (w_inb[at].astype(F32) * gainb[...]).astype(BF16)
        if i == 0:
            copies[2].wait()
        g_ref[at] = dot(scaled[at], gateb[...]).astype(BF16)
        if i == 0:
            copies[3].wait()
        u_ref[at] = dot(scaled[at], upb[...]).astype(BF16)


def down_kernel(w0_ref, w1_ref, out_ref, d0_ref, d1_ref, w0b, w1b, outb, sem):
    copies = fetch((out_ref, w0_ref, w1_ref), (outb, w0b, w1b), sem)
    copies[0].wait()
    tall = 256
    for copy, w, d_ref in ((copies[1], w0b, d0_ref), (copies[2], w1b, d1_ref)):
        copy.wait()
        for i in range(w.shape[0] // tall):
            at = pl.ds(i * tall, tall)
            d_ref[at] = dot(w[at], outb[...]).astype(BF16)


def forward_kernel(
    x_ref, g0_ref, u0_ref, d0_ref, g1_ref, u1_ref, d1_ref, part_ref, gate_ref, up_ref,
    xb, g0b, u0b, d0b, g1b, u1b, d1b, gateb, upb, sem, out_sem,
):
    copies = fetch(
        (x_ref, g0_ref, u0_ref, d0_ref, g1_ref, u1_ref, d1_ref), (xb, g0b, u0b, d0b, g1b, u1b, d1b), sem
    )
    copies[0].wait()
    x = xb[...].reshape(-1, xb.shape[-1])
    part, outs = None, []
    for side, (g, u, d) in enumerate(((g0b, u0b, d0b), (g1b, u1b, d1b))):
        copies[1 + 3 * side].wait()
        gate = dot(x, g[...])
        gateb[side] = gate
        copies[2 + 3 * side].wait()
        upper = dot(x, u[...])
        upb[side] = upper
        for i, (buf, ref) in enumerate(((gateb, gate_ref), (upb, up_ref))):
            out = pltpu.make_async_copy(buf.at[side], ref.at[side], out_sem.at[2 * side + i])
            out.start()
            outs.append(out)
        act = (gate * jax.nn.sigmoid(gate) * upper).astype(BF16)
        copies[3 + 3 * side].wait()
        term = dot(act, d[...])
        part = term if part is None else part + term
    part_ref[...] = part.astype(BF16).reshape(part_ref.shape)
    for out in outs:
        out.wait()


def slopes_kernel(gate_ref, up_ref, a0_ref, b0_ref, a1_ref, b1_ref):
    for side, (a_ref, b_ref) in enumerate(((a0_ref, b0_ref), (a1_ref, b1_ref))):
        gate, upper = gate_ref[side], up_ref[side]
        sigma = jax.nn.sigmoid(gate)
        a_ref[...] = (upper * sigma * (1.0 + gate * (1.0 - sigma))).astype(BF16)
        b_ref[...] = (gate * sigma).astype(BF16)


def error_kernel(parts_ref, base_ref, err_ref):
    total = base_ref[...]
    for d in range(parts_ref.shape[0]):
        total = total + parts_ref[d].astype(F32)
    total = total.astype(BF16)
    for d in range(err_ref.shape[0]):
        err_ref[d] = total


def hidden_grads(err_buf, down_buf, a_buf, b_buf, copies):
    copies[0].wait()
    dpred = (err_buf[...].astype(F32) / 64.0).astype(BF16).reshape(-1, err_buf.shape[-1])
    copies[1].wait()
    dact = nt(dpred, down_buf[...])
    copies[2].wait()
    dgate = (dact * a_buf[...].astype(F32)).astype(BF16)
    copies[3].wait()
    return dgate, (dact * b_buf[...].astype(F32)).astype(BF16)


def own_kernel(err_ref, d_ref, a_ref, b_ref, dg_ref, du_ref, errb, db, ab, bb, sem):
    copies = fetch((err_ref, d_ref, a_ref, b_ref), (errb, db, ab, bb), sem)
    dg_ref[...], du_ref[...] = hidden_grads(errb, db, ab, bb, copies)


def group_block(flip, shift):
    y, zh = lax.axis_index("y"), lax.axis_index("zh")
    zh = 1 - zh if flip else zh
    return lax.rem(y + shift + 4, 4) * 2 + zh


def other_kernel(err_ref, d_ref, a_ref, b_ref, x0_ref, dg_ref, du_ref, x1_ref, *refs):
    outs, (errb, db, ab, bb, x0b, dgb, dub, x1b, yb, sem, out_sem) = refs[: len(SENT)], refs[len(SENT) :]
    copies = fetch(
        (err_ref, d_ref, a_ref, b_ref, x0_ref, dg_ref, du_ref, x1_ref),
        (errb, db, ab, bb, x0b, dgb, dub, x1b),
        sem,
    )
    dgate, dup = hidden_grads(errb, db, ab, bb, copies)
    for c in copies[4:]:
        c.wait()
    width, tall = dgate.shape[1], 256
    for i in range(yb.shape[0] // tall):
        at = pl.ds(i * tall, tall)
        yb[at, :width] = (dot(x0b[at], dgb[...]) + dot(x1b[at], dgate)).astype(BF16)
        yb[at, width:] = (dot(x0b[at], dub[...]) + dot(x1b[at], dup)).astype(BF16)
    rows, sends = outs[0].shape[0], []
    for i, (flip, d) in enumerate(SENT):
        at = pl.ds(pl.multiple_of(group_block(flip, d) * rows, rows), rows)
        sends.append(pltpu.make_async_copy(yb.at[at], outs[i], out_sem.at[i]))
        sends[-1].start()
    for c in sends:
        c.wait()


def last_kernel(w_ref, *refs):
    parts, (gate_ref, up_ref, wb, yb, sem, y_sem) = refs[: len(GOT)], refs[len(GOT) :]
    rows = parts[0].shape[0]
    slots = [pl.ds(i * rows, rows) for i in range(len(GOT))]
    blocks = [pl.ds(pl.multiple_of(group_block(flip, -d) * rows, rows), rows) for flip, d in GOT]
    copies = fetch([w_ref.at[b] for b in blocks], [wb.at[i] for i in slots], sem)
    copies += fetch(parts, [yb.at[i] for i in slots], y_sem)
    for c in copies:
        c.wait()
    width = gate_ref.shape[1]
    gate_ref[...] = tn(wb[...], yb[:, :width])
    up_ref[...] = tn(wb[...], yb[:, width:])


VM = pl.BlockSpec(memory_space=pltpu.VMEM)
HB = pl.BlockSpec(memory_space=pl.ANY)


def vmem_like(a, tail=False):
    shape = (a.shape[0], TAIL, LANES) if tail else a.shape
    return pltpu.VMEM(shape, a.dtype)


def evolve(line_pos, line_vel, stiff, contact, offset, attach, plat_pos, pick, dest):
    sds = jax.ShapeDtypeStruct
    large = (line_pos, line_vel, contact)
    small = (stiff, offset, attach, plat_pos, pick, dest)
    return pl.pallas_call(
        evolve_kernel,
        out_shape=(
            sds((ROWS, LANES), F32),
            sds((2 * COUNT, FEATS), BF16),
            sds((3 * STEPS, LANES), F32),
            sds((3, NODES, LANES), F32),
        ),
        in_specs=[HB] * 9,
        out_specs=(VM,) * 4,
        scratch_shapes=[vmem_like(a) for a in large + small]
        + [
            pltpu.VMEM((3 * NODES, LANES * (STEPS + 1)), BF16),
            pltpu.VMEM((ROWS, LANES), F32),
            pltpu.SemaphoreType.DMA((2, 2 + STEPS)),
        ],
        compiler_params=pltpu.CompilerParams(vmem_limit_bytes=LIMIT),
        cost_estimate=pl.CostEstimate(flops=260000000, bytes_accessed=3000000, transcendentals=0),
        name="evolve",
    )(line_pos, line_vel, stiff, contact, offset, attach, plat_pos, pick, dest)


def finish(recv, bound, rows, plats, lines, w_in, fpos):
    sds = jax.ShapeDtypeStruct
    args = (recv, bound, rows, *plats, *lines, w_in)
    at = 3 + len(plats)
    bufs = [vmem_like(a, at <= i < at + 3) for i, a in enumerate(args)]
    out = (
        sds((recv.shape[0], COUNT, FEATS), BF16),
        sds((COUNT, FEATS), BF16),
        sds((COUNT, w_in.shape[1]), BF16),
        sds((3, LANES), F32),
    )
    return pl.pallas_call(
        finish_kernel,
        out_shape=out + (sds(fpos.shape, F32),),
        in_specs=[HB] * (len(args) + 1),
        out_specs=(VM,) * len(out) + (HB,),
        scratch_shapes=bufs
        + [
            pltpu.VMEM((3 * TAIL, LANES * (STEPS + 1)), F32),
            pltpu.VMEM((3, TAIL, LANES), F32),
            pltpu.SemaphoreType.DMA((len(args),)),
            pltpu.SemaphoreType.DMA,
        ],
        input_output_aliases={len(args): len(out)},
        compiler_params=pltpu.CompilerParams(vmem_limit_bytes=LIMIT),
        cost_estimate=pl.CostEstimate(flops=300000000, bytes_accessed=4000000, transcendentals=0),
        name="finish",
    )(*args, fpos)


PARAMS = pltpu.CompilerParams(vmem_limit_bytes=LIMIT)
MIDDLE = pltpu.CompilerParams(vmem_limit_bytes=24 * 1024 * 1024)
SMALL = pltpu.CompilerParams(vmem_limit_bytes=16 * 1024 * 1024)


def staged(kernel, name, args, out_shape, scratch, flops, sems, out_specs=VM, bufs=None, params=PARAMS):
    bufs = [vmem_like(a) for a in args] if bufs is None else bufs
    return pl.pallas_call(
        kernel,
        out_shape=out_shape,
        in_specs=[HB] * len(args),
        out_specs=out_specs,
        scratch_shapes=bufs + scratch + [pltpu.SemaphoreType.DMA((n,)) for n in sems],
        compiler_params=params,
        cost_estimate=pl.CostEstimate(flops=flops, bytes_accessed=8000000, transcendentals=0),
        name=name,
    )(*args)


def cut(shape, parts, offset=0):
    block = shape[:-1] + (shape[-1] // parts,)
    return pl.BlockSpec(block, lambda i: (0,) * (len(shape) - 1) + (i + offset,))


def exchange(x, axes):
    return lax.all_to_all(x, axes, split_axis=0, concat_axis=0, tiled=True)


def dot(left, right):
    return jnp.dot(left, right, preferred_element_type=F32)


def tn(left, right):
    return lax.dot_general(left, right, (((0,), (0,)), ((), ())), preferred_element_type=F32)


def swap(x, axis="core"):
    return lax.ppermute(x, axis, SWAP)


def shift(x, d):
    return lax.ppermute(x, "y", [(i, (i + d) % 4) for i in range(4)])


def total(first, *others):
    out = first.astype(F32)
    for o in others:
        out = out + o.astype(F32)
    return out.astype(BF16)


def after(x, *others):
    return lax.optimization_barrier((x,) + others)[0]


def body(
    line_pos, line_vel, stiffness, contact, offset, attach, plat_pos, plat_vel, inv_mass, restoring,
    kernel, vel_hist, wave, sample_pick, sample_dest, w_in, gain, w_gate, w_up, w_down, w_out,
):
    sds = jax.ShapeDtypeStruct
    chips = lax.axis_size(CHIP)
    groups = lax.axis_size(GRP)
    half = chips * COUNT
    width = w_gate.shape[1]
    stiff, att, pick, dest = stiffness[None], attach[None], sample_pick[None], sample_dest.reshape(1, -1)
    pay, rows, bound, fpos = evolve(
        line_pos, line_vel, stiff, contact, offset, att, plat_pos, pick, dest
    )
    pay = jnp.broadcast_to((pay + swap(pay))[None], (chips,) + pay.shape)
    pay, w_in_late, w_down_late = lax.optimization_barrier((pay, w_in, w_down))
    recv = exchange(pay, CHIP)
    product = sds((FEATS, width), BF16)
    gate_w, up_w = staged(
        products_kernel, "products", (w_in_late, gain[None], w_gate, w_up), (product, product),
        [pltpu.VMEM(w_in.shape, BF16)], 3300000000, (4,), (VM,) * 2,
    )
    gate_o, up_o = swap(gate_w), swap(up_w)
    w_down_o = swap(w_down)
    turned = lambda a: a.transpose(1, 0, 2)
    x_own, target, hidden, final_plat, final_pos = finish(
        recv, bound, rows,
        (plat_pos, plat_vel, inv_mass, restoring, turned(kernel), turned(vel_hist), turned(wave)),
        (line_pos, line_vel, contact, stiff, offset, att, pick),
        w_in, fpos,
    )
    x_own, w_down_late, w_down_o, hidden = lax.optimization_barrier((x_own, w_down_late, w_down_o, hidden))
    x = exchange(x_own, CHIP)
    product = sds((width, FEATS), BF16)
    down_w, down_o = staged(
        down_kernel, "down", (w_down_late, w_down_o, w_out), (product, product), [], 3300000000, (3,), (VM,) * 2
    )
    base = lax.optimization_barrier(dot(hidden, w_out) - target.astype(F32))
    args = (x, gate_w, up_w, down_w, gate_o, up_o, down_o)
    wide = sds((2, half, width), F32)
    part, gate, upper = staged(
        forward_kernel, "forward", args, (sds(x.shape, BF16), wide, wide),
        [pltpu.VMEM(wide.shape, F32)] * 2, 2500000000, (7, 4), (VM, HB, HB),
    )
    part, gate, upper, x_late, w_in_late = lax.optimization_barrier((part, gate, upper, x, w_in_late))
    parts = exchange(part, CHIP)
    slope = sds((half, width), BF16)
    wide_rows = pl.BlockSpec((2, half // 4, width), lambda i: (0, i, 0))
    slope_rows = pl.BlockSpec((half // 4, width), lambda i: (i, 0))
    slope_a, slope_b, slope_ao, slope_bo = pl.pallas_call(
        slopes_kernel, grid=(4,), out_shape=(slope,) * 4, in_specs=[wide_rows] * 2,
        out_specs=(slope_rows,) * 4, compiler_params=PARAMS, name="slopes",
        cost_estimate=pl.CostEstimate(flops=8000000, bytes_accessed=6000000, transcendentals=1000000),
    )(gate, upper)
    slope_ao, slope_bo = swap(slope_ao), swap(slope_bo)
    x_late, slope_a = lax.optimization_barrier((x_late, slope_a))
    x_late = lax.optimization_barrier(x_late.reshape(half, FEATS).T)
    x_other = swap(x_late)
    at = lax.axis_index(GRP)
    block = w_in.shape[1] // groups
    w_own = lax.optimization_barrier(lax.dynamic_slice_in_dim(w_in_late, at * block, block, 1))
    gain_own = lax.dynamic_slice_in_dim(gain, at * block, block, 0)
    w_own = lax.optimization_barrier((w_own.astype(F32) * gain_own).astype(BF16))
    err_own = pl.pallas_call(
        error_kernel, grid=(3,), out_shape=sds((chips, COUNT, FEATS), BF16),
        in_specs=[cut(parts.shape, 3), cut(base.shape, 3)], out_specs=cut(parts.shape, 3),
        compiler_params=SMALL, name="error",
    )(parts, base)
    err_own, slope_ao, slope_bo = lax.optimization_barrier((err_own, slope_ao, slope_bo))
    err = exchange(err_own, CHIP)
    err_other = swap(err)
    dg, du = staged(
        own_kernel, "own", (err, down_w, slope_a, slope_b), (slope, slope), [], 400000000, (4,), (VM,) * 2,
    )
    piece = sds((FEATS // groups, 2 * width), BF16)
    pieces = staged(
        other_kernel, "other", (err_other, down_w, slope_ao, slope_bo, x_late, dg, du, x_other),
        (piece,) * len(SENT), [pltpu.VMEM((FEATS, 2 * width), BF16)], 2000000000, (8, len(SENT)),
        (HB,) * len(SENT),
    )
    moved = [shift(p, d) if d else p for p, (_, d) in zip(pieces, SENT)]
    theirs = swap(total(*moved[:4]), "zh")
    grads = total(*moved[4:], theirs)
    grads, err_late, err_other = lax.optimization_barrier((grads, err, err_other))
    twin = swap(grads, "zh")
    got = [grads, twin] + [shift(v, d) for v in (grads, twin) for d in SHIFTS]
    grad = sds((block, width), F32)
    grad_gate, grad_up = staged(
        last_kernel, "last", (w_own, *got), (grad, grad), [], 400000000, (len(GOT),) * 2, (VM,) * 2,
        bufs=[vmem_like(w_own), pltpu.VMEM((FEATS, 2 * width), BF16)], params=MIDDLE,
    )
    err_all = jnp.concatenate([err_late, err_other], axis=0).reshape(2 * half, FEATS)
    core = lax.axis_index("core")
    codes = recv[:, CODE_ROW : CODE_ROW + 2, :COUNT]
    codes = jnp.where(core == 0, codes, codes[:, ::-1]).transpose(1, 0, 2).reshape(1, 2 * half)
    me = lax.axis_index(CHIP) * 2 + core
    number = jnp.arange(2 * half, dtype=jnp.int32)
    source = ((number // COUNT) % chips) * 2 + (number // half + core) % 2
    slot = jnp.arange(2 * chips * CAP, dtype=jnp.int32)[:, None]
    match = (source[None] == slot // CAP) & (codes == (me * CAP + slot % CAP).astype(F32))
    slot_error = dot(match.astype(BF16), err_all).astype(BF16)
    return (final_pos, final_plat, slot_error, grad_gate, grad_up)


def solution(mesh):
    sizes = (4, 2, 2, 4, 2)
    if mesh.devices.shape[0] == 1:
        sizes = (1, 1, 2, 4, 2)
    fine = Mesh(mesh.devices.reshape(sizes), ALL)
    in_specs = (
        P(None, None, ALL),
        P(None, None, ALL),
        P(ALL),
        P(None, None, ALL),
        P(None, ALL),
        P(ALL),
        P(None, GRP),
        P(None, GRP),
        P(None, GRP),
        P(None, GRP),
        P(None, None, GRP),
        P(None, None, GRP),
        P(None, None, GRP),
        P(ALL),
        P(ALL, None),
        P(),
        P(),
        P(None, DEV),
        P(None, DEV),
        P(DEV, None),
        P(),
    )
    out_specs = (
        P(None, None, ALL),
        P(None, GRP),
        P(ALL, None),
        P(GRP, DEV),
        P(GRP, DEV),
    )
    return jax.shard_map(body, mesh=fine, in_specs=in_specs, out_specs=out_specs, check_vma=False)
```

```python
import functools
import jax
import jax.numpy as jnp
from jax import lax
from jax.experimental import pallas as pl
from jax.experimental.pallas import tpu as pltpu
from jax.sharding import Mesh, PartitionSpec as P

STEPS = 8
CAP = 8
NODES = 256
TAIL = 8
LANES = 128
COUNT = 64
FEATS = 768
ROWS = 72
ONES_ROW = 24
CODE_ROW = 67
LIMIT = 60 * 1024 * 1024
HIGH = lax.Precision.HIGHEST
F32 = jnp.float32
BF16 = jnp.bfloat16
DEV = ("zl", "x", "core")
CHIP = ("zl", "x")
GRP = ("y", "zh")
ALL = GRP + DEV
PAIRS = [(s, t) for s in range(2, STEPS) for t in range(1, s)]
SWAP = [(0, 1), (1, 0)]
SHIFTS = (1, 3, 2)
SENT = [(flip, d) for flip in (1, 0) for d in SHIFTS + (0,)]
GOT = [(0, 0), (1, 0)] + [(flip, d) for flip in (0, 1) for d in SHIFTS]


def nt(left, right, precision=None):
    return lax.dot_general(
        left, right, (((1,), (1,)), ((), ())), precision=precision, preferred_element_type=F32
    )


def iota(shape, dim):
    return lax.broadcasted_iota(jnp.int32, shape, dim)


def pick_matrix(pick_ref):
    count = pick_ref.shape[1]
    eye = iota((count, count), 0) == iota((count, count), 1)
    pick = jnp.sum(jnp.where(eye, pick_ref[...].astype(F32), 0.0), axis=1, keepdims=True).astype(jnp.int32)
    at = (pick >> 3) + LANES * (pick & 7)
    at = jnp.concatenate([at, at + LANES], axis=0)
    return (iota((2 * count, LANES * (STEPS + 1)), 1) == at).astype(F32).astype(BF16)


def fetch(refs, bufs, sem):
    copies = [pltpu.make_async_copy(r, b, sem.at[i]) for i, (r, b) in enumerate(zip(refs, bufs))]
    for c in copies:
        c.start()
    return copies


def evolve_kernel(
    pos_ref, vel_ref, stiff_ref, contact_ref, off_ref, attach_ref, plat_ref, pick_ref, dest_ref,
    pay_ref, rows_ref, bound_ref, fpos_ref,
    posb, velb, contactb, stiffb, offb, attachb, platb, pickb, destb, stack, lin, sem,
):
    small = fetch(
        (stiff_ref, off_ref, attach_ref, plat_ref, pick_ref, dest_ref),
        (stiffb, offb, attachb, platb, pickb, destb),
        sem.at[0],
    )
    large = fetch(
        (pos_ref, vel_ref) + tuple(contact_ref.at[s] for s in range(STEPS)),
        (posb, velb) + tuple(contactb.at[s] for s in range(STEPS)),
        sem.at[1],
    )
    for c in small:
        c.wait()
    k = stiffb[...]
    onehot = (attachb[...] == iota((LANES, LANES), 0)).astype(F32)
    off = offb[...]
    fair = jnp.dot(platb[...], onehot, precision=HIGH, preferred_element_type=F32) + off
    picks = pick_matrix(pickb)
    row = iota((NODES, LANES), 0)
    first, last, bulk = row == 0, row == NODES - 1, row < NODES - TAIL
    lin[...] = jnp.zeros_like(lin)
    lin[ONES_ROW : ONES_ROW + 1] = jnp.ones((1, LANES), F32)
    large[0].wait()
    large[1].wait()
    pos = [jnp.where(last, fair[c : c + 1], posb[c]) for c in range(3)]
    vel = [velb[c] for c in range(3)]
    for step in range(STEPS):
        large[2 + step].wait()
        touch = contactb[step].astype(F32)
        damp = 0.02 + 0.1 * touch
        for c in range(3):
            p = pos[c]
            stack[c * NODES : (c + 1) * NODES, step * LANES : (step + 1) * LANES] = jnp.where(bulk, p, 0.0).astype(BF16)
            bound_ref[step * 3 + c : step * 3 + c + 1] = p[NODES - TAIL - 1 : NODES - TAIL]
            lin[step * 3 + c : step * 3 + c + 1] = p[NODES - 2 : NODES - 1] - p[NODES - 1 : NODES]
            accel = k * (pltpu.roll(p, NODES - 1, 0) - 2.0 * p + pltpu.roll(p, 1, 0)) - damp * vel[c]
            if c == 2:
                accel = accel + (-0.05 - 0.3 * touch * (p + 2.0))
            vel[c] = vel[c] + accel
            pos[c] = jnp.where(first, p, jnp.where(last, off[c : c + 1], p + vel[c]))
    for c in range(3):
        stack[c * NODES : (c + 1) * NODES, STEPS * LANES :] = jnp.where(bulk, pos[c], 0.0).astype(BF16)
        fpos_ref[c] = pos[c]
    rows_ref[...] = nt(picks, stack[...]).astype(BF16)
    trow = iota((TAIL, LANES), 0)
    zero = jnp.zeros((TAIL, LANES), F32)
    for kind in range(2):
        rp, rv = [zero] * 6, [zero] * 6
        for step in range(1, STEPS):
            for t in range(1, step):
                at = ONES_ROW + 1 + 2 * PAIRS.index((step, t)) + kind
                lin[at : at + 1] = rp[t - 1][TAIL - 2 : TAIL - 1]
            if step == STEPS - 1:
                break
            touch = contactb[step, NODES - TAIL : NODES].astype(F32)
            damp = 0.02 + 0.1 * touch
            for t in range(1, step + 1):
                p = jnp.where(trow == TAIL - 1, 1.0 if t == step else 0.0, rp[t - 1])
                up = pltpu.roll(p, TAIL - 1, 0)
                down = jnp.where(trow == 0, 0.0, pltpu.roll(p, 1, 0))
                accel = k * (up - 2.0 * p + down) - damp * rv[t - 1]
                if kind == 1:
                    accel = accel - 0.3 * touch * p
                rv[t - 1] = rv[t - 1] + accel
                rp[t - 1] = p + rv[t - 1]
    sums = nt(lin[...] * k, onehot, HIGH)
    count = destb.shape[1]
    lane, sub = iota((count, count), 1), iota((count, count), 0)
    dest = destb[...].astype(F32)
    dest_col = jnp.sum(jnp.where(lane == sub, dest, 0.0), axis=1, keepdims=True)
    rank = jnp.sum(jnp.where((dest_col == dest) & (sub < lane), 1.0, 0.0), axis=0, keepdims=True)
    codes = jnp.concatenate([dest * CAP + rank, jnp.full((1, LANES - count), -1.0, F32)], axis=1)
    pay_ref[...] = jnp.where(iota((ROWS, LANES), 0) == CODE_ROW + lax.axis_index("core"), codes, sums)


def finish_kernel(
    recv_ref, bound_ref, rows_ref, plat_ref, plat_vel_ref, inv_ref, rest_ref, kern_ref, hist_ref, wave_ref,
    pos_ref, vel_ref, contact_ref, stiff_ref, off_ref, attach_ref, pick_ref, w_in_ref, fpos_in,
    x_ref, t_ref, h_ref, plat_out, fpos_ref,
    recvb, boundb, rowsb, platb, plat_velb, invb, restb, kernb, histb, waveb,
    posb, velb, contactb, stiffb, offb, attachb, pickb, w_inb, tails, final, sem, out_sem,
):
    at = pl.ds(NODES - TAIL, TAIL)
    copies = fetch(
        (
            recv_ref, plat_ref, plat_vel_ref, inv_ref, rest_ref, kern_ref, hist_ref, wave_ref,
            stiff_ref, off_ref, attach_ref, pick_ref, bound_ref, rows_ref,
            pos_ref.at[:, at, :], vel_ref.at[:, at, :], contact_ref.at[:, at, :], w_in_ref,
        ),
        (
            recvb, platb, plat_velb, invb, restb, kernb, histb, waveb,
            stiffb, offb, attachb, pickb, boundb, rowsb, posb, velb, contactb, w_inb,
        ),
        sem,
    )
    for c in copies[:-1]:
        c.wait()
    total = recvb[0]
    for d in range(1, recvb.shape[0]):
        total = total + recvb[d]
    q, u = platb[...], plat_velb[...]
    hist = [histb[:, m] for m in range(STEPS)]
    kern = [kernb[:, m] for m in range(STEPS)]
    ones = total[ONES_ROW : ONES_ROW + 1]
    qs = [q]
    for step in range(STEPS):
        force = total[3 * step : 3 * step + 3]
        if step > 0:
            force = force - ones * q
        for t in range(1, step):
            at = ONES_ROW + 1 + 2 * PAIRS.index((step, t))
            coef = jnp.concatenate([total[at : at + 1], total[at : at + 2]], axis=0)
            force = force + coef * qs[t]
        memory = kern[0] * hist[0]
        for m in range(1, STEPS):
            memory = memory + kern[m] * hist[m]
        u = u + invb[...] * (force - restb[...] * q - memory + waveb[:, step])
        q = q + u
        hist = [u] + hist[:-1]
        qs.append(q)
    plat_out[...] = q
    k = stiffb[...]
    onehot = (attachb[...] == iota((LANES, LANES), 0)).astype(F32)
    fair = jnp.dot(jnp.concatenate(qs, axis=0), onehot, precision=HIGH, preferred_element_type=F32)
    trow = iota((TAIL, LANES), 0)
    pos = [posb[c] for c in range(3)]
    vel = [velb[c] for c in range(3)]
    for step in range(STEPS + 1):
        for c in range(3):
            here = fair[step * 3 + c : step * 3 + c + 1] + offb[c : c + 1]
            p = jnp.where(trow == TAIL - 1, here, pos[c])
            tails[c * TAIL : (c + 1) * TAIL, step * LANES : (step + 1) * LANES] = p
            if step == STEPS:
                final[c] = p
                continue
            touch = contactb[step].astype(F32)
            up = pltpu.roll(p, TAIL - 1, 0)
            bound = boundb[step * 3 + c : step * 3 + c + 1]
            down = jnp.where(trow == 0, bound, pltpu.roll(p, 1, 0))
            accel = k * (up - 2.0 * p + down) - (0.02 + 0.1 * touch) * vel[c]
            if c == 2:
                accel = accel + (-0.05 - 0.3 * touch * (p + 2.0))
            vel[c] = vel[c] + accel
            pos[c] = p + vel[c]
    copy = pltpu.make_async_copy(final, fpos_ref.at[:, NODES - TAIL : NODES, :], out_sem)
    copy.start()
    picked = nt(pick_matrix(pickb), tails[...].astype(BF16)).astype(BF16)
    at = iota((3 * TAIL, FEATS), 0)
    where = (at // TAIL) * NODES + (NODES - TAIL) + at % TAIL
    place = (iota((3 * TAIL, FEATS), 1) == where).astype(F32).astype(BF16)
    rows = rowsb[...].astype(F32) + jnp.dot(picked, place, preferred_element_type=F32)
    count = t_ref.shape[0]
    t_ref[...] = rows[count:].astype(BF16)
    copies[-1].wait()
    hidden = jnp.dot(rows[:count].astype(BF16), w_inb[...], preferred_element_type=F32).astype(BF16)
    h_ref[...] = hidden
    wide = hidden.astype(F32)
    scale = lax.rsqrt(jnp.mean(wide * wide, axis=1, keepdims=True) + 1e-06)
    scaled = (rows[:count] * scale).astype(BF16)
    for d in range(x_ref.shape[0]):
        x_ref[d] = scaled
    copy.wait()


def products_kernel(w_in_ref, gain_ref, gate_ref, up_ref, g_ref, u_ref, w_inb, gainb, gateb, upb, scaled, sem):
    copies = fetch((gain_ref, w_in_ref, gate_ref, up_ref), (gainb, w_inb, gateb, upb), sem)
    copies[0].wait()
    copies[1].wait()
    rows = 256
    for i in range(w_inb.shape[0] // rows):
        at = pl.ds(i * rows, rows)
        scaled[at] = (w_inb[at].astype(F32) * gainb[...]).astype(BF16)
        if i == 0:
            copies[2].wait()
        g_ref[at] = dot(scaled[at], gateb[...]).astype(BF16)
        if i == 0:
            copies[3].wait()
        u_ref[at] = dot(scaled[at], upb[...]).astype(BF16)


def down_kernel(w0_ref, w1_ref, out_ref, d0_ref, d1_ref, w0b, w1b, outb, sem):
    copies = fetch((out_ref, w0_ref, w1_ref), (outb, w0b, w1b), sem)
    copies[0].wait()
    tall = 256
    for copy, w, d_ref in ((copies[1], w0b, d0_ref), (copies[2], w1b, d1_ref)):
        copy.wait()
        for i in range(w.shape[0] // tall):
            at = pl.ds(i * tall, tall)
            d_ref[at] = dot(w[at], outb[...]).astype(BF16)


def forward_kernel(
    x_ref, g0_ref, u0_ref, d0_ref, g1_ref, u1_ref, d1_ref, part_ref, gate_ref, up_ref,
    xb, g0b, u0b, d0b, g1b, u1b, d1b, gateb, upb, sem, out_sem,
):
    copies = fetch(
        (x_ref, g0_ref, u0_ref, d0_ref, g1_ref, u1_ref, d1_ref), (xb, g0b, u0b, d0b, g1b, u1b, d1b), sem
    )
    copies[0].wait()
    x = xb[...].reshape(-1, xb.shape[-1])
    part, outs = None, []
    for side, (g, u, d) in enumerate(((g0b, u0b, d0b), (g1b, u1b, d1b))):
        copies[1 + 3 * side].wait()
        gate = dot(x, g[...])
        gateb[side] = gate
        copies[2 + 3 * side].wait()
        upper = dot(x, u[...])
        upb[side] = upper
        for i, (buf, ref) in enumerate(((gateb, gate_ref), (upb, up_ref))):
            out = pltpu.make_async_copy(buf.at[side], ref.at[side], out_sem.at[2 * side + i])
            out.start()
            outs.append(out)
        act = (gate * jax.nn.sigmoid(gate) * upper).astype(BF16)
        copies[3 + 3 * side].wait()
        term = dot(act, d[...])
        part = term if part is None else part + term
    part_ref[...] = part.astype(BF16).reshape(part_ref.shape)
    for out in outs:
        out.wait()


def slopes_kernel(gate_ref, up_ref, a0_ref, b0_ref, a1_ref, b1_ref):
    for side, (a_ref, b_ref) in enumerate(((a0_ref, b0_ref), (a1_ref, b1_ref))):
        gate, upper = gate_ref[side], up_ref[side]
        sigma = jax.nn.sigmoid(gate)
        a_ref[...] = (upper * sigma * (1.0 + gate * (1.0 - sigma))).astype(BF16)
        b_ref[...] = (gate * sigma).astype(BF16)


def error_kernel(parts_ref, base_ref, err_ref):
    total = base_ref[...]
    for d in range(parts_ref.shape[0]):
        total = total + parts_ref[d].astype(F32)
    err_ref[...] = total.astype(BF16)


def chip_block(flip, shift):
    zl, x = lax.axis_index("zl"), lax.axis_index("x")
    zl = 1 - zl if flip else zl
    return zl * 4 + lax.rem(x + shift + 4, 4)


def place(pieces, errb, sem):
    return fetch(pieces, [errb.at[chip_block(flip, -d)] for flip, d in GOT], sem)


def hidden_grads(pieces, copies, err_buf, down_buf, a_buf, b_buf, err_ref, err_sem):
    for c in pieces:
        c.wait()
    out = pltpu.make_async_copy(err_buf, err_ref, err_sem.at[0])
    out.start()
    dpred = (err_buf[...].astype(F32) / 64.0).astype(BF16).reshape(-1, err_buf.shape[-1])
    copies[0].wait()
    dact = nt(dpred, down_buf[...])
    copies[1].wait()
    dgate = (dact * a_buf[...].astype(F32)).astype(BF16)
    copies[2].wait()
    return dgate, (dact * b_buf[...].astype(F32)).astype(BF16), out


def own_kernel(*refs):
    pieces, refs = refs[: len(GOT)], refs[len(GOT) :]
    d_ref, a_ref, b_ref, dg_ref, du_ref, err_ref, errb, db, ab, bb, sem, piece_sem, err_sem = refs
    placed = place(pieces, errb, piece_sem)
    copies = fetch((d_ref, a_ref, b_ref), (db, ab, bb), sem)
    dg_ref[...], du_ref[...], out = hidden_grads(placed, copies, errb, db, ab, bb, err_ref, err_sem)
    out.wait()


def group_block(flip, shift):
    y, zh = lax.axis_index("y"), lax.axis_index("zh")
    zh = 1 - zh if flip else zh
    return lax.rem(y + shift + 4, 4) * 2 + zh


def other_kernel(*refs):
    pieces, refs = refs[: len(GOT)], refs[len(GOT) :]
    (d_ref, a_ref, b_ref, x0_ref, dg_ref, du_ref, x1_ref), refs = refs[:7], refs[7:]
    outs, refs = refs[: len(SENT)], refs[len(SENT) :]
    err_ref, errb, db, ab, bb, x0b, dgb, dub, x1b, yb, sem, piece_sem, out_sem, err_sem = refs
    placed = place(pieces, errb, piece_sem)
    copies = fetch(
        (d_ref, a_ref, b_ref, x0_ref, dg_ref, du_ref, x1_ref), (db, ab, bb, x0b, dgb, dub, x1b), sem
    )
    dgate, dup, err_out = hidden_grads(placed, copies, errb, db, ab, bb, err_ref, err_sem)
    for c in copies[3:]:
        c.wait()
    width, tall = dgate.shape[1], 256
    for i in range(yb.shape[0] // tall):
        at = pl.ds(i * tall, tall)
        yb[at, :width] = (dot(x0b[at], dgb[...]) + dot(x1b[at], dgate)).astype(BF16)
        yb[at, width:] = (dot(x0b[at], dub[...]) + dot(x1b[at], dup)).astype(BF16)
    rows, sends = outs[0].shape[0], []
    for i, (flip, d) in enumerate(SENT):
        at = pl.ds(pl.multiple_of(group_block(flip, d) * rows, rows), rows)
        sends.append(pltpu.make_async_copy(yb.at[at], outs[i], out_sem.at[i]))
        sends[-1].start()
    for c in sends:
        c.wait()
    err_out.wait()


def last_kernel(w_ref, *refs):
    count = len(GOT)
    rows = refs[0].shape[0]
    blocks = [pl.ds(pl.multiple_of(group_block(flip, -d) * rows, rows), rows) for flip, d in GOT]
    w = jnp.concatenate([w_ref[b] for b in blocks], axis=0)
    for side, out_ref in enumerate(refs[2 * count :]):
        y = jnp.concatenate([r[...] for r in refs[side * count : (side + 1) * count]], axis=0)
        out_ref[...] = tn(w, y)


VM = pl.BlockSpec(memory_space=pltpu.VMEM)
HB = pl.BlockSpec(memory_space=pl.ANY)


def vmem_like(a, tail=False):
    shape = (a.shape[0], TAIL, LANES) if tail else a.shape
    return pltpu.VMEM(shape, a.dtype)


def evolve(line_pos, line_vel, stiff, contact, offset, attach, plat_pos, pick, dest):
    sds = jax.ShapeDtypeStruct
    large = (line_pos, line_vel, contact)
    small = (stiff, offset, attach, plat_pos, pick, dest)
    return pl.pallas_call(
        evolve_kernel,
        out_shape=(
            sds((ROWS, LANES), F32),
            sds((2 * COUNT, FEATS), BF16),
            sds((3 * STEPS, LANES), F32),
            sds((3, NODES, LANES), F32),
        ),
        in_specs=[HB] * 9,
        out_specs=(VM,) * 4,
        scratch_shapes=[vmem_like(a) for a in large + small]
        + [
            pltpu.VMEM((3 * NODES, LANES * (STEPS + 1)), BF16),
            pltpu.VMEM((ROWS, LANES), F32),
            pltpu.SemaphoreType.DMA((2, 2 + STEPS)),
        ],
        compiler_params=pltpu.CompilerParams(vmem_limit_bytes=LIMIT),
        cost_estimate=pl.CostEstimate(flops=260000000, bytes_accessed=3000000, transcendentals=0),
        name="evolve",
    )(line_pos, line_vel, stiff, contact, offset, attach, plat_pos, pick, dest)


def finish(recv, bound, rows, plats, lines, w_in, fpos):
    sds = jax.ShapeDtypeStruct
    args = (recv, bound, rows, *plats, *lines, w_in)
    at = 3 + len(plats)
    bufs = [vmem_like(a, at <= i < at + 3) for i, a in enumerate(args)]
    out = (
        sds((recv.shape[0], COUNT, FEATS), BF16),
        sds((COUNT, FEATS), BF16),
        sds((COUNT, w_in.shape[1]), BF16),
        sds((3, LANES), F32),
    )
    return pl.pallas_call(
        finish_kernel,
        out_shape=out + (sds(fpos.shape, F32),),
        in_specs=[HB] * (len(args) + 1),
        out_specs=(VM,) * len(out) + (HB,),
        scratch_shapes=bufs
        + [
            pltpu.VMEM((3 * TAIL, LANES * (STEPS + 1)), F32),
            pltpu.VMEM((3, TAIL, LANES), F32),
            pltpu.SemaphoreType.DMA((len(args),)),
            pltpu.SemaphoreType.DMA,
        ],
        input_output_aliases={len(args): len(out)},
        compiler_params=pltpu.CompilerParams(vmem_limit_bytes=LIMIT),
        cost_estimate=pl.CostEstimate(flops=300000000, bytes_accessed=4000000, transcendentals=0),
        name="finish",
    )(*args, fpos)


PARAMS = pltpu.CompilerParams(vmem_limit_bytes=LIMIT)
MIDDLE = pltpu.CompilerParams(vmem_limit_bytes=24 * 1024 * 1024)
SMALL = pltpu.CompilerParams(vmem_limit_bytes=16 * 1024 * 1024)


def staged(kernel, name, args, out_shape, scratch, flops, sems, out_specs=VM, bufs=None, params=PARAMS):
    bufs = [vmem_like(a) for a in args] if bufs is None else bufs
    return pl.pallas_call(
        kernel,
        out_shape=out_shape,
        in_specs=[HB] * len(args),
        out_specs=out_specs,
        scratch_shapes=bufs + scratch + [pltpu.SemaphoreType.DMA((n,)) for n in sems],
        compiler_params=params,
        cost_estimate=pl.CostEstimate(flops=flops, bytes_accessed=8000000, transcendentals=0),
        name=name,
    )(*args)


def cut(shape, parts, offset=0):
    block = shape[:-1] + (shape[-1] // parts,)
    return pl.BlockSpec(block, lambda i: (0,) * (len(shape) - 1) + (i + offset,))


def exchange(x, axes):
    return lax.all_to_all(x, axes, split_axis=0, concat_axis=0, tiled=True)


def dot(left, right):
    return jnp.dot(left, right, preferred_element_type=F32)


def tn(left, right):
    return lax.dot_general(left, right, (((0,), (0,)), ((), ())), preferred_element_type=F32)


def swap(x, axis="core"):
    return lax.ppermute(x, axis, SWAP)


def shift(x, d, axis):
    return lax.ppermute(x, axis, [(i, (i + d) % 4) for i in range(4)])


def gather(x, pair_axis, ring_axis):
    twin = swap(x, pair_axis)
    return [x, twin] + [shift(v, d, ring_axis) for v in (x, twin) for d in SHIFTS]


def total(first, *others):
    out = first.astype(F32)
    for o in others:
        out = out + o.astype(F32)
    return out.astype(BF16)


def after(x, *others):
    return lax.optimization_barrier((x,) + others)[0]


def body(
    line_pos, line_vel, stiffness, contact, offset, attach, plat_pos, plat_vel, inv_mass, restoring,
    kernel, vel_hist, wave, sample_pick, sample_dest, w_in, gain, w_gate, w_up, w_down, w_out,
):
    sds = jax.ShapeDtypeStruct
    chips = lax.axis_size(CHIP)
    groups = lax.axis_size(GRP)
    half = chips * COUNT
    width = w_gate.shape[1]
    stiff, att, pick, dest = stiffness[None], attach[None], sample_pick[None], sample_dest.reshape(1, -1)
    pay, rows, bound, fpos = evolve(
        line_pos, line_vel, stiff, contact, offset, att, plat_pos, pick, dest
    )
    pay = jnp.broadcast_to((pay + swap(pay))[None], (chips,) + pay.shape)
    pay, w_in_late, w_down_late = lax.optimization_barrier((pay, w_in, w_down))
    recv = exchange(pay, CHIP)
    product = sds((FEATS, width), BF16)
    gate_w, up_w = staged(
        products_kernel, "products", (w_in_late, gain[None], w_gate, w_up), (product, product),
        [pltpu.VMEM(w_in.shape, BF16)], 3300000000, (4,), (VM,) * 2,
    )
    gate_o, up_o = swap(gate_w), swap(up_w)
    w_down_o = swap(w_down)
    turned = lambda a: a.transpose(1, 0, 2)
    x_own, target, hidden, final_plat, final_pos = finish(
        recv, bound, rows,
        (plat_pos, plat_vel, inv_mass, restoring, turned(kernel), turned(vel_hist), turned(wave)),
        (line_pos, line_vel, contact, stiff, offset, att, pick),
        w_in, fpos,
    )
    x_own, w_down_late, w_down_o, hidden = lax.optimization_barrier((x_own, w_down_late, w_down_o, hidden))
    x = exchange(x_own, CHIP)
    product = sds((width, FEATS), BF16)
    down_w, down_o = staged(
        down_kernel, "down", (w_down_late, w_down_o, w_out), (product, product), [], 3300000000, (3,), (VM,) * 2
    )
    base = lax.optimization_barrier(dot(hidden, w_out) - target.astype(F32))
    args = (x, gate_w, up_w, down_w, gate_o, up_o, down_o)
    wide = sds((2, half, width), F32)
    part, gate, upper = staged(
        forward_kernel, "forward", args, (sds(x.shape, BF16), wide, wide),
        [pltpu.VMEM(wide.shape, F32)] * 2, 2500000000, (7, 4), (VM, HB, HB),
    )
    part, gate, upper, x_late, w_in_late = lax.optimization_barrier((part, gate, upper, x, w_in_late))
    parts = exchange(part, CHIP)
    slope = sds((half, width), BF16)
    wide_rows = pl.BlockSpec((2, half // 4, width), lambda i: (0, i, 0))
    slope_rows = pl.BlockSpec((half // 4, width), lambda i: (i, 0))
    slope_a, slope_b, slope_ao, slope_bo = pl.pallas_call(
        slopes_kernel, grid=(4,), out_shape=(slope,) * 4, in_specs=[wide_rows] * 2,
        out_specs=(slope_rows,) * 4, compiler_params=PARAMS, name="slopes",
        cost_estimate=pl.CostEstimate(flops=8000000, bytes_accessed=6000000, transcendentals=1000000),
    )(gate, upper)
    slope_ao, slope_bo = swap(slope_ao), swap(slope_bo)
    x_late, slope_a = lax.optimization_barrier((x_late, slope_a))
    x_late = lax.optimization_barrier(x_late.reshape(half, FEATS).T)
    x_other = swap(x_late)
    at = lax.axis_index(GRP)
    block = w_in.shape[1] // groups
    w_own = lax.optimization_barrier(lax.dynamic_slice_in_dim(w_in_late, at * block, block, 1))
    gain_own = lax.dynamic_slice_in_dim(gain, at * block, block, 0)
    w_own = lax.optimization_barrier((w_own.astype(F32) * gain_own).astype(BF16))
    err_own = pl.pallas_call(
        error_kernel, grid=(3,), out_shape=sds(base.shape, BF16),
        in_specs=[cut(parts.shape, 3), cut(base.shape, 3)], out_specs=cut(base.shape, 3),
        compiler_params=SMALL, name="error",
    )(parts, base)
    err_own, slope_ao, slope_bo = lax.optimization_barrier((err_own, slope_ao, slope_bo))
    err = gather(err_own, "zl", "x")
    err_swapped = [swap(v) for v in err]
    rows_err = sds((chips, COUNT, FEATS), BF16)
    args = (down_w, slope_a, slope_b)
    dg, du, err = staged(
        own_kernel, "own", (*err, *args), (slope, slope, rows_err), [], 400000000, (3, len(GOT), 1), (VM, VM, HB),
        bufs=[pltpu.VMEM(rows_err.shape, BF16)] + [vmem_like(v) for v in args], params=MIDDLE,
    )
    piece = sds((FEATS // groups, 2 * width), BF16)
    args = (down_w, slope_ao, slope_bo, x_late, dg, du, x_other)
    *pieces, err_other = staged(
        other_kernel, "other", (*err_swapped, *args), (piece,) * len(SENT) + (rows_err,),
        [pltpu.VMEM((FEATS, 2 * width), BF16)], 2000000000, (7, len(GOT), len(SENT), 1), (HB,) * (len(SENT) + 1),
        bufs=[pltpu.VMEM(rows_err.shape, BF16)] + [vmem_like(v) for v in args], params=MIDDLE,
    )
    moved = [shift(p, d, "y") if d else p for p, (_, d) in zip(pieces, SENT)]
    theirs = swap(total(*moved[:4]), "zh")
    grads = total(*moved[4:], theirs)
    grads, err_late, err_other = lax.optimization_barrier((grads, err, err_other))
    got = gather(grads, "zh", "y")
    grad = sds((block, width), F32)
    grad_gate, grad_up = pl.pallas_call(
        last_kernel, grid=(2,), out_shape=(grad, grad),
        in_specs=[pl.BlockSpec(w_own.shape, lambda i: (0, 0))]
        + [cut(piece.shape, 4)] * len(GOT) + [cut(piece.shape, 4, 2)] * len(GOT),
        out_specs=(cut(grad.shape, 2),) * 2, compiler_params=SMALL, name="last",
    )(w_own, *got, *got)
    err_all = jnp.concatenate([err_late, err_other], axis=0).reshape(2 * half, FEATS)
    core = lax.axis_index("core")
    codes = recv[:, CODE_ROW : CODE_ROW + 2, :COUNT]
    codes = jnp.where(core == 0, codes, codes[:, ::-1]).transpose(1, 0, 2).reshape(1, 2 * half)
    me = lax.axis_index(CHIP) * 2 + core
    number = jnp.arange(2 * half, dtype=jnp.int32)
    source = ((number // COUNT) % chips) * 2 + (number // half + core) % 2
    slot = jnp.arange(2 * chips * CAP, dtype=jnp.int32)[:, None]
    match = (source[None] == slot // CAP) & (codes == (me * CAP + slot % CAP).astype(F32))
    slot_error = dot(match.astype(BF16), err_all).astype(BF16)
    return (final_pos, final_plat, slot_error, grad_gate, grad_up)


def solution(mesh):
    sizes = (4, 2, 2, 4, 2)
    if mesh.devices.shape[0] == 1:
        sizes = (1, 1, 2, 4, 2)
    fine = Mesh(mesh.devices.reshape(sizes), ALL)
    in_specs = (
        P(None, None, ALL),
        P(None, None, ALL),
        P(ALL),
        P(None, None, ALL),
        P(None, ALL),
        P(ALL),
        P(None, GRP),
        P(None, GRP),
        P(None, GRP),
        P(None, GRP),
        P(None, None, GRP),
        P(None, None, GRP),
        P(None, None, GRP),
        P(ALL),
        P(ALL, None),
        P(),
        P(),
        P(None, DEV),
        P(None, DEV),
        P(DEV, None),
        P(),
    )
    out_specs = (
        P(None, None, ALL),
        P(None, GRP),
        P(ALL, None),
        P(GRP, DEV),
        P(GRP, DEV),
    )
    return jax.shard_map(body, mesh=fine, in_specs=in_specs, out_specs=out_specs, check_vma=False)
```

```python
import functools
import jax
import jax.numpy as jnp
from jax import lax
from jax.experimental import pallas as pl
from jax.experimental.pallas import tpu as pltpu
from jax.sharding import Mesh, PartitionSpec as P

STEPS = 8
CAP = 8
NODES = 256
TAIL = 8
LANES = 128
COUNT = 64
FEATS = 768
ROWS = 72
ONES_ROW = 24
CODE_ROW = 67
LIMIT = 60 * 1024 * 1024
HIGH = lax.Precision.HIGHEST
F32 = jnp.float32
BF16 = jnp.bfloat16
DEV = ("zl", "x", "core")
CHIP = ("zl", "x")
GRP = ("y", "zh")
ALL = GRP + DEV
PAIRS = [(s, t) for s in range(2, STEPS) for t in range(1, s)]
SWAP = [(0, 1), (1, 0)]
SHIFTS = (1, 3, 2)
SENT = [(flip, d) for flip in (1, 0) for d in SHIFTS + (0,)]
GOT = [(0, 0), (1, 0)] + [(flip, d) for flip in (0, 1) for d in SHIFTS]


def nt(left, right, precision=None):
    return lax.dot_general(
        left, right, (((1,), (1,)), ((), ())), precision=precision, preferred_element_type=F32
    )


def iota(shape, dim):
    return lax.broadcasted_iota(jnp.int32, shape, dim)


def pick_matrix(pick_ref):
    count = pick_ref.shape[1]
    eye = iota((count, count), 0) == iota((count, count), 1)
    pick = jnp.sum(jnp.where(eye, pick_ref[...].astype(F32), 0.0), axis=1, keepdims=True).astype(jnp.int32)
    at = (pick >> 3) + LANES * (pick & 7)
    at = jnp.concatenate([at, at + LANES], axis=0)
    return (iota((2 * count, LANES * (STEPS + 1)), 1) == at).astype(F32).astype(BF16)


def fetch(refs, bufs, sem):
    copies = [pltpu.make_async_copy(r, b, sem.at[i]) for i, (r, b) in enumerate(zip(refs, bufs))]
    for c in copies:
        c.start()
    return copies


def evolve_kernel(
    pos_ref, vel_ref, stiff_ref, contact_ref, off_ref, attach_ref, plat_ref, pick_ref, dest_ref,
    pay_ref, rows_ref, bound_ref, fpos_ref,
    posb, velb, contactb, stiffb, offb, attachb, platb, pickb, destb, stack, lin, sem,
):
    small = fetch(
        (stiff_ref, off_ref, attach_ref, plat_ref, pick_ref, dest_ref),
        (stiffb, offb, attachb, platb, pickb, destb),
        sem.at[0],
    )
    large = fetch(
        (pos_ref, vel_ref) + tuple(contact_ref.at[s] for s in range(STEPS)),
        (posb, velb) + tuple(contactb.at[s] for s in range(STEPS)),
        sem.at[1],
    )
    for c in small:
        c.wait()
    k = stiffb[...]
    onehot = (attachb[...] == iota((LANES, LANES), 0)).astype(F32)
    off = offb[...]
    fair = jnp.dot(platb[...], onehot, precision=HIGH, preferred_element_type=F32) + off
    picks = pick_matrix(pickb)
    row = iota((NODES, LANES), 0)
    first, last, bulk = row == 0, row == NODES - 1, row < NODES - TAIL
    lin[...] = jnp.zeros_like(lin)
    lin[ONES_ROW : ONES_ROW + 1] = jnp.ones((1, LANES), F32)
    large[0].wait()
    large[1].wait()
    pos = [jnp.where(last, fair[c : c + 1], posb[c]) for c in range(3)]
    vel = [velb[c] for c in range(3)]
    for step in range(STEPS):
        large[2 + step].wait()
        touch = contactb[step].astype(F32)
        damp = 0.02 + 0.1 * touch
        for c in range(3):
            p = pos[c]
            stack[c * NODES : (c + 1) * NODES, step * LANES : (step + 1) * LANES] = jnp.where(bulk, p, 0.0).astype(BF16)
            bound_ref[step * 3 + c : step * 3 + c + 1] = p[NODES - TAIL - 1 : NODES - TAIL]
            lin[step * 3 + c : step * 3 + c + 1] = p[NODES - 2 : NODES - 1] - p[NODES - 1 : NODES]
            accel = k * (pltpu.roll(p, NODES - 1, 0) - 2.0 * p + pltpu.roll(p, 1, 0)) - damp * vel[c]
            if c == 2:
                accel = accel + (-0.05 - 0.3 * touch * (p + 2.0))
            vel[c] = vel[c] + accel
            pos[c] = jnp.where(first, p, jnp.where(last, off[c : c + 1], p + vel[c]))
    for c in range(3):
        stack[c * NODES : (c + 1) * NODES, STEPS * LANES :] = jnp.where(bulk, pos[c], 0.0).astype(BF16)
        fpos_ref[c] = pos[c]
    rows_ref[...] = nt(picks, stack[...]).astype(BF16)
    trow = iota((TAIL, LANES), 0)
    zero = jnp.zeros((TAIL, LANES), F32)
    for kind in range(2):
        rp, rv = [zero] * 6, [zero] * 6
        for step in range(1, STEPS):
            for t in range(1, step):
                at = ONES_ROW + 1 + 2 * PAIRS.index((step, t)) + kind
                lin[at : at + 1] = rp[t - 1][TAIL - 2 : TAIL - 1]
            if step == STEPS - 1:
                break
            touch = contactb[step, NODES - TAIL : NODES].astype(F32)
            damp = 0.02 + 0.1 * touch
            for t in range(1, step + 1):
                p = jnp.where(trow == TAIL - 1, 1.0 if t == step else 0.0, rp[t - 1])
                up = pltpu.roll(p, TAIL - 1, 0)
                down = jnp.where(trow == 0, 0.0, pltpu.roll(p, 1, 0))
                accel = k * (up - 2.0 * p + down) - damp * rv[t - 1]
                if kind == 1:
                    accel = accel - 0.3 * touch * p
                rv[t - 1] = rv[t - 1] + accel
                rp[t - 1] = p + rv[t - 1]
    sums = nt(lin[...] * k, onehot, HIGH)
    count = destb.shape[1]
    lane, sub = iota((count, count), 1), iota((count, count), 0)
    dest = destb[...].astype(F32)
    dest_col = jnp.sum(jnp.where(lane == sub, dest, 0.0), axis=1, keepdims=True)
    rank = jnp.sum(jnp.where((dest_col == dest) & (sub < lane), 1.0, 0.0), axis=0, keepdims=True)
    codes = jnp.concatenate([dest * CAP + rank, jnp.full((1, LANES - count), -1.0, F32)], axis=1)
    pay_ref[...] = jnp.where(iota((ROWS, LANES), 0) == CODE_ROW + lax.axis_index("core"), codes, sums)


def finish_kernel(
    recv_ref, bound_ref, rows_ref, plat_ref, plat_vel_ref, inv_ref, rest_ref, kern_ref, hist_ref, wave_ref,
    pos_ref, vel_ref, contact_ref, stiff_ref, off_ref, attach_ref, pick_ref, w_in_ref, fpos_in,
    x_ref, t_ref, h_ref, plat_out, fpos_ref,
    recvb, boundb, rowsb, platb, plat_velb, invb, restb, kernb, histb, waveb,
    posb, velb, contactb, stiffb, offb, attachb, pickb, w_inb, tails, final, sem, out_sem,
):
    at = pl.ds(NODES - TAIL, TAIL)
    copies = fetch(
        (
            recv_ref, plat_ref, plat_vel_ref, inv_ref, rest_ref, kern_ref, hist_ref, wave_ref,
            stiff_ref, off_ref, attach_ref, pick_ref, bound_ref, rows_ref,
            pos_ref.at[:, at, :], vel_ref.at[:, at, :], contact_ref.at[:, at, :], w_in_ref,
        ),
        (
            recvb, platb, plat_velb, invb, restb, kernb, histb, waveb,
            stiffb, offb, attachb, pickb, boundb, rowsb, posb, velb, contactb, w_inb,
        ),
        sem,
    )
    for c in copies[:-1]:
        c.wait()
    total = recvb[0]
    for d in range(1, recvb.shape[0]):
        total = total + recvb[d]
    q, u = platb[...], plat_velb[...]
    hist = [histb[:, m] for m in range(STEPS)]
    kern = [kernb[:, m] for m in range(STEPS)]
    ones = total[ONES_ROW : ONES_ROW + 1]
    qs = [q]
    for step in range(STEPS):
        force = total[3 * step : 3 * step + 3]
        if step > 0:
            force = force - ones * q
        for t in range(1, step):
            at = ONES_ROW + 1 + 2 * PAIRS.index((step, t))
            coef = jnp.concatenate([total[at : at + 1], total[at : at + 2]], axis=0)
            force = force + coef * qs[t]
        memory = kern[0] * hist[0]
        for m in range(1, STEPS):
            memory = memory + kern[m] * hist[m]
        u = u + invb[...] * (force - restb[...] * q - memory + waveb[:, step])
        q = q + u
        hist = [u] + hist[:-1]
        qs.append(q)
    plat_out[...] = q
    k = stiffb[...]
    onehot = (attachb[...] == iota((LANES, LANES), 0)).astype(F32)
    fair = jnp.dot(jnp.concatenate(qs, axis=0), onehot, precision=HIGH, preferred_element_type=F32)
    trow = iota((TAIL, LANES), 0)
    pos = [posb[c] for c in range(3)]
    vel = [velb[c] for c in range(3)]
    for step in range(STEPS + 1):
        for c in range(3):
            here = fair[step * 3 + c : step * 3 + c + 1] + offb[c : c + 1]
            p = jnp.where(trow == TAIL - 1, here, pos[c])
            tails[c * TAIL : (c + 1) * TAIL, step * LANES : (step + 1) * LANES] = p
            if step == STEPS:
                final[c] = p
                continue
            touch = contactb[step].astype(F32)
            up = pltpu.roll(p, TAIL - 1, 0)
            bound = boundb[step * 3 + c : step * 3 + c + 1]
            down = jnp.where(trow == 0, bound, pltpu.roll(p, 1, 0))
            accel = k * (up - 2.0 * p + down) - (0.02 + 0.1 * touch) * vel[c]
            if c == 2:
                accel = accel + (-0.05 - 0.3 * touch * (p + 2.0))
            vel[c] = vel[c] + accel
            pos[c] = p + vel[c]
    copy = pltpu.make_async_copy(final, fpos_ref.at[:, NODES - TAIL : NODES, :], out_sem)
    copy.start()
    picked = nt(pick_matrix(pickb), tails[...].astype(BF16)).astype(BF16)
    at = iota((3 * TAIL, FEATS), 0)
    where = (at // TAIL) * NODES + (NODES - TAIL) + at % TAIL
    place = (iota((3 * TAIL, FEATS), 1) == where).astype(F32).astype(BF16)
    rows = rowsb[...].astype(F32) + jnp.dot(picked, place, preferred_element_type=F32)
    count = t_ref.shape[0]
    t_ref[...] = rows[count:].astype(BF16)
    copies[-1].wait()
    hidden = jnp.dot(rows[:count].astype(BF16), w_inb[...], preferred_element_type=F32).astype(BF16)
    h_ref[...] = hidden
    wide = hidden.astype(F32)
    scale = lax.rsqrt(jnp.mean(wide * wide, axis=1, keepdims=True) + 1e-06)
    scaled = (rows[:count] * scale).astype(BF16)
    for d in range(x_ref.shape[0]):
        x_ref[d] = scaled
    copy.wait()


def products_kernel(w_in_ref, gain_ref, gate_ref, up_ref, g_ref, u_ref, w_inb, gainb, gateb, upb, scaled, sem):
    copies = fetch((gain_ref, w_in_ref, gate_ref, up_ref), (gainb, w_inb, gateb, upb), sem)
    copies[0].wait()
    copies[1].wait()
    rows = 256
    for i in range(w_inb.shape[0] // rows):
        at = pl.ds(i * rows, rows)
        scaled[at] = (w_inb[at].astype(F32) * gainb[...]).astype(BF16)
        if i == 0:
            copies[2].wait()
        g_ref[at] = dot(scaled[at], gateb[...]).astype(BF16)
        if i == 0:
            copies[3].wait()
        u_ref[at] = dot(scaled[at], upb[...]).astype(BF16)


def down_kernel(w0_ref, w1_ref, out_ref, d0_ref, d1_ref, w0b, w1b, outb, sem):
    copies = fetch((out_ref, w0_ref, w1_ref), (outb, w0b, w1b), sem)
    copies[0].wait()
    tall = 256
    for copy, w, d_ref in ((copies[1], w0b, d0_ref), (copies[2], w1b, d1_ref)):
        copy.wait()
        for i in range(w.shape[0] // tall):
            at = pl.ds(i * tall, tall)
            d_ref[at] = dot(w[at], outb[...]).astype(BF16)


def forward_kernel(
    x_ref, g0_ref, u0_ref, d0_ref, g1_ref, u1_ref, d1_ref, part_ref, gate_ref, up_ref,
    xb, g0b, u0b, d0b, g1b, u1b, d1b, gateb, upb, sem, out_sem,
):
    copies = fetch(
        (x_ref, g0_ref, u0_ref, d0_ref, g1_ref, u1_ref, d1_ref), (xb, g0b, u0b, d0b, g1b, u1b, d1b), sem
    )
    copies[0].wait()
    x = xb[...].reshape(-1, xb.shape[-1])
    part, outs = None, []
    for side, (g, u, d) in enumerate(((g0b, u0b, d0b), (g1b, u1b, d1b))):
        copies[1 + 3 * side].wait()
        gate = dot(x, g[...])
        gateb[side] = gate
        copies[2 + 3 * side].wait()
        upper = dot(x, u[...])
        upb[side] = upper
        for i, (buf, ref) in enumerate(((gateb, gate_ref), (upb, up_ref))):
            out = pltpu.make_async_copy(buf.at[side], ref.at[side], out_sem.at[2 * side + i])
            out.start()
            outs.append(out)
        act = (gate * jax.nn.sigmoid(gate) * upper).astype(BF16)
        copies[3 + 3 * side].wait()
        term = dot(act, d[...])
        part = term if part is None else part + term
    part_ref[...] = part.astype(BF16).reshape(part_ref.shape)
    for out in outs:
        out.wait()


def slopes_kernel(gate_ref, up_ref, a0_ref, b0_ref, a1_ref, b1_ref):
    for side, (a_ref, b_ref) in enumerate(((a0_ref, b0_ref), (a1_ref, b1_ref))):
        gate, upper = gate_ref[side], up_ref[side]
        sigma = jax.nn.sigmoid(gate)
        a_ref[...] = (upper * sigma * (1.0 + gate * (1.0 - sigma))).astype(BF16)
        b_ref[...] = (gate * sigma).astype(BF16)


def error_kernel(parts_ref, base_ref, err_ref):
    total = base_ref[...]
    for d in range(parts_ref.shape[0]):
        total = total + parts_ref[d].astype(F32)
    total = total.astype(BF16)
    for d in range(err_ref.shape[0]):
        err_ref[d] = total


def hidden_grads(err_buf, down_buf, a_buf, b_buf, copies):
    copies[0].wait()
    dpred = (err_buf[...].astype(F32) / 64.0).astype(BF16).reshape(-1, err_buf.shape[-1])
    copies[1].wait()
    dact = nt(dpred, down_buf[...])
    copies[2].wait()
    dgate = (dact * a_buf[...].astype(F32)).astype(BF16)
    copies[3].wait()
    return dgate, (dact * b_buf[...].astype(F32)).astype(BF16)


def own_kernel(err_ref, d_ref, a_ref, b_ref, dg_ref, du_ref, errb, db, ab, bb, sem):
    copies = fetch((err_ref, d_ref, a_ref, b_ref), (errb, db, ab, bb), sem)
    dg_ref[...], du_ref[...] = hidden_grads(errb, db, ab, bb, copies)


def group_block(flip, shift):
    y, zh = lax.axis_index("y"), lax.axis_index("zh")
    zh = 1 - zh if flip else zh
    return lax.rem(y + shift + 4, 4) * 2 + zh


def other_kernel(err_ref, d_ref, a_ref, b_ref, x0_ref, dg_ref, du_ref, x1_ref, *refs):
    outs, (errb, db, ab, bb, x0b, dgb, dub, x1b, yb, sem, out_sem) = refs[: len(SENT)], refs[len(SENT) :]
    copies = fetch(
        (err_ref, d_ref, a_ref, b_ref, x0_ref, dg_ref, du_ref, x1_ref),
        (errb, db, ab, bb, x0b, dgb, dub, x1b),
        sem,
    )
    dgate, dup = hidden_grads(errb, db, ab, bb, copies)
    for c in copies[4:]:
        c.wait()
    width, rows = dgate.shape[1], outs[0].shape[0]
    y, zh = lax.axis_index("y"), lax.axis_index("zh")
    sends = []
    for i, d in enumerate(SHIFTS + (0,)):
        at = pl.ds(pl.multiple_of(lax.rem(y + d, 4) * (2 * rows), 2 * rows), 2 * rows)
        slot = pl.ds(i * 2 * rows, 2 * rows)
        left, right = x0b[at], x1b[at]
        yb[slot, :width] = (dot(left, dgb[...]) + dot(right, dgate)).astype(BF16)
        yb[slot, width:] = (dot(left, dub[...]) + dot(right, dup)).astype(BF16)
        for flip in (1, 0):
            at = pl.ds(pl.multiple_of(i * 2 * rows + (1 - zh if flip else zh) * rows, rows), rows)
            j = SENT.index((flip, d))
            sends.append(pltpu.make_async_copy(yb.at[at], outs[j], out_sem.at[j]))
            sends[-1].start()
    for c in sends:
        c.wait()


def last_kernel(w_ref, *refs):
    count = len(GOT)
    rows = refs[0].shape[0]
    blocks = [pl.ds(pl.multiple_of(group_block(flip, -d) * rows, rows), rows) for flip, d in GOT]
    w = jnp.concatenate([w_ref[b] for b in blocks], axis=0)
    for side, out_ref in enumerate(refs[2 * count :]):
        y = jnp.concatenate([r[...] for r in refs[side * count : (side + 1) * count]], axis=0)
        out_ref[...] = tn(w, y)


VM = pl.BlockSpec(memory_space=pltpu.VMEM)
HB = pl.BlockSpec(memory_space=pl.ANY)


def vmem_like(a, tail=False):
    shape = (a.shape[0], TAIL, LANES) if tail else a.shape
    return pltpu.VMEM(shape, a.dtype)


def evolve(line_pos, line_vel, stiff, contact, offset, attach, plat_pos, pick, dest):
    sds = jax.ShapeDtypeStruct
    large = (line_pos, line_vel, contact)
    small = (stiff, offset, attach, plat_pos, pick, dest)
    return pl.pallas_call(
        evolve_kernel,
        out_shape=(
            sds((ROWS, LANES), F32),
            sds((2 * COUNT, FEATS), BF16),
            sds((3 * STEPS, LANES), F32),
            sds((3, NODES, LANES), F32),
        ),
        in_specs=[HB] * 9,
        out_specs=(VM,) * 4,
        scratch_shapes=[vmem_like(a) for a in large + small]
        + [
            pltpu.VMEM((3 * NODES, LANES * (STEPS + 1)), BF16),
            pltpu.VMEM((ROWS, LANES), F32),
            pltpu.SemaphoreType.DMA((2, 2 + STEPS)),
        ],
        compiler_params=pltpu.CompilerParams(vmem_limit_bytes=LIMIT),
        cost_estimate=pl.CostEstimate(flops=260000000, bytes_accessed=3000000, transcendentals=0),
        name="evolve",
    )(line_pos, line_vel, stiff, contact, offset, attach, plat_pos, pick, dest)


def finish(recv, bound, rows, plats, lines, w_in, fpos):
    sds = jax.ShapeDtypeStruct
    args = (recv, bound, rows, *plats, *lines, w_in)
    at = 3 + len(plats)
    bufs = [vmem_like(a, at <= i < at + 3) for i, a in enumerate(args)]
    out = (
        sds((recv.shape[0], COUNT, FEATS), BF16),
        sds((COUNT, FEATS), BF16),
        sds((COUNT, w_in.shape[1]), BF16),
        sds((3, LANES), F32),
    )
    return pl.pallas_call(
        finish_kernel,
        out_shape=out + (sds(fpos.shape, F32),),
        in_specs=[HB] * (len(args) + 1),
        out_specs=(VM,) * len(out) + (HB,),
        scratch_shapes=bufs
        + [
            pltpu.VMEM((3 * TAIL, LANES * (STEPS + 1)), F32),
            pltpu.VMEM((3, TAIL, LANES), F32),
            pltpu.SemaphoreType.DMA((len(args),)),
            pltpu.SemaphoreType.DMA,
        ],
        input_output_aliases={len(args): len(out)},
        compiler_params=pltpu.CompilerParams(vmem_limit_bytes=LIMIT),
        cost_estimate=pl.CostEstimate(flops=300000000, bytes_accessed=4000000, transcendentals=0),
        name="finish",
    )(*args, fpos)


PARAMS = pltpu.CompilerParams(vmem_limit_bytes=LIMIT)
MIDDLE = pltpu.CompilerParams(vmem_limit_bytes=24 * 1024 * 1024)
SMALL = pltpu.CompilerParams(vmem_limit_bytes=16 * 1024 * 1024)


def staged(kernel, name, args, out_shape, scratch, flops, sems, out_specs=VM, bufs=None, params=PARAMS):
    bufs = [vmem_like(a) for a in args] if bufs is None else bufs
    return pl.pallas_call(
        kernel,
        out_shape=out_shape,
        in_specs=[HB] * len(args),
        out_specs=out_specs,
        scratch_shapes=bufs + scratch + [pltpu.SemaphoreType.DMA((n,)) for n in sems],
        compiler_params=params,
        cost_estimate=pl.CostEstimate(flops=flops, bytes_accessed=8000000, transcendentals=0),
        name=name,
    )(*args)


def cut(shape, parts, offset=0):
    block = shape[:-1] + (shape[-1] // parts,)
    return pl.BlockSpec(block, lambda i: (0,) * (len(shape) - 1) + (i + offset,))


def exchange(x, axes):
    return lax.all_to_all(x, axes, split_axis=0, concat_axis=0, tiled=True)


def dot(left, right):
    return jnp.dot(left, right, preferred_element_type=F32)


def tn(left, right):
    return lax.dot_general(left, right, (((0,), (0,)), ((), ())), preferred_element_type=F32)


def swap(x, axis="core"):
    return lax.ppermute(x, axis, SWAP)


def shift(x, d):
    return lax.ppermute(x, "y", [(i, (i + d) % 4) for i in range(4)])


def total(first, *others):
    out = first.astype(F32)
    for o in others:
        out = out + o.astype(F32)
    return out.astype(BF16)


def after(x, *others):
    return lax.optimization_barrier((x,) + others)[0]


def body(
    line_pos, line_vel, stiffness, contact, offset, attach, plat_pos, plat_vel, inv_mass, restoring,
    kernel, vel_hist, wave, sample_pick, sample_dest, w_in, gain, w_gate, w_up, w_down, w_out,
):
    sds = jax.ShapeDtypeStruct
    chips = lax.axis_size(CHIP)
    groups = lax.axis_size(GRP)
    half = chips * COUNT
    width = w_gate.shape[1]
    stiff, att, pick, dest = stiffness[None], attach[None], sample_pick[None], sample_dest.reshape(1, -1)
    pay, rows, bound, fpos = evolve(
        line_pos, line_vel, stiff, contact, offset, att, plat_pos, pick, dest
    )
    pay = jnp.broadcast_to((pay + swap(pay))[None], (chips,) + pay.shape)
    pay, w_in_late, w_down_late = lax.optimization_barrier((pay, w_in, w_down))
    recv = exchange(pay, CHIP)
    product = sds((FEATS, width), BF16)
    gate_w, up_w = staged(
        products_kernel, "products", (w_in_late, gain[None], w_gate, w_up), (product, product),
        [pltpu.VMEM(w_in.shape, BF16)], 3300000000, (4,), (VM,) * 2,
    )
    gate_o, up_o = swap(gate_w), swap(up_w)
    w_down_o = swap(w_down)
    turned = lambda a: a.transpose(1, 0, 2)
    x_own, target, hidden, final_plat, final_pos = finish(
        recv, bound, rows,
        (plat_pos, plat_vel, inv_mass, restoring, turned(kernel), turned(vel_hist), turned(wave)),
        (line_pos, line_vel, contact, stiff, offset, att, pick),
        w_in, fpos,
    )
    x_own, w_down_late, w_down_o, hidden = lax.optimization_barrier((x_own, w_down_late, w_down_o, hidden))
    x = exchange(x_own, CHIP)
    product = sds((width, FEATS), BF16)
    down_w, down_o = staged(
        down_kernel, "down", (w_down_late, w_down_o, w_out), (product, product), [], 3300000000, (3,), (VM,) * 2
    )
    base = lax.optimization_barrier(dot(hidden, w_out) - target.astype(F32))
    args = (x, gate_w, up_w, down_w, gate_o, up_o, down_o)
    wide = sds((2, half, width), F32)
    part, gate, upper = staged(
        forward_kernel, "forward", args, (sds(x.shape, BF16), wide, wide),
        [pltpu.VMEM(wide.shape, F32)] * 2, 2500000000, (7, 4), (VM, HB, HB),
    )
    part, gate, upper, x_late, w_in_late = lax.optimization_barrier((part, gate, upper, x, w_in_late))
    parts = exchange(part, CHIP)
    slope = sds((half, width), BF16)
    wide_rows = pl.BlockSpec((2, half // 4, width), lambda i: (0, i, 0))
    slope_rows = pl.BlockSpec((half // 4, width), lambda i: (i, 0))
    slope_a, slope_b, slope_ao, slope_bo = pl.pallas_call(
        slopes_kernel, grid=(4,), out_shape=(slope,) * 4, in_specs=[wide_rows] * 2,
        out_specs=(slope_rows,) * 4, compiler_params=PARAMS, name="slopes",
        cost_estimate=pl.CostEstimate(flops=8000000, bytes_accessed=6000000, transcendentals=1000000),
    )(gate, upper)
    slope_ao, slope_bo = swap(slope_ao), swap(slope_bo)
    x_late, slope_a = lax.optimization_barrier((x_late, slope_a))
    x_late = lax.optimization_barrier(x_late.reshape(half, FEATS).T)
    x_other = swap(x_late)
    err_own = pl.pallas_call(
        error_kernel, grid=(3,), out_shape=sds((chips, COUNT, FEATS), BF16),
        in_specs=[cut(parts.shape, 3), cut(base.shape, 3)], out_specs=cut(parts.shape, 3),
        compiler_params=SMALL, name="error",
    )(parts, base)
    err_own, slope_ao, slope_bo = lax.optimization_barrier((err_own, slope_ao, slope_bo))
    err = exchange(err_own, CHIP)
    err_other = swap(err)
    dg, du = staged(
        own_kernel, "own", (err, down_w, slope_a, slope_b), (slope, slope), [], 400000000, (4,), (VM,) * 2,
    )
    piece = sds((FEATS // groups, 2 * width), BF16)
    pieces = staged(
        other_kernel, "other", (err_other, down_w, slope_ao, slope_bo, x_late, dg, du, x_other),
        (piece,) * len(SENT), [pltpu.VMEM((FEATS, 2 * width), BF16)], 2000000000, (8, len(SENT)),
        (HB,) * len(SENT),
    )
    pieces = list(pieces)
    pieces[0], gain_late, w_in_late = lax.optimization_barrier((pieces[0], gain, w_in_late))
    at = lax.axis_index(GRP)
    block = w_in.shape[1] // groups
    w_own = lax.optimization_barrier(lax.dynamic_slice_in_dim(w_in_late, at * block, block, 1))
    gain_own = lax.dynamic_slice_in_dim(gain_late, at * block, block, 0)
    w_own = lax.optimization_barrier((w_own.astype(F32) * gain_own).astype(BF16))
    moved = [shift(p, d) if d else p for p, (_, d) in zip(pieces, SENT)]
    theirs = swap(total(*moved[:4]), "zh")
    grads = total(*moved[4:], theirs)
    grads, err_late, err_other = lax.optimization_barrier((grads, err, err_other))
    twin = swap(grads, "zh")
    got = [grads, twin] + [shift(v, d) for v in (grads, twin) for d in SHIFTS]
    grad = sds((block, width), F32)
    grad_gate, grad_up = pl.pallas_call(
        last_kernel, grid=(2,), out_shape=(grad, grad),
        in_specs=[pl.BlockSpec(w_own.shape, lambda i: (0, 0))]
        + [cut(piece.shape, 4)] * len(GOT) + [cut(piece.shape, 4, 2)] * len(GOT),
        out_specs=(cut(grad.shape, 2),) * 2, compiler_params=SMALL, name="last",
    )(w_own, *got, *got)
    err_all = jnp.concatenate([err_late, err_other], axis=0).reshape(2 * half, FEATS)
    core = lax.axis_index("core")
    codes = recv[:, CODE_ROW : CODE_ROW + 2, :COUNT]
    codes = jnp.where(core == 0, codes, codes[:, ::-1]).transpose(1, 0, 2).reshape(1, 2 * half)
    me = lax.axis_index(CHIP) * 2 + core
    number = jnp.arange(2 * half, dtype=jnp.int32)
    source = ((number // COUNT) % chips) * 2 + (number // half + core) % 2
    slot = jnp.arange(2 * chips * CAP, dtype=jnp.int32)[:, None]
    match = (source[None] == slot // CAP) & (codes == (me * CAP + slot % CAP).astype(F32))
    slot_error = dot(match.astype(BF16), err_all).astype(BF16)
    return (final_pos, final_plat, slot_error, grad_gate, grad_up)


def solution(mesh):
    sizes = (4, 2, 2, 4, 2)
    if mesh.devices.shape[0] == 1:
        sizes = (1, 1, 2, 4, 2)
    fine = Mesh(mesh.devices.reshape(sizes), ALL)
    in_specs = (
        P(None, None, ALL),
        P(None, None, ALL),
        P(ALL),
        P(None, None, ALL),
        P(None, ALL),
        P(ALL),
        P(None, GRP),
        P(None, GRP),
        P(None, GRP),
        P(None, GRP),
        P(None, None, GRP),
        P(None, None, GRP),
        P(None, None, GRP),
        P(ALL),
        P(ALL, None),
        P(),
        P(),
        P(None, DEV),
        P(None, DEV),
        P(DEV, None),
        P(),
    )
    out_specs = (
        P(None, None, ALL),
        P(None, GRP),
        P(ALL, None),
        P(GRP, DEV),
        P(GRP, DEV),
    )
    return jax.shard_map(body, mesh=fine, in_specs=in_specs, out_specs=out_specs, check_vma=False)
```

```python
import functools
import jax
import jax.numpy as jnp
from jax import lax
from jax.experimental import pallas as pl
from jax.experimental.pallas import tpu as pltpu
from jax.sharding import Mesh, PartitionSpec as P

STEPS = 8
CAP = 8
NODES = 256
TAIL = 8
LANES = 128
COUNT = 64
FEATS = 768
ROWS = 72
ONES_ROW = 24
CODE_ROW = 67
LIMIT = 60 * 1024 * 1024
HIGH = lax.Precision.HIGHEST
F32 = jnp.float32
BF16 = jnp.bfloat16
DEV = ("zl", "x", "core")
CHIP = ("zl", "x")
GRP = ("y", "zh")
ALL = GRP + DEV
PAIRS = [(s, t) for s in range(2, STEPS) for t in range(1, s)]
SWAP = [(0, 1), (1, 0)]
SHIFTS = (1, 3, 2)
SENT = [(flip, d) for flip in (1, 0) for d in SHIFTS + (0,)]
GOT = [(0, 0), (1, 0)] + [(flip, d) for flip in (0, 1) for d in SHIFTS]


def nt(left, right, precision=None):
    return lax.dot_general(
        left, right, (((1,), (1,)), ((), ())), precision=precision, preferred_element_type=F32
    )


def iota(shape, dim):
    return lax.broadcasted_iota(jnp.int32, shape, dim)


def pick_matrix(pick_ref):
    count = pick_ref.shape[1]
    eye = iota((count, count), 0) == iota((count, count), 1)
    pick = jnp.sum(jnp.where(eye, pick_ref[...].astype(F32), 0.0), axis=1, keepdims=True).astype(jnp.int32)
    at = (pick >> 3) + LANES * (pick & 7)
    at = jnp.concatenate([at, at + LANES], axis=0)
    return (iota((2 * count, LANES * (STEPS + 1)), 1) == at).astype(F32).astype(BF16)


def fetch(refs, bufs, sem):
    copies = [pltpu.make_async_copy(r, b, sem.at[i]) for i, (r, b) in enumerate(zip(refs, bufs))]
    for c in copies:
        c.start()
    return copies


def evolve_kernel(
    pos_ref, vel_ref, stiff_ref, contact_ref, off_ref, attach_ref, plat_ref, pick_ref, dest_ref,
    pay_ref, rows_ref, bound_ref, fpos_ref,
    posb, velb, contactb, stiffb, offb, attachb, platb, pickb, destb, stack, lin, sem,
):
    small = fetch(
        (stiff_ref, off_ref, attach_ref, plat_ref, pick_ref, dest_ref),
        (stiffb, offb, attachb, platb, pickb, destb),
        sem.at[0],
    )
    large = fetch(
        (pos_ref, vel_ref) + tuple(contact_ref.at[s] for s in range(STEPS)),
        (posb, velb) + tuple(contactb.at[s] for s in range(STEPS)),
        sem.at[1],
    )
    for c in small:
        c.wait()
    k = stiffb[...]
    onehot = (attachb[...] == iota((LANES, LANES), 0)).astype(F32)
    off = offb[...]
    fair = jnp.dot(platb[...], onehot, precision=HIGH, preferred_element_type=F32) + off
    picks = pick_matrix(pickb)
    row = iota((NODES, LANES), 0)
    first, last, bulk = row == 0, row == NODES - 1, row < NODES - TAIL
    lin[...] = jnp.zeros_like(lin)
    lin[ONES_ROW : ONES_ROW + 1] = jnp.ones((1, LANES), F32)
    large[0].wait()
    large[1].wait()
    pos = [jnp.where(last, fair[c : c + 1], posb[c]) for c in range(3)]
    vel = [velb[c] for c in range(3)]
    for step in range(STEPS):
        large[2 + step].wait()
        touch = contactb[step].astype(F32)
        damp = 0.02 + 0.1 * touch
        for c in range(3):
            p = pos[c]
            stack[c * NODES : (c + 1) * NODES, step * LANES : (step + 1) * LANES] = jnp.where(bulk, p, 0.0).astype(BF16)
            bound_ref[step * 3 + c : step * 3 + c + 1] = p[NODES - TAIL - 1 : NODES - TAIL]
            lin[step * 3 + c : step * 3 + c + 1] = p[NODES - 2 : NODES - 1] - p[NODES - 1 : NODES]
            accel = k * (pltpu.roll(p, NODES - 1, 0) - 2.0 * p + pltpu.roll(p, 1, 0)) - damp * vel[c]
            if c == 2:
                accel = accel + (-0.05 - 0.3 * touch * (p + 2.0))
            vel[c] = vel[c] + accel
            pos[c] = jnp.where(first, p, jnp.where(last, off[c : c + 1], p + vel[c]))
    for c in range(3):
        stack[c * NODES : (c + 1) * NODES, STEPS * LANES :] = jnp.where(bulk, pos[c], 0.0).astype(BF16)
        fpos_ref[c] = pos[c]
    rows_ref[...] = nt(picks, stack[...]).astype(BF16)
    trow = iota((TAIL, LANES), 0)
    zero = jnp.zeros((TAIL, LANES), F32)
    for kind in range(2):
        rp, rv = [zero] * 6, [zero] * 6
        for step in range(1, STEPS):
            for t in range(1, step):
                at = ONES_ROW + 1 + 2 * PAIRS.index((step, t)) + kind
                lin[at : at + 1] = rp[t - 1][TAIL - 2 : TAIL - 1]
            if step == STEPS - 1:
                break
            touch = contactb[step, NODES - TAIL : NODES].astype(F32)
            damp = 0.02 + 0.1 * touch
            for t in range(1, step + 1):
                p = jnp.where(trow == TAIL - 1, 1.0 if t == step else 0.0, rp[t - 1])
                up = pltpu.roll(p, TAIL - 1, 0)
                down = jnp.where(trow == 0, 0.0, pltpu.roll(p, 1, 0))
                accel = k * (up - 2.0 * p + down) - damp * rv[t - 1]
                if kind == 1:
                    accel = accel - 0.3 * touch * p
                rv[t - 1] = rv[t - 1] + accel
                rp[t - 1] = p + rv[t - 1]
    sums = nt(lin[...] * k, onehot, HIGH)
    count = destb.shape[1]
    lane, sub = iota((count, count), 1), iota((count, count), 0)
    dest = destb[...].astype(F32)
    dest_col = jnp.sum(jnp.where(lane == sub, dest, 0.0), axis=1, keepdims=True)
    rank = jnp.sum(jnp.where((dest_col == dest) & (sub < lane), 1.0, 0.0), axis=0, keepdims=True)
    codes = jnp.concatenate([dest * CAP + rank, jnp.full((1, LANES - count), -1.0, F32)], axis=1)
    pay_ref[...] = jnp.where(iota((ROWS, LANES), 0) == CODE_ROW + lax.axis_index("core"), codes, sums)


def finish_kernel(
    recv_ref, bound_ref, rows_ref, plat_ref, plat_vel_ref, inv_ref, rest_ref, kern_ref, hist_ref, wave_ref,
    pos_ref, vel_ref, contact_ref, stiff_ref, off_ref, attach_ref, pick_ref, w_in_ref, fpos_in,
    x_ref, t_ref, h_ref, plat_out, fpos_ref,
    recvb, boundb, rowsb, platb, plat_velb, invb, restb, kernb, histb, waveb,
    posb, velb, contactb, stiffb, offb, attachb, pickb, w_inb, tails, final, sem, out_sem,
):
    at = pl.ds(NODES - TAIL, TAIL)
    copies = fetch(
        (
            recv_ref, plat_ref, plat_vel_ref, inv_ref, rest_ref, kern_ref, hist_ref, wave_ref,
            stiff_ref, off_ref, attach_ref, pick_ref, bound_ref, rows_ref,
            pos_ref.at[:, at, :], vel_ref.at[:, at, :], contact_ref.at[:, at, :], w_in_ref,
        ),
        (
            recvb, platb, plat_velb, invb, restb, kernb, histb, waveb,
            stiffb, offb, attachb, pickb, boundb, rowsb, posb, velb, contactb, w_inb,
        ),
        sem,
    )
    copies[10].wait()
    copies[11].wait()
    picks = pick_matrix(pickb)
    onehot = (attachb[...] == iota((LANES, LANES), 0)).astype(F32)
    at = iota((3 * TAIL, FEATS), 0)
    where = (at // TAIL) * NODES + (NODES - TAIL) + at % TAIL
    place = (iota((3 * TAIL, FEATS), 1) == where).astype(F32).astype(BF16)
    for c in copies[:10] + copies[12:-1]:
        c.wait()
    total = recvb[0]
    for d in range(1, recvb.shape[0]):
        total = total + recvb[d]
    q, u = platb[...], plat_velb[...]
    hist = [histb[:, m] for m in range(STEPS)]
    kern = [kernb[:, m] for m in range(STEPS)]
    ones = total[ONES_ROW : ONES_ROW + 1]
    qs = [q]
    for step in range(STEPS):
        force = total[3 * step : 3 * step + 3]
        if step > 0:
            force = force - ones * q
        for t in range(1, step):
            at = ONES_ROW + 1 + 2 * PAIRS.index((step, t))
            coef = jnp.concatenate([total[at : at + 1], total[at : at + 2]], axis=0)
            force = force + coef * qs[t]
        memory = kern[0] * hist[0]
        for m in range(1, STEPS):
            memory = memory + kern[m] * hist[m]
        u = u + invb[...] * (force - restb[...] * q - memory + waveb[:, step])
        q = q + u
        hist = [u] + hist[:-1]
        qs.append(q)
    plat_out[...] = q
    k = stiffb[...]
    fair = jnp.dot(jnp.concatenate(qs, axis=0), onehot, precision=HIGH, preferred_element_type=F32)
    trow = iota((TAIL, LANES), 0)
    pos = [posb[c] for c in range(3)]
    vel = [velb[c] for c in range(3)]
    for step in range(STEPS + 1):
        for c in range(3):
            here = fair[step * 3 + c : step * 3 + c + 1] + offb[c : c + 1]
            p = jnp.where(trow == TAIL - 1, here, pos[c])
            tails[c * TAIL : (c + 1) * TAIL, step * LANES : (step + 1) * LANES] = p
            if step == STEPS:
                final[c] = p
                continue
            touch = contactb[step].astype(F32)
            up = pltpu.roll(p, TAIL - 1, 0)
            bound = boundb[step * 3 + c : step * 3 + c + 1]
            down = jnp.where(trow == 0, bound, pltpu.roll(p, 1, 0))
            accel = k * (up - 2.0 * p + down) - (0.02 + 0.1 * touch) * vel[c]
            if c == 2:
                accel = accel + (-0.05 - 0.3 * touch * (p + 2.0))
            vel[c] = vel[c] + accel
            pos[c] = p + vel[c]
    copy = pltpu.make_async_copy(final, fpos_ref.at[:, NODES - TAIL : NODES, :], out_sem)
    copy.start()
    picked = nt(picks, tails[...].astype(BF16)).astype(BF16)
    rows = rowsb[...].astype(F32) + jnp.dot(picked, place, preferred_element_type=F32)
    count = t_ref.shape[0]
    t_ref[...] = rows[count:].astype(BF16)
    copies[-1].wait()
    hidden = jnp.dot(rows[:count].astype(BF16), w_inb[...], preferred_element_type=F32).astype(BF16)
    h_ref[...] = hidden
    wide = hidden.astype(F32)
    scale = lax.rsqrt(jnp.mean(wide * wide, axis=1, keepdims=True) + 1e-06)
    scaled = (rows[:count] * scale).astype(BF16)
    for d in range(x_ref.shape[0]):
        x_ref[d] = scaled
    copy.wait()


def products_kernel(w_in_ref, gain_ref, gate_ref, up_ref, g_ref, u_ref, w_inb, gainb, gateb, upb, scaled, sem):
    copies = fetch((gain_ref, w_in_ref, gate_ref, up_ref), (gainb, w_inb, gateb, upb), sem)
    copies[0].wait()
    copies[1].wait()
    rows = 256
    for i in range(w_inb.shape[0] // rows):
        at = pl.ds(i * rows, rows)
        scaled[at] = (w_inb[at].astype(F32) * gainb[...]).astype(BF16)
        if i == 0:
            copies[2].wait()
        g_ref[at] = dot(scaled[at], gateb[...]).astype(BF16)
        if i == 0:
            copies[3].wait()
        u_ref[at] = dot(scaled[at], upb[...]).astype(BF16)


def down_kernel(w0_ref, w1_ref, out_ref, d0_ref, d1_ref, w0b, w1b, outb, sem):
    copies = fetch((out_ref, w0_ref, w1_ref), (outb, w0b, w1b), sem)
    copies[0].wait()
    tall = 256
    for copy, w, d_ref in ((copies[1], w0b, d0_ref), (copies[2], w1b, d1_ref)):
        copy.wait()
        for i in range(w.shape[0] // tall):
            at = pl.ds(i * tall, tall)
            d_ref[at] = dot(w[at], outb[...]).astype(BF16)


def forward_kernel(
    x_ref, g0_ref, u0_ref, d0_ref, g1_ref, u1_ref, d1_ref, part_ref, gate_ref, up_ref,
    xb, g0b, u0b, d0b, g1b, u1b, d1b, gateb, upb, sem, out_sem,
):
    copies = fetch(
        (x_ref, g0_ref, u0_ref, d0_ref, g1_ref, u1_ref, d1_ref), (xb, g0b, u0b, d0b, g1b, u1b, d1b), sem
    )
    copies[0].wait()
    x = xb[...].reshape(-1, xb.shape[-1])
    outs = []

    def keep(side):
        for i, (buf, ref) in enumerate(((gateb, gate_ref), (upb, up_ref))):
            out = pltpu.make_async_copy(buf.at[side], ref.at[side], out_sem.at[2 * side + i])
            out.start()
            outs.append(out)

    copies[1].wait()
    gate0 = dot(x, g0b[...])
    gateb[0] = gate0
    copies[2].wait()
    up0 = dot(x, u0b[...])
    upb[0] = up0
    keep(0)
    for c in copies[3:]:
        c.wait()
    gate1, up1 = dot(x, g1b[...]), dot(x, u1b[...])
    gateb[1] = gate1
    upb[1] = up1
    act0 = (gate0 * jax.nn.sigmoid(gate0) * up0).astype(BF16)
    part = dot(act0, d0b[...])
    keep(1)
    act1 = (gate1 * jax.nn.sigmoid(gate1) * up1).astype(BF16)
    part = part + dot(act1, d1b[...])
    part_ref[...] = part.astype(BF16).reshape(part_ref.shape)
    for out in outs:
        out.wait()


def slopes_kernel(gate_ref, up_ref, a0_ref, b0_ref, a1_ref, b1_ref):
    for side, (a_ref, b_ref) in enumerate(((a0_ref, b0_ref), (a1_ref, b1_ref))):
        gate, upper = gate_ref[side], up_ref[side]
        sigma = jax.nn.sigmoid(gate)
        a_ref[...] = (upper * sigma * (1.0 + gate * (1.0 - sigma))).astype(BF16)
        b_ref[...] = (gate * sigma).astype(BF16)


def error_kernel(parts_ref, base_ref, err_ref):
    total = base_ref[...]
    for d in range(parts_ref.shape[0]):
        total = total + parts_ref[d].astype(F32)
    total = total.astype(BF16)
    for d in range(err_ref.shape[0]):
        err_ref[d] = total


def hidden_grads(err_buf, down_buf, a_buf, b_buf, copies):
    copies[0].wait()
    dpred = (err_buf[...].astype(F32) / 64.0).astype(BF16).reshape(-1, err_buf.shape[-1])
    copies[1].wait()
    dact = nt(dpred, down_buf[...])
    copies[2].wait()
    dgate = (dact * a_buf[...].astype(F32)).astype(BF16)
    copies[3].wait()
    return dgate, (dact * b_buf[...].astype(F32)).astype(BF16)


def own_kernel(err_ref, d_ref, a_ref, b_ref, dg_ref, du_ref, errb, db, ab, bb, sem):
    copies = fetch((err_ref, d_ref, a_ref, b_ref), (errb, db, ab, bb), sem)
    dg_ref[...], du_ref[...] = hidden_grads(errb, db, ab, bb, copies)


def group_block(flip, shift):
    y, zh = lax.axis_index("y"), lax.axis_index("zh")
    zh = 1 - zh if flip else zh
    return lax.rem(y + shift + 4, 4) * 2 + zh


def other_kernel(err_ref, d_ref, a_ref, b_ref, x0_ref, dg_ref, du_ref, x1_ref, *refs):
    outs, (errb, db, ab, bb, x0b, dgb, dub, x1b, yb, sem, out_sem) = refs[: len(SENT)], refs[len(SENT) :]
    copies = fetch(
        (err_ref, d_ref, a_ref, b_ref, x0_ref, dg_ref, du_ref, x1_ref),
        (errb, db, ab, bb, x0b, dgb, dub, x1b),
        sem,
    )
    dgate, dup = hidden_grads(errb, db, ab, bb, copies)
    for c in copies[4:]:
        c.wait()
    width, rows = dgate.shape[1], outs[0].shape[0]
    y, zh = lax.axis_index("y"), lax.axis_index("zh")
    sends = []
    for i, d in enumerate(SHIFTS + (0,)):
        at = pl.ds(pl.multiple_of(lax.rem(y + d, 4) * (2 * rows), 2 * rows), 2 * rows)
        slot = pl.ds(i * 2 * rows, 2 * rows)
        left, right = x0b[at], x1b[at]
        yb[slot, :width] = (dot(left, dgb[...]) + dot(right, dgate)).astype(BF16)
        yb[slot, width:] = (dot(left, dub[...]) + dot(right, dup)).astype(BF16)
        for flip in (1, 0):
            at = pl.ds(pl.multiple_of(i * 2 * rows + (1 - zh if flip else zh) * rows, rows), rows)
            j = SENT.index((flip, d))
            sends.append(pltpu.make_async_copy(yb.at[at], outs[j], out_sem.at[j]))
            sends[-1].start()
    for c in sends:
        c.wait()


def last_kernel(w_ref, *refs):
    count = len(GOT)
    rows = refs[0].shape[0]
    blocks = [pl.ds(pl.multiple_of(group_block(flip, -d) * rows, rows), rows) for flip, d in GOT]
    w = jnp.concatenate([w_ref[b] for b in blocks], axis=0)
    for side, out_ref in enumerate(refs[2 * count :]):
        y = jnp.concatenate([r[...] for r in refs[side * count : (side + 1) * count]], axis=0)
        out_ref[...] = tn(w, y)


VM = pl.BlockSpec(memory_space=pltpu.VMEM)
HB = pl.BlockSpec(memory_space=pl.ANY)


def vmem_like(a, tail=False):
    shape = (a.shape[0], TAIL, LANES) if tail else a.shape
    return pltpu.VMEM(shape, a.dtype)


def evolve(line_pos, line_vel, stiff, contact, offset, attach, plat_pos, pick, dest):
    sds = jax.ShapeDtypeStruct
    large = (line_pos, line_vel, contact)
    small = (stiff, offset, attach, plat_pos, pick, dest)
    return pl.pallas_call(
        evolve_kernel,
        out_shape=(
            sds((ROWS, LANES), F32),
            sds((2 * COUNT, FEATS), BF16),
            sds((3 * STEPS, LANES), F32),
            sds((3, NODES, LANES), F32),
        ),
        in_specs=[HB] * 9,
        out_specs=(VM,) * 4,
        scratch_shapes=[vmem_like(a) for a in large + small]
        + [
            pltpu.VMEM((3 * NODES, LANES * (STEPS + 1)), BF16),
            pltpu.VMEM((ROWS, LANES), F32),
            pltpu.SemaphoreType.DMA((2, 2 + STEPS)),
        ],
        compiler_params=pltpu.CompilerParams(vmem_limit_bytes=LIMIT),
        cost_estimate=pl.CostEstimate(flops=260000000, bytes_accessed=3000000, transcendentals=0),
        name="evolve",
    )(line_pos, line_vel, stiff, contact, offset, attach, plat_pos, pick, dest)


def finish(recv, bound, rows, plats, lines, w_in, fpos):
    sds = jax.ShapeDtypeStruct
    args = (recv, bound, rows, *plats, *lines, w_in)
    at = 3 + len(plats)
    bufs = [vmem_like(a, at <= i < at + 3) for i, a in enumerate(args)]
    out = (
        sds((recv.shape[0], COUNT, FEATS), BF16),
        sds((COUNT, FEATS), BF16),
        sds((COUNT, w_in.shape[1]), BF16),
        sds((3, LANES), F32),
    )
    return pl.pallas_call(
        finish_kernel,
        out_shape=out + (sds(fpos.shape, F32),),
        in_specs=[HB] * (len(args) + 1),
        out_specs=(VM,) * len(out) + (HB,),
        scratch_shapes=bufs
        + [
            pltpu.VMEM((3 * TAIL, LANES * (STEPS + 1)), F32),
            pltpu.VMEM((3, TAIL, LANES), F32),
            pltpu.SemaphoreType.DMA((len(args),)),
            pltpu.SemaphoreType.DMA,
        ],
        input_output_aliases={len(args): len(out)},
        compiler_params=pltpu.CompilerParams(vmem_limit_bytes=LIMIT),
        cost_estimate=pl.CostEstimate(flops=300000000, bytes_accessed=4000000, transcendentals=0),
        name="finish",
    )(*args, fpos)


PARAMS = pltpu.CompilerParams(vmem_limit_bytes=LIMIT)
MIDDLE = pltpu.CompilerParams(vmem_limit_bytes=24 * 1024 * 1024)
SMALL = pltpu.CompilerParams(vmem_limit_bytes=16 * 1024 * 1024)


def staged(kernel, name, args, out_shape, scratch, flops, sems, out_specs=VM, bufs=None, params=PARAMS):
    bufs = [vmem_like(a) for a in args] if bufs is None else bufs
    return pl.pallas_call(
        kernel,
        out_shape=out_shape,
        in_specs=[HB] * len(args),
        out_specs=out_specs,
        scratch_shapes=bufs + scratch + [pltpu.SemaphoreType.DMA((n,)) for n in sems],
        compiler_params=params,
        cost_estimate=pl.CostEstimate(flops=flops, bytes_accessed=8000000, transcendentals=0),
        name=name,
    )(*args)


def cut(shape, parts, offset=0):
    block = shape[:-1] + (shape[-1] // parts,)
    return pl.BlockSpec(block, lambda i: (0,) * (len(shape) - 1) + (i + offset,))


def exchange(x, axes):
    return lax.all_to_all(x, axes, split_axis=0, concat_axis=0, tiled=True)


def dot(left, right):
    return jnp.dot(left, right, preferred_element_type=F32)


def tn(left, right):
    return lax.dot_general(left, right, (((0,), (0,)), ((), ())), preferred_element_type=F32)


def swap(x, axis="core"):
    return lax.ppermute(x, axis, SWAP)


def shift(x, d):
    return lax.ppermute(x, "y", [(i, (i + d) % 4) for i in range(4)])


def total(first, *others):
    out = first.astype(F32)
    for o in others:
        out = out + o.astype(F32)
    return out.astype(BF16)


def after(x, *others):
    return lax.optimization_barrier((x,) + others)[0]


def body(
    line_pos, line_vel, stiffness, contact, offset, attach, plat_pos, plat_vel, inv_mass, restoring,
    kernel, vel_hist, wave, sample_pick, sample_dest, w_in, gain, w_gate, w_up, w_down, w_out,
):
    sds = jax.ShapeDtypeStruct
    chips = lax.axis_size(CHIP)
    groups = lax.axis_size(GRP)
    half = chips * COUNT
    width = w_gate.shape[1]
    stiff, att, pick, dest = stiffness[None], attach[None], sample_pick[None], sample_dest.reshape(1, -1)
    pay, rows, bound, fpos = evolve(
        line_pos, line_vel, stiff, contact, offset, att, plat_pos, pick, dest
    )
    pay = jnp.broadcast_to((pay + swap(pay))[None], (chips,) + pay.shape)
    pay, w_in_late, w_down_late = lax.optimization_barrier((pay, w_in, w_down))
    recv = exchange(pay, CHIP)
    product = sds((FEATS, width), BF16)
    gate_w, up_w = staged(
        products_kernel, "products", (w_in_late, gain[None], w_gate, w_up), (product, product),
        [pltpu.VMEM(w_in.shape, BF16)], 3300000000, (4,), (VM,) * 2,
    )
    gate_o, up_o = swap(gate_w), swap(up_w)
    w_down_o = swap(w_down)
    turned = lambda a: a.transpose(1, 0, 2)
    x_own, target, hidden, final_plat, final_pos = finish(
        recv, bound, rows,
        (plat_pos, plat_vel, inv_mass, restoring, turned(kernel), turned(vel_hist), turned(wave)),
        (line_pos, line_vel, contact, stiff, offset, att, pick),
        w_in, fpos,
    )
    x_own, w_down_late, w_down_o, hidden = lax.optimization_barrier((x_own, w_down_late, w_down_o, hidden))
    x = exchange(x_own, CHIP)
    product = sds((width, FEATS), BF16)
    down_w, down_o = staged(
        down_kernel, "down", (w_down_late, w_down_o, w_out), (product, product), [], 3300000000, (3,), (VM,) * 2
    )
    base = lax.optimization_barrier(dot(hidden, w_out) - target.astype(F32))
    args = (x, gate_w, up_w, down_w, gate_o, up_o, down_o)
    wide = sds((2, half, width), F32)
    part, gate, upper = staged(
        forward_kernel, "forward", args, (sds(x.shape, BF16), wide, wide),
        [pltpu.VMEM(wide.shape, F32)] * 2, 2500000000, (7, 4), (VM, HB, HB),
    )
    part, gate, upper, x_late, w_in_late = lax.optimization_barrier((part, gate, upper, x, w_in_late))
    parts = exchange(part, CHIP)
    slope = sds((half, width), BF16)
    wide_rows = pl.BlockSpec((2, half // 4, width), lambda i: (0, i, 0))
    slope_rows = pl.BlockSpec((half // 4, width), lambda i: (i, 0))
    slope_a, slope_b, slope_ao, slope_bo = pl.pallas_call(
        slopes_kernel, grid=(4,), out_shape=(slope,) * 4, in_specs=[wide_rows] * 2,
        out_specs=(slope_rows,) * 4, compiler_params=PARAMS, name="slopes",
        cost_estimate=pl.CostEstimate(flops=8000000, bytes_accessed=6000000, transcendentals=1000000),
    )(gate, upper)
    slope_ao, slope_bo = swap(slope_ao), swap(slope_bo)
    x_late, slope_a = lax.optimization_barrier((x_late, slope_a))
    x_late = lax.optimization_barrier(x_late.reshape(half, FEATS).T)
    x_other = swap(x_late)
    err_own = pl.pallas_call(
        error_kernel, grid=(3,), out_shape=sds((chips, COUNT, FEATS), BF16),
        in_specs=[cut(parts.shape, 3), cut(base.shape, 3)], out_specs=cut(parts.shape, 3),
        compiler_params=SMALL, name="error",
    )(parts, base)
    err_own, slope_ao, slope_bo = lax.optimization_barrier((err_own, slope_ao, slope_bo))
    err = exchange(err_own, CHIP)
    err_other = swap(err)
    dg, du = staged(
        own_kernel, "own", (err, down_w, slope_a, slope_b), (slope, slope), [], 400000000, (4,), (VM,) * 2,
    )
    piece = sds((FEATS // groups, 2 * width), BF16)
    pieces = staged(
        other_kernel, "other", (err_other, down_w, slope_ao, slope_bo, x_late, dg, du, x_other),
        (piece,) * len(SENT), [pltpu.VMEM((FEATS, 2 * width), BF16)], 2000000000, (8, len(SENT)),
        (HB,) * len(SENT),
    )
    pieces = list(pieces)
    pieces[0], gain_late, w_in_late = lax.optimization_barrier((pieces[0], gain, w_in_late))
    at = lax.axis_index(GRP)
    block = w_in.shape[1] // groups
    w_own = lax.optimization_barrier(lax.dynamic_slice_in_dim(w_in_late, at * block, block, 1))
    gain_own = lax.dynamic_slice_in_dim(gain_late, at * block, block, 0)
    w_own = lax.optimization_barrier((w_own.astype(F32) * gain_own).astype(BF16))
    moved = [shift(p, d) if d else p for p, (_, d) in zip(pieces, SENT)]
    theirs = swap(total(*moved[:4]), "zh")
    grads = total(*moved[4:], theirs)
    grads, err_late, err_other = lax.optimization_barrier((grads, err, err_other))
    twin = swap(grads, "zh")
    got = [grads, twin] + [shift(v, d) for v in (grads, twin) for d in SHIFTS]
    grad = sds((block, width), F32)
    grad_gate, grad_up = pl.pallas_call(
        last_kernel, grid=(2,), out_shape=(grad, grad),
        in_specs=[pl.BlockSpec(w_own.shape, lambda i: (0, 0))]
        + [cut(piece.shape, 4)] * len(GOT) + [cut(piece.shape, 4, 2)] * len(GOT),
        out_specs=(cut(grad.shape, 2),) * 2, compiler_params=SMALL, name="last",
    )(w_own, *got, *got)
    err_all = jnp.concatenate([err_late, err_other], axis=0).reshape(2 * half, FEATS)
    core = lax.axis_index("core")
    codes = recv[:, CODE_ROW : CODE_ROW + 2, :COUNT]
    codes = jnp.where(core == 0, codes, codes[:, ::-1]).transpose(1, 0, 2).reshape(1, 2 * half)
    me = lax.axis_index(CHIP) * 2 + core
    number = jnp.arange(2 * half, dtype=jnp.int32)
    source = ((number // COUNT) % chips) * 2 + (number // half + core) % 2
    slot = jnp.arange(2 * chips * CAP, dtype=jnp.int32)[:, None]
    match = (source[None] == slot // CAP) & (codes == (me * CAP + slot % CAP).astype(F32))
    slot_error = dot(match.astype(BF16), err_all).astype(BF16)
    return (final_pos, final_plat, slot_error, grad_gate, grad_up)


def solution(mesh):
    sizes = (4, 2, 2, 4, 2)
    if mesh.devices.shape[0] == 1:
        sizes = (1, 1, 2, 4, 2)
    fine = Mesh(mesh.devices.reshape(sizes), ALL)
    in_specs = (
        P(None, None, ALL),
        P(None, None, ALL),
        P(ALL),
        P(None, None, ALL),
        P(None, ALL),
        P(ALL),
        P(None, GRP),
        P(None, GRP),
        P(None, GRP),
        P(None, GRP),
        P(None, None, GRP),
        P(None, None, GRP),
        P(None, None, GRP),
        P(ALL),
        P(ALL, None),
        P(),
        P(),
        P(None, DEV),
        P(None, DEV),
        P(DEV, None),
        P(),
    )
    out_specs = (
        P(None, None, ALL),
        P(None, GRP),
        P(ALL, None),
        P(GRP, DEV),
        P(GRP, DEV),
    )
    return jax.shard_map(body, mesh=fine, in_specs=in_specs, out_specs=out_specs, check_vma=False)
```

```python
import functools
import jax
import jax.numpy as jnp
from jax import lax
from jax.experimental import pallas as pl
from jax.experimental.pallas import tpu as pltpu
from jax.sharding import Mesh, PartitionSpec as P

STEPS = 8
CAP = 8
NODES = 256
TAIL = 8
LANES = 128
COUNT = 64
FEATS = 768
ROWS = 72
ONES_ROW = 24
CODE_ROW = 67
LIMIT = 60 * 1024 * 1024
HIGH = lax.Precision.HIGHEST
F32 = jnp.float32
BF16 = jnp.bfloat16
DEV = ("zl", "x", "core")
CHIP = ("zl", "x")
GRP = ("y", "zh")
ALL = GRP + DEV
PAIRS = [(s, t) for s in range(2, STEPS) for t in range(1, s)]
SWAP = [(0, 1), (1, 0)]
SHIFTS = (1, 3, 2)
SENT = [(flip, d) for flip in (1, 0) for d in SHIFTS + (0,)]
GOT = [(0, 0), (1, 0)] + [(flip, d) for flip in (0, 1) for d in SHIFTS]


def nt(left, right, precision=None):
    return lax.dot_general(
        left, right, (((1,), (1,)), ((), ())), precision=precision, preferred_element_type=F32
    )


def iota(shape, dim):
    return lax.broadcasted_iota(jnp.int32, shape, dim)


def pick_matrix(pick_ref):
    count = pick_ref.shape[1]
    eye = iota((count, count), 0) == iota((count, count), 1)
    pick = jnp.sum(jnp.where(eye, pick_ref[...].astype(F32), 0.0), axis=1, keepdims=True).astype(jnp.int32)
    at = (pick >> 3) + LANES * (pick & 7)
    at = jnp.concatenate([at, at + LANES], axis=0)
    return (iota((2 * count, LANES * (STEPS + 1)), 1) == at).astype(F32).astype(BF16)


def fetch(refs, bufs, sem):
    copies = [pltpu.make_async_copy(r, b, sem.at[i]) for i, (r, b) in enumerate(zip(refs, bufs))]
    for c in copies:
        c.start()
    return copies


def evolve_kernel(
    pos_ref, vel_ref, stiff_ref, contact_ref, off_ref, attach_ref, plat_ref, pick_ref, dest_ref,
    pay_ref, rows_ref, bound_ref, fpos_ref,
    posb, velb, contactb, stiffb, offb, attachb, platb, pickb, destb, stack, lin, sem,
):
    small = fetch(
        (stiff_ref, off_ref, attach_ref, plat_ref, pick_ref, dest_ref),
        (stiffb, offb, attachb, platb, pickb, destb),
        sem.at[0],
    )
    large = fetch(
        (pos_ref, vel_ref) + tuple(contact_ref.at[s] for s in range(STEPS)),
        (posb, velb) + tuple(contactb.at[s] for s in range(STEPS)),
        sem.at[1],
    )
    for c in small:
        c.wait()
    k = stiffb[...]
    onehot = (attachb[...] == iota((LANES, LANES), 0)).astype(F32)
    off = offb[...]
    fair = jnp.dot(platb[...], onehot, precision=HIGH, preferred_element_type=F32) + off
    picks = pick_matrix(pickb)
    row = iota((NODES, LANES), 0)
    first, last, bulk = row == 0, row == NODES - 1, row < NODES - TAIL
    lin[...] = jnp.zeros_like(lin)
    lin[ONES_ROW : ONES_ROW + 1] = jnp.ones((1, LANES), F32)
    large[0].wait()
    large[1].wait()
    pos = [jnp.where(last, fair[c : c + 1], posb[c]) for c in range(3)]
    vel = [velb[c] for c in range(3)]
    for step in range(STEPS):
        large[2 + step].wait()
        touch = contactb[step].astype(F32)
        damp = 0.02 + 0.1 * touch
        for c in range(3):
            p = pos[c]
            stack[c * NODES : (c + 1) * NODES, step * LANES : (step + 1) * LANES] = jnp.where(bulk, p, 0.0).astype(BF16)
            bound_ref[step * 3 + c : step * 3 + c + 1] = p[NODES - TAIL - 1 : NODES - TAIL]
            lin[step * 3 + c : step * 3 + c + 1] = p[NODES - 2 : NODES - 1] - p[NODES - 1 : NODES]
            accel = k * (pltpu.roll(p, NODES - 1, 0) - 2.0 * p + pltpu.roll(p, 1, 0)) - damp * vel[c]
            if c == 2:
                accel = accel + (-0.05 - 0.3 * touch * (p + 2.0))
            vel[c] = vel[c] + accel
            pos[c] = jnp.where(first, p, jnp.where(last, off[c : c + 1], p + vel[c]))
    for c in range(3):
        stack[c * NODES : (c + 1) * NODES, STEPS * LANES :] = jnp.where(bulk, pos[c], 0.0).astype(BF16)
        fpos_ref[c] = pos[c]
    rows_ref[...] = nt(picks, stack[...]).astype(BF16)
    trow = iota((TAIL, LANES), 0)
    zero = jnp.zeros((TAIL, LANES), F32)
    for kind in range(2):
        rp, rv = [zero] * 6, [zero] * 6
        for step in range(1, STEPS):
            for t in range(1, step):
                at = ONES_ROW + 1 + 2 * PAIRS.index((step, t)) + kind
                lin[at : at + 1] = rp[t - 1][TAIL - 2 : TAIL - 1]
            if step == STEPS - 1:
                break
            touch = contactb[step, NODES - TAIL : NODES].astype(F32)
            damp = 0.02 + 0.1 * touch
            for t in range(1, step + 1):
                p = jnp.where(trow == TAIL - 1, 1.0 if t == step else 0.0, rp[t - 1])
                up = pltpu.roll(p, TAIL - 1, 0)
                down = jnp.where(trow == 0, 0.0, pltpu.roll(p, 1, 0))
                accel = k * (up - 2.0 * p + down) - damp * rv[t - 1]
                if kind == 1:
                    accel = accel - 0.3 * touch * p
                rv[t - 1] = rv[t - 1] + accel
                rp[t - 1] = p + rv[t - 1]
    sums = nt(lin[...] * k, onehot, HIGH)
    count = destb.shape[1]
    lane, sub = iota((count, count), 1), iota((count, count), 0)
    dest = destb[...].astype(F32)
    dest_col = jnp.sum(jnp.where(lane == sub, dest, 0.0), axis=1, keepdims=True)
    rank = jnp.sum(jnp.where((dest_col == dest) & (sub < lane), 1.0, 0.0), axis=0, keepdims=True)
    codes = jnp.concatenate([dest * CAP + rank, jnp.full((1, LANES - count), -1.0, F32)], axis=1)
    pay_ref[...] = jnp.where(iota((ROWS, LANES), 0) == CODE_ROW + lax.axis_index("core"), codes, sums)


def finish_kernel(
    recv_ref, bound_ref, rows_ref, plat_ref, plat_vel_ref, inv_ref, rest_ref, kern_ref, hist_ref, wave_ref,
    pos_ref, vel_ref, contact_ref, stiff_ref, off_ref, attach_ref, pick_ref, w_in_ref, fpos_in,
    x_ref, t_ref, h_ref, plat_out, fpos_ref,
    recvb, boundb, rowsb, platb, plat_velb, invb, restb, kernb, histb, waveb,
    posb, velb, contactb, stiffb, offb, attachb, pickb, w_inb, tails, final, sem, out_sem,
):
    at = pl.ds(NODES - TAIL, TAIL)
    copies = fetch(
        (
            recv_ref, plat_ref, plat_vel_ref, inv_ref, rest_ref, kern_ref, hist_ref, wave_ref,
            stiff_ref, off_ref, attach_ref, pick_ref, bound_ref, rows_ref,
            pos_ref.at[:, at, :], vel_ref.at[:, at, :], contact_ref.at[:, at, :], w_in_ref,
        ),
        (
            recvb, platb, plat_velb, invb, restb, kernb, histb, waveb,
            stiffb, offb, attachb, pickb, boundb, rowsb, posb, velb, contactb, w_inb,
        ),
        sem,
    )
    copies[10].wait()
    copies[11].wait()
    picks = pick_matrix(pickb)
    onehot = (attachb[...] == iota((LANES, LANES), 0)).astype(F32)
    at = iota((3 * TAIL, FEATS), 0)
    where = (at // TAIL) * NODES + (NODES - TAIL) + at % TAIL
    place = (iota((3 * TAIL, FEATS), 1) == where).astype(F32).astype(BF16)
    for c in copies[:10] + copies[12:-1]:
        c.wait()
    total = recvb[0]
    for d in range(1, recvb.shape[0]):
        total = total + recvb[d]
    q, u = platb[...], plat_velb[...]
    hist = [histb[:, m] for m in range(STEPS)]
    kern = [kernb[:, m] for m in range(STEPS)]
    ones = total[ONES_ROW : ONES_ROW + 1]
    qs = [q]
    for step in range(STEPS):
        force = total[3 * step : 3 * step + 3]
        if step > 0:
            force = force - ones * q
        for t in range(1, step):
            at = ONES_ROW + 1 + 2 * PAIRS.index((step, t))
            coef = jnp.concatenate([total[at : at + 1], total[at : at + 2]], axis=0)
            force = force + coef * qs[t]
        memory = kern[0] * hist[0]
        for m in range(1, STEPS):
            memory = memory + kern[m] * hist[m]
        u = u + invb[...] * (force - restb[...] * q - memory + waveb[:, step])
        q = q + u
        hist = [u] + hist[:-1]
        qs.append(q)
    plat_out[...] = q
    k = stiffb[...]
    fair = jnp.dot(jnp.concatenate(qs, axis=0), onehot, precision=HIGH, preferred_element_type=F32)
    trow = iota((TAIL, LANES), 0)
    pos = [posb[c] for c in range(3)]
    vel = [velb[c] for c in range(3)]
    for step in range(STEPS + 1):
        for c in range(3):
            here = fair[step * 3 + c : step * 3 + c + 1] + offb[c : c + 1]
            p = jnp.where(trow == TAIL - 1, here, pos[c])
            tails[c * TAIL : (c + 1) * TAIL, step * LANES : (step + 1) * LANES] = p
            if step == STEPS:
                final[c] = p
                continue
            touch = contactb[step].astype(F32)
            up = pltpu.roll(p, TAIL - 1, 0)
            bound = boundb[step * 3 + c : step * 3 + c + 1]
            down = jnp.where(trow == 0, bound, pltpu.roll(p, 1, 0))
            accel = k * (up - 2.0 * p + down) - (0.02 + 0.1 * touch) * vel[c]
            if c == 2:
                accel = accel + (-0.05 - 0.3 * touch * (p + 2.0))
            vel[c] = vel[c] + accel
            pos[c] = p + vel[c]
    copy = pltpu.make_async_copy(final, fpos_ref.at[:, NODES - TAIL : NODES, :], out_sem)
    copy.start()
    picked = nt(picks, tails[...].astype(BF16)).astype(BF16)
    rows = rowsb[...].astype(F32) + jnp.dot(picked, place, preferred_element_type=F32)
    count = t_ref.shape[0]
    t_ref[...] = rows[count:].astype(BF16)
    copies[-1].wait()
    hidden = jnp.dot(rows[:count].astype(BF16), w_inb[...], preferred_element_type=F32).astype(BF16)
    h_ref[...] = hidden
    wide = hidden.astype(F32)
    scale = lax.rsqrt(jnp.mean(wide * wide, axis=1, keepdims=True) + 1e-06)
    scaled = (rows[:count] * scale).astype(BF16)
    for d in range(x_ref.shape[0]):
        x_ref[d] = scaled
    copy.wait()


def products_kernel(w_in_ref, gain_ref, gate_ref, up_ref, g_ref, u_ref, w_inb, gainb, gateb, upb, scaled, sem):
    copies = fetch((gain_ref, w_in_ref, gate_ref, up_ref), (gainb, w_inb, gateb, upb), sem)
    copies[0].wait()
    copies[1].wait()
    rows = 256
    for i in range(w_inb.shape[0] // rows):
        at = pl.ds(i * rows, rows)
        scaled[at] = (w_inb[at].astype(F32) * gainb[...]).astype(BF16)
        if i == 0:
            copies[2].wait()
        g_ref[at] = dot(scaled[at], gateb[...]).astype(BF16)
        if i == 0:
            copies[3].wait()
        u_ref[at] = dot(scaled[at], upb[...]).astype(BF16)


def down_kernel(w0_ref, w1_ref, out_ref, d0_ref, d1_ref, w0b, w1b, outb, sem):
    copies = fetch((out_ref, w0_ref, w1_ref), (outb, w0b, w1b), sem)
    copies[0].wait()
    tall = 256
    for copy, w, d_ref in ((copies[1], w0b, d0_ref), (copies[2], w1b, d1_ref)):
        copy.wait()
        for i in range(w.shape[0] // tall):
            at = pl.ds(i * tall, tall)
            d_ref[at] = dot(w[at], outb[...]).astype(BF16)


def forward_kernel(
    x_ref, g0_ref, u0_ref, d0_ref, g1_ref, u1_ref, d1_ref, part_ref, gate_ref, up_ref,
    xb, g0b, u0b, d0b, g1b, u1b, d1b, gateb, upb, sem, out_sem,
):
    copies = fetch(
        (x_ref, g0_ref, u0_ref, d0_ref, g1_ref, u1_ref, d1_ref), (xb, g0b, u0b, d0b, g1b, u1b, d1b), sem
    )
    copies[0].wait()
    x = xb[...].reshape(-1, xb.shape[-1])
    outs = []

    def keep(side):
        for i, (buf, ref) in enumerate(((gateb, gate_ref), (upb, up_ref))):
            out = pltpu.make_async_copy(buf.at[side], ref.at[side], out_sem.at[2 * side + i])
            out.start()
            outs.append(out)

    copies[1].wait()
    gate0 = dot(x, g0b[...])
    gateb[0] = gate0
    copies[2].wait()
    up0 = dot(x, u0b[...])
    upb[0] = up0
    keep(0)
    for c in copies[3:]:
        c.wait()
    gate1, up1 = dot(x, g1b[...]), dot(x, u1b[...])
    gateb[1] = gate1
    upb[1] = up1
    act0 = (gate0 * jax.nn.sigmoid(gate0) * up0).astype(BF16)
    part = dot(act0, d0b[...])
    keep(1)
    act1 = (gate1 * jax.nn.sigmoid(gate1) * up1).astype(BF16)
    part = part + dot(act1, d1b[...])
    part_ref[...] = part.astype(BF16).reshape(part_ref.shape)
    for out in outs:
        out.wait()


def slopes_kernel(gate_ref, up_ref, a0_ref, b0_ref, a1_ref, b1_ref):
    for side, (a_ref, b_ref) in enumerate(((a0_ref, b0_ref), (a1_ref, b1_ref))):
        gate, upper = gate_ref[side], up_ref[side]
        sigma = jax.nn.sigmoid(gate)
        a_ref[...] = (upper * sigma * (1.0 + gate * (1.0 - sigma))).astype(BF16)
        b_ref[...] = (gate * sigma).astype(BF16)


def error_kernel(parts_ref, base_ref, err_ref):
    total = base_ref[...]
    for d in range(parts_ref.shape[0]):
        total = total + parts_ref[d].astype(F32)
    total = total.astype(BF16)
    for d in range(err_ref.shape[0]):
        err_ref[d] = total


def hidden_grads(err_buf, down_buf, a_buf, b_buf, copies):
    copies[0].wait()
    dpred = (err_buf[...].astype(F32) / 64.0).astype(BF16).reshape(-1, err_buf.shape[-1])
    copies[1].wait()
    dact = nt(dpred, down_buf[...])
    copies[2].wait()
    dgate = (dact * a_buf[...].astype(F32)).astype(BF16)
    copies[3].wait()
    return dgate, (dact * b_buf[...].astype(F32)).astype(BF16)


def own_kernel(err_ref, d_ref, a_ref, b_ref, dg_ref, du_ref, errb, db, ab, bb, sem):
    copies = fetch((err_ref, d_ref, a_ref, b_ref), (errb, db, ab, bb), sem)
    dg_ref[...], du_ref[...] = hidden_grads(errb, db, ab, bb, copies)


def group_block(flip, shift):
    y, zh = lax.axis_index("y"), lax.axis_index("zh")
    zh = 1 - zh if flip else zh
    return lax.rem(y + shift + 4, 4) * 2 + zh


def other_kernel(err_ref, d_ref, a_ref, b_ref, x0_ref, dg_ref, du_ref, x1_ref, *refs):
    outs, (errb, db, ab, bb, x0b, dgb, dub, x1b, yb, sem, out_sem) = refs[: len(SENT)], refs[len(SENT) :]
    copies = fetch(
        (err_ref, d_ref, a_ref, b_ref, x0_ref, dg_ref, du_ref, x1_ref),
        (errb, db, ab, bb, x0b, dgb, dub, x1b),
        sem,
    )
    dgate, dup = hidden_grads(errb, db, ab, bb, copies)
    for c in copies[4:]:
        c.wait()
    width, rows = dgate.shape[1], outs[0].shape[0]
    y, zh = lax.axis_index("y"), lax.axis_index("zh")
    sends = []
    for i, d in enumerate(SHIFTS + (0,)):
        at = pl.ds(pl.multiple_of(lax.rem(y + d, 4) * (2 * rows), 2 * rows), 2 * rows)
        slot = pl.ds(i * 2 * rows, 2 * rows)
        left, right = x0b[at], x1b[at]
        yb[slot, :width] = (dot(left, dgb[...]) + dot(right, dgate)).astype(BF16)
        yb[slot, width:] = (dot(left, dub[...]) + dot(right, dup)).astype(BF16)
        for flip in (1, 0):
            at = pl.ds(pl.multiple_of(i * 2 * rows + (1 - zh if flip else zh) * rows, rows), rows)
            j = SENT.index((flip, d))
            sends.append(pltpu.make_async_copy(yb.at[at], outs[j], out_sem.at[j]))
            sends[-1].start()
    for c in sends:
        c.wait()


def last_kernel(w_ref, *refs):
    count = len(GOT)
    rows = refs[0].shape[0]
    blocks = [pl.ds(pl.multiple_of(group_block(flip, -d) * rows, rows), rows) for flip, d in GOT]
    w = jnp.concatenate([w_ref[b] for b in blocks], axis=0)
    for side, out_ref in enumerate(refs[2 * count :]):
        y = jnp.concatenate([r[...] for r in refs[side * count : (side + 1) * count]], axis=0)
        out_ref[...] = tn(w, y)


VM = pl.BlockSpec(memory_space=pltpu.VMEM)
HB = pl.BlockSpec(memory_space=pl.ANY)


def vmem_like(a, tail=False):
    shape = (a.shape[0], TAIL, LANES) if tail else a.shape
    return pltpu.VMEM(shape, a.dtype)


def evolve(line_pos, line_vel, stiff, contact, offset, attach, plat_pos, pick, dest):
    sds = jax.ShapeDtypeStruct
    large = (line_pos, line_vel, contact)
    small = (stiff, offset, attach, plat_pos, pick, dest)
    return pl.pallas_call(
        evolve_kernel,
        out_shape=(
            sds((ROWS, LANES), F32),
            sds((2 * COUNT, FEATS), BF16),
            sds((3 * STEPS, LANES), F32),
            sds((3, NODES, LANES), F32),
        ),
        in_specs=[HB] * 9,
        out_specs=(VM,) * 4,
        scratch_shapes=[vmem_like(a) for a in large + small]
        + [
            pltpu.VMEM((3 * NODES, LANES * (STEPS + 1)), BF16),
            pltpu.VMEM((ROWS, LANES), F32),
            pltpu.SemaphoreType.DMA((2, 2 + STEPS)),
        ],
        compiler_params=pltpu.CompilerParams(vmem_limit_bytes=LIMIT),
        cost_estimate=pl.CostEstimate(flops=260000000, bytes_accessed=3000000, transcendentals=0),
        name="evolve",
    )(line_pos, line_vel, stiff, contact, offset, attach, plat_pos, pick, dest)


def finish(recv, bound, rows, plats, lines, w_in, fpos):
    sds = jax.ShapeDtypeStruct
    args = (recv, bound, rows, *plats, *lines, w_in)
    at = 3 + len(plats)
    bufs = [vmem_like(a, at <= i < at + 3) for i, a in enumerate(args)]
    out = (
        sds((recv.shape[0], COUNT, FEATS), BF16),
        sds((COUNT, FEATS), BF16),
        sds((COUNT, w_in.shape[1]), BF16),
        sds((3, LANES), F32),
    )
    return pl.pallas_call(
        finish_kernel,
        out_shape=out + (sds(fpos.shape, F32),),
        in_specs=[HB] * (len(args) + 1),
        out_specs=(VM,) * len(out) + (HB,),
        scratch_shapes=bufs
        + [
            pltpu.VMEM((3 * TAIL, LANES * (STEPS + 1)), F32),
            pltpu.VMEM((3, TAIL, LANES), F32),
            pltpu.SemaphoreType.DMA((len(args),)),
            pltpu.SemaphoreType.DMA,
        ],
        input_output_aliases={len(args): len(out)},
        compiler_params=pltpu.CompilerParams(vmem_limit_bytes=LIMIT),
        cost_estimate=pl.CostEstimate(flops=300000000, bytes_accessed=4000000, transcendentals=0),
        name="finish",
    )(*args, fpos)


PARAMS = pltpu.CompilerParams(vmem_limit_bytes=LIMIT)
MIDDLE = pltpu.CompilerParams(vmem_limit_bytes=24 * 1024 * 1024)
SMALL = pltpu.CompilerParams(vmem_limit_bytes=16 * 1024 * 1024)


def staged(kernel, name, args, out_shape, scratch, flops, sems, out_specs=VM, bufs=None, params=PARAMS):
    bufs = [vmem_like(a) for a in args] if bufs is None else bufs
    return pl.pallas_call(
        kernel,
        out_shape=out_shape,
        in_specs=[HB] * len(args),
        out_specs=out_specs,
        scratch_shapes=bufs + scratch + [pltpu.SemaphoreType.DMA((n,)) for n in sems],
        compiler_params=params,
        cost_estimate=pl.CostEstimate(flops=flops, bytes_accessed=8000000, transcendentals=0),
        name=name,
    )(*args)


def cut(shape, parts, offset=0):
    block = shape[:-1] + (shape[-1] // parts,)
    return pl.BlockSpec(block, lambda i: (0,) * (len(shape) - 1) + (i + offset,))


def exchange(x, axes):
    return lax.all_to_all(x, axes, split_axis=0, concat_axis=0, tiled=True)


def dot(left, right):
    return jnp.dot(left, right, preferred_element_type=F32)


def tn(left, right):
    return lax.dot_general(left, right, (((0,), (0,)), ((), ())), preferred_element_type=F32)


def swap(x, axis="core"):
    return lax.ppermute(x, axis, SWAP)


def shift(x, d):
    return lax.ppermute(x, "y", [(i, (i + d) % 4) for i in range(4)])


def total(first, *others):
    out = first.astype(F32)
    for o in others:
        out = out + o.astype(F32)
    return out.astype(BF16)


def after(x, *others):
    return lax.optimization_barrier((x,) + others)[0]


def body(
    line_pos, line_vel, stiffness, contact, offset, attach, plat_pos, plat_vel, inv_mass, restoring,
    kernel, vel_hist, wave, sample_pick, sample_dest, w_in, gain, w_gate, w_up, w_down, w_out,
):
    sds = jax.ShapeDtypeStruct
    chips = lax.axis_size(CHIP)
    groups = lax.axis_size(GRP)
    half = chips * COUNT
    width = w_gate.shape[1]
    stiff, att, pick, dest = stiffness[None], attach[None], sample_pick[None], sample_dest.reshape(1, -1)
    pay, rows, bound, fpos = evolve(
        line_pos, line_vel, stiff, contact, offset, att, plat_pos, pick, dest
    )
    pay = jnp.broadcast_to((pay + swap(pay))[None], (chips,) + pay.shape)
    pay, w_in_late, w_down_late = lax.optimization_barrier((pay, w_in, w_down))
    recv = exchange(pay, CHIP)
    product = sds((FEATS, width), BF16)
    gate_w, up_w = staged(
        products_kernel, "products", (w_in_late, gain[None], w_gate, w_up), (product, product),
        [pltpu.VMEM(w_in.shape, BF16)], 3300000000, (4,), (VM,) * 2,
    )
    gate_o, up_o = swap(gate_w), swap(up_w)
    w_down_o = swap(w_down)
    turned = lambda a: a.transpose(1, 0, 2)
    x_own, target, hidden, final_plat, final_pos = finish(
        recv, bound, rows,
        (plat_pos, plat_vel, inv_mass, restoring, turned(kernel), turned(vel_hist), turned(wave)),
        (line_pos, line_vel, contact, stiff, offset, att, pick),
        w_in, fpos,
    )
    x_own, w_down_late, w_down_o, hidden = lax.optimization_barrier((x_own, w_down_late, w_down_o, hidden))
    x = exchange(x_own, CHIP)
    product = sds((width, FEATS), BF16)
    down_w, down_o = staged(
        down_kernel, "down", (w_down_late, w_down_o, w_out), (product, product), [], 3300000000, (3,), (VM,) * 2
    )
    base = lax.optimization_barrier(dot(hidden, w_out) - target.astype(F32))
    args = (x, gate_w, up_w, down_w, gate_o, up_o, down_o)
    wide = sds((2, half, width), F32)
    part, gate, upper = staged(
        forward_kernel, "forward", args, (sds(x.shape, BF16), wide, wide),
        [pltpu.VMEM(wide.shape, F32)] * 2, 2500000000, (7, 4), (VM, HB, HB),
    )
    part, gate, upper, x_late, w_in_late = lax.optimization_barrier((part, gate, upper, x, w_in_late))
    parts = exchange(part, CHIP)
    slope = sds((half, width), BF16)
    wide_rows = pl.BlockSpec((2, half // 4, width), lambda i: (0, i, 0))
    slope_rows = pl.BlockSpec((half // 4, width), lambda i: (i, 0))
    slope_a, slope_b, slope_ao, slope_bo = pl.pallas_call(
        slopes_kernel, grid=(4,), out_shape=(slope,) * 4, in_specs=[wide_rows] * 2,
        out_specs=(slope_rows,) * 4, compiler_params=PARAMS, name="slopes",
        cost_estimate=pl.CostEstimate(flops=8000000, bytes_accessed=6000000, transcendentals=1000000),
    )(gate, upper)
    slope_ao, slope_bo = swap(slope_ao), swap(slope_bo)
    x_late, slope_a = lax.optimization_barrier((x_late, slope_a))
    x_late = lax.optimization_barrier(x_late.reshape(half, FEATS).T)
    x_other = swap(x_late)
    err_own = pl.pallas_call(
        error_kernel, grid=(3,), out_shape=sds((chips, COUNT, FEATS), BF16),
        in_specs=[cut(parts.shape, 3), cut(base.shape, 3)], out_specs=cut(parts.shape, 3),
        compiler_params=SMALL, name="error",
    )(parts, base)
    err_own, slope_ao, slope_bo = lax.optimization_barrier((err_own, slope_ao, slope_bo))
    err = exchange(err_own, CHIP)
    err_other = swap(err)
    dg, du = staged(
        own_kernel, "own", (err, down_w, slope_a, slope_b), (slope, slope), [], 400000000, (4,), (VM,) * 2,
    )
    piece = sds((FEATS // groups, 2 * width), BF16)
    pieces = staged(
        other_kernel, "other", (err_other, down_w, slope_ao, slope_bo, x_late, dg, du, x_other),
        (piece,) * len(SENT), [pltpu.VMEM((FEATS, 2 * width), BF16)], 2000000000, (8, len(SENT)),
        (HB,) * len(SENT),
    )
    pieces = list(pieces)
    pieces[0], gain_late, w_in_late = lax.optimization_barrier((pieces[0], gain, w_in_late))
    at = lax.axis_index(GRP)
    block = w_in.shape[1] // groups
    w_own = lax.optimization_barrier(lax.dynamic_slice_in_dim(w_in_late, at * block, block, 1))
    gain_own = lax.dynamic_slice_in_dim(gain_late, at * block, block, 0)
    w_own = lax.optimization_barrier((w_own.astype(F32) * gain_own).astype(BF16))
    moved = [shift(p, d) if d else p for p, (_, d) in zip(pieces, SENT)]
    theirs = swap(total(*moved[:4]), "zh")
    grads = total(*moved[4:], theirs)
    grads, err_late, err_other, recv = lax.optimization_barrier((grads, err, err_other, recv))
    twin = swap(grads, "zh")
    got = [grads, twin] + [shift(v, d) for v in (grads, twin) for d in SHIFTS]
    grad = sds((block, width), F32)
    grad_gate, grad_up = pl.pallas_call(
        last_kernel, grid=(2,), out_shape=(grad, grad),
        in_specs=[pl.BlockSpec(w_own.shape, lambda i: (0, 0))]
        + [cut(piece.shape, 4)] * len(GOT) + [cut(piece.shape, 4, 2)] * len(GOT),
        out_specs=(cut(grad.shape, 2),) * 2, compiler_params=SMALL, name="last",
    )(w_own, *got, *got)
    err_all = jnp.concatenate([err_late, err_other], axis=0).reshape(2 * half, FEATS)
    core = lax.axis_index("core")
    codes = recv[:, CODE_ROW : CODE_ROW + 2, :COUNT]
    codes = jnp.where(core == 0, codes, codes[:, ::-1]).transpose(1, 0, 2).reshape(1, 2 * half)
    me = lax.axis_index(CHIP) * 2 + core
    number = jnp.arange(2 * half, dtype=jnp.int32)
    source = ((number // COUNT) % chips) * 2 + (number // half + core) % 2
    slot = jnp.arange(2 * chips * CAP, dtype=jnp.int32)[:, None]
    match = (source[None] == slot // CAP) & (codes == (me * CAP + slot % CAP).astype(F32))
    slot_error = dot(match.astype(BF16), err_all).astype(BF16)
    return (final_pos, final_plat, slot_error, grad_gate, grad_up)


def solution(mesh):
    sizes = (4, 2, 2, 4, 2)
    if mesh.devices.shape[0] == 1:
        sizes = (1, 1, 2, 4, 2)
    fine = Mesh(mesh.devices.reshape(sizes), ALL)
    in_specs = (
        P(None, None, ALL),
        P(None, None, ALL),
        P(ALL),
        P(None, None, ALL),
        P(None, ALL),
        P(ALL),
        P(None, GRP),
        P(None, GRP),
        P(None, GRP),
        P(None, GRP),
        P(None, None, GRP),
        P(None, None, GRP),
        P(None, None, GRP),
        P(ALL),
        P(ALL, None),
        P(),
        P(),
        P(None, DEV),
        P(None, DEV),
        P(DEV, None),
        P(),
    )
    out_specs = (
        P(None, None, ALL),
        P(None, GRP),
        P(ALL, None),
        P(GRP, DEV),
        P(GRP, DEV),
    )
    return jax.shard_map(body, mesh=fine, in_specs=in_specs, out_specs=out_specs, check_vma=False)
```
